32 devices in a mesh: grp: 4 (over y, x), seq: 8 (over z, core).
Axes of the slice: x: 2, y: 2, z: 4, core: 2. Of those that a mesh axis runs over, the one named last changes fastest.
Arguments:
- tokens: bfloat16 [4, 4, 1024, 384], P('grp', None, 'seq'), may hold values from -6 to 6
- cotangent: bfloat16 [4, 4, 1024, 384], P('grp', None, 'seq'), may hold values from -6 to 6
- lengths: int32 [4, 4, 8], P('grp'), may hold values from 1 to 1017, as said below
- valid_mask: int32 [4, 4, 1024], P('grp'), may hold values 0 or 1
- lead_index: int32 [4], P('grp'), may hold values from 0 to 7
- sample_counts: int32 [4], replicated, may hold values from 1 to 16
- lead_table: bfloat16 [8, 384], replicated, may hold values from -6 to 6
- modulation_weight: bfloat16 [384, 2304], replicated, may hold values from -0.3125 to 0.3125
- modulation_bias: bfloat16 [2304], replicated, may hold values from -4 to 4
- attend_weight: bfloat16 [384, 1152], replicated, may hold values from -0.3125 to 0.3125
- output_weight: bfloat16 [384, 384], replicated, may hold values from -1.25 to 1.25
- output_bias: bfloat16 [384], replicated, may hold values from -4 to 4
- expand_weight: bfloat16 [384, 1536], replicated, may hold values from -0.3125 to 0.3125
- expand_bias: bfloat16 [1536], replicated, may hold values from -4 to 4
- shrink_weight: bfloat16 [1536, 384], replicated, may hold values from -0.15625 to 0.15625
- shrink_bias: bfloat16 [384], replicated, may hold values from -4 to 4
Outputs:
- output: bfloat16 [4, 4, 1024, 384], P('grp', None, 'seq')
- grad_tokens: float32 [4, 4, 1024, 384], P('grp', None, 'seq')
- grad_lead_table: float32 [8, 384], replicated
- grad_modulation_weight: float32 [384, 2304], replicated
- grad_modulation_bias: float32 [2304], replicated
- grad_attend_weight: float32 [384, 1152], replicated
- grad_output_weight: float32 [384, 384], replicated
- grad_output_bias: float32 [384], replicated
- grad_expand_weight: float32 [384, 1536], replicated
- grad_expand_bias: float32 [1536], replicated
- grad_shrink_weight: float32 [1536, 384], replicated
- grad_shrink_bias: float32 [384], replicated
The draws below stay inside these ranges and needn't reach their ends.
Inputs may be any that keep to these rules, and one draw needn't show every extreme that they name: Each sequence's 8 lengths are positive and sum to 1024. In every group one sequence holds a document of 1017 positions.
All inputs are finite; a program needn't handle non-finite values. No bound on the sum of `valid_mask` on one device may be relied on, other than what follows from the above.
Results may differ from the reference program's by a relative error of at most 0.02.
Values may be sent and summed in bfloat16 or wider, within the bound.
No kernel may reach another device: no remote copies, remote signals or barrier semaphores. Data moves between devices by JAX's collectives and lax.ppermute only.
A program may use at most 320 MiB of HBM per device.

```python
import math
import jax
import jax.numpy as jnp
from jax import lax

D = 384
HEADS = 6
HD = 64
FF = 1536
LEADS = 8
DOCS = 8
SEQS = 4
GROUPS = 4
SEQ_LEN = 1024


def sequence_lengths(cut_key, long_flag, long_slot):
    cuts = jax.random.permutation(cut_key, SEQ_LEN - 1)[:DOCS - 1] + 1
    cuts = jnp.sort(cuts.astype(jnp.int32))
    bounds = jnp.concatenate([jnp.zeros((1,), jnp.int32), cuts, jnp.full((1,), SEQ_LEN, jnp.int32)])
    spread = bounds[1:] - bounds[:-1]
    documents = jnp.arange(DOCS, dtype=jnp.int32)
    single = jnp.where(documents == long_slot, SEQ_LEN - DOCS + 1, 1).astype(jnp.int32)
    return jnp.where(long_flag, single, spread).astype(jnp.int32)


def draw_lengths(key, part):
    key = jax.random.fold_in(key, 11)
    pick_key, slot_key, cut_key = jax.random.split(key, 3)
    long_sequence = jax.random.randint(pick_key, (GROUPS,), 0, SEQS)
    long_slots = jax.random.randint(slot_key, (GROUPS * SEQS,), 0, DOCS)
    cut_keys = jax.random.split(cut_key, GROUPS * SEQS)
    long_flags = (jnp.arange(SEQS)[None, :] == long_sequence[:, None]).reshape(-1)
    drawn = jax.vmap(sequence_lengths)(cut_keys, long_flags, long_slots)
    return drawn.reshape(GROUPS, SEQS, DOCS).astype(jnp.int32)


def set_ends(values, stream_key, low, top_value):
    shape = values.shape
    place = [jax.random.randint(jax.random.fold_in(stream_key, axis), (), 0, shape[axis]) for axis in range(len(shape))]
    values = values.at[tuple(place)].set(low)
    longest = shape.index(max(shape))
    place[longest] = (place[longest] + 1) % shape[longest]
    return values.at[tuple(place)].set(top_value)


def shard_levels(key, extent, pieces, smallest, top_value):
    loudness, own = 1.0, jax.random.fold_in(key, 6)
    for axis_at, blocks in pieces:
        heights = jnp.exp(jax.random.uniform(jax.random.fold_in(own, axis_at), (blocks,), jnp.float32, smallest / len(pieces), top_value / len(pieces)))
        loudness = loudness * jnp.repeat(heights, extent[axis_at] // blocks).reshape([-1 if axis == axis_at else 1 for axis in range(len(extent))])
    return loudness


def scatter_about(own_key, dims, deviation, bound, cuts=(), kind=jnp.bfloat16):
    entries = jax.random.normal(own_key, dims, jnp.float32) * deviation
    if len(cuts) > 0:
        entries = shard_levels(own_key, dims, cuts, -0.22, 0.18) * entries
    return jnp.clip(entries, min=-bound, max=bound).astype(kind)


def setup_inputs(seed: int = 0) -> dict:
    key_of = jax.random.split(jax.random.key(seed), 17)
    tokens = scatter_about(key_of[0], (GROUPS, SEQS, SEQ_LEN, D), 1.0, 6.0, ((0, 4), (2, 8)))
    cotangent = scatter_about(key_of[1], (GROUPS, SEQS, SEQ_LEN, D), 1.0, 6.0, ((0, 4), (2, 8)))
    lengths = draw_lengths(jax.random.fold_in(key_of[16], 71), 0)
    valid_mask = set_ends((jax.random.randint(key_of[3], (GROUPS, SEQS, SEQ_LEN), 0, 8) < 7).astype(jnp.int32), jax.random.fold_in(key_of[3], 1), 0, 1)
    lead_index = set_ends(jax.random.randint(key_of[4], (GROUPS,), 0, LEADS), jax.random.fold_in(key_of[4], 1), 0, LEADS - 1).astype(jnp.int32)
    sample_counts = set_ends(jax.random.randint(key_of[5], (GROUPS,), 1, 17), jax.random.fold_in(key_of[5], 1), 1, 16).astype(jnp.int32)
    lead_table = scatter_about(key_of[6], (LEADS, D), 1.0, 6.0)
    modulation_weight = scatter_about(key_of[7], (D, 6 * D), D ** -0.5, 0.3125)
    modulation_bias = scatter_about(key_of[8], (6 * D,), 0.3, 4.0)
    attend_weight = scatter_about(key_of[9], (D, 3 * D), D ** -0.5, 0.3125)
    output_weight = scatter_about(key_of[10], (D, D), (D // 16) ** -0.5, 1.25)
    output_bias = scatter_about(key_of[11], (D,), 0.3, 4.0)
    expand_weight = scatter_about(key_of[12], (D, FF), D ** -0.5, 0.3125)
    expand_bias = scatter_about(key_of[13], (FF,), 0.3, 4.0)
    shrink_weight = scatter_about(key_of[14], (FF, D), FF ** -0.5, 0.15625)
    shrink_bias = scatter_about(key_of[15], (D,), 0.3, 4.0)
    return {"tokens": tokens, "cotangent": cotangent, "lengths": lengths, "valid_mask": valid_mask, "lead_index": lead_index, "sample_counts": sample_counts, "lead_table": lead_table, "modulation_weight": modulation_weight, "modulation_bias": modulation_bias, "attend_weight": attend_weight, "output_weight": output_weight, "output_bias": output_bias, "expand_weight": expand_weight, "expand_bias": expand_bias, "shrink_weight": shrink_weight, "shrink_bias": shrink_bias}


PRECISE = lax.Precision.HIGHEST
EPSILON = 1e-06
MASKED = -1e+30

@jax.custom_vjp
def low(v):
    return lax.optimization_barrier(v.astype(jnp.bfloat16)).astype(jnp.float32)

@jax.custom_vjp
def low_back(v):
    return v

def low_keep(v):
    return (low(v), None)

def low_pass(kept, grad):
    return (grad,)

def back_keep(v):
    return (v, None)

def back_low(kept, grad):
    return (low(grad),)
low.defvjp(low_keep, low_pass)
low_back.defvjp(back_keep, back_low)

def product(left, right):
    return jnp.dot(left, right, precision=PRECISE, preferred_element_type=jnp.float32)

def layer_norm(values):
    centred = values - lax.optimization_barrier(jnp.mean(values, axis=-1, keepdims=True))
    return centred * lax.rsqrt(lax.optimization_barrier(jnp.mean(centred * centred, axis=-1, keepdims=True)) + EPSILON)

def query_block(block_index, queries, key_heads, value_heads, segments, valid_mask):
    block_size = min(512, SEQ_LEN)
    first_row = block_index * block_size
    positions = jnp.arange(SEQ_LEN, dtype=jnp.int32)
    row_queries = lax.dynamic_slice_in_dim(queries, first_row, block_size, 0).reshape(block_size, HEADS, HD)
    row_segments = lax.dynamic_slice_in_dim(segments, first_row, block_size, 0)
    row_positions = first_row + jnp.arange(block_size, dtype=jnp.int32)
    raw_scores = jnp.einsum('qhd,khd->qhk', row_queries, key_heads, precision=PRECISE) * (1.0 / math.sqrt(HD))
    scores = low_back(raw_scores)
    allow_mask = (row_segments[:, None] == segments[None, :]) & ((valid_mask[None, :] > 0) | (row_positions[:, None] == positions[None, :]))
    scores = jnp.where(allow_mask[:, None, :], scores, MASKED)
    highest = lax.optimization_barrier(jnp.max(scores, axis=-1, keepdims=True))
    expo = jnp.exp(scores - highest)
    probs = expo / lax.optimization_barrier(jnp.sum(expo, axis=-1, keepdims=True))
    mixed = jnp.einsum('qhk,khd->qhd', low(probs), value_heads, precision=PRECISE)
    return mixed.reshape(block_size, D)

def sequence_attention(queries, key_rows, value_rows, segments, valid_mask):
    block_size = min(512, SEQ_LEN)
    key_heads = key_rows.reshape(SEQ_LEN, HEADS, HD)
    value_heads = value_rows.reshape(SEQ_LEN, HEADS, HD)
    block_rows = jax.checkpoint(query_block)
    blocks = lax.map(lambda block_index: block_rows(block_index, queries, key_heads, value_heads, segments, valid_mask), jnp.arange(SEQ_LEN // block_size, dtype=jnp.int32))
    return blocks.reshape(SEQ_LEN, D)

def group_forward(tokens, lead_table, modulation_weight, modulation_bias, attend_weight, output_weight, output_bias, expand_weight, expand_bias, shrink_weight, shrink_bias, onehot, segments, valid_mask):
    embedding = product(onehot[None, :], lead_table)[0]
    lifted = low(jax.nn.silu(embedding))
    modulation = product(lifted[None, :], modulation_weight)[0] + modulation_bias
    shift_one, scale_one, gate_one, shift_two, scale_two, gate_two = jnp.split(modulation, 6)
    inputs = tokens.reshape(SEQS * SEQ_LEN, D)
    mixed_one = low(layer_norm(inputs) * (1.0 + scale_one) + shift_one)
    projected = low_back(low(product(mixed_one, attend_weight)))
    queries = projected[:, :D].reshape(SEQS, SEQ_LEN, D)
    key_rows = projected[:, D:2 * D].reshape(SEQS, SEQ_LEN, D)
    value_rows = projected[:, 2 * D:].reshape(SEQS, SEQ_LEN, D)
    attended = lax.map(lambda item: sequence_attention(*item), (queries, key_rows, value_rows, segments, valid_mask))
    attended = low_back(low(attended.reshape(SEQS * SEQ_LEN, D)))
    branch_one = low_back(product(attended, output_weight) + output_bias)
    residual = inputs + gate_one * branch_one
    mixed_two = low(layer_norm(residual) * (1.0 + scale_two) + shift_two)
    hidden = low_back(product(mixed_two, expand_weight) + expand_bias)
    activated = low(jax.nn.gelu(hidden, approximate=True))
    branch_two = low_back(product(activated, shrink_weight) + shrink_bias)
    return (residual + gate_two * branch_two).reshape(SEQS, SEQ_LEN, D)

def reference(tokens, cotangent, lengths, valid_mask, lead_index, sample_counts, lead_table, modulation_weight, modulation_bias, attend_weight, output_weight, output_bias, expand_weight, expand_bias, shrink_weight, shrink_bias):
    weights = tuple((item.astype(jnp.float32) for item in (lead_table, modulation_weight, modulation_bias, attend_weight, output_weight, output_bias, expand_weight, expand_bias, shrink_weight, shrink_bias)))
    counted = sample_counts.astype(jnp.float32)
    shares = counted / jnp.sum(counted) * (GROUPS / math.sqrt(SEQS * SEQ_LEN))
    positions = jnp.arange(SEQ_LEN, dtype=jnp.int32)
    outputs = []
    input_grads = []
    totals = [jnp.zeros_like(item) for item in weights]
    for group in range(GROUPS):
        onehot = (jnp.arange(LEADS, dtype=jnp.int32) == lead_index[group].astype(jnp.int32)).astype(jnp.float32)
        doc_ends = jnp.cumsum(lengths[group], axis=-1).astype(jnp.int32)
        segments = lax.optimization_barrier(jnp.sum((positions[None, :, None] >= doc_ends[:, None, :]).astype(jnp.int32), axis=-1)).astype(jnp.int32)
        group_valid = valid_mask[group]

        def forward(group_tokens, *params):
            return group_forward(group_tokens, *params, onehot, segments, group_valid)
        result, pullback = jax.vjp(forward, tokens[group].astype(jnp.float32), *weights)
        grads = pullback(cotangent[group].astype(jnp.float32))
        outputs.append(result)
        input_grads.append(grads[0])
        totals = [total + shares[group] * grad for total, grad in zip(totals, grads[1:])]
    return (jnp.stack(outputs).astype(jnp.bfloat16), jnp.stack(input_grads), totals[0], totals[1], totals[2], totals[3], totals[4], totals[5], totals[6], totals[7], totals[8], totals[9])
```

```python
from functools import partial
import math

import jax
import jax.numpy as jnp
from jax import lax
from jax.sharding import PartitionSpec as P

HEADS = 6
LEADS = 8

EPSILON = 1e-06
MASKED = -1e30

bf16 = jnp.bfloat16
f32 = jnp.float32


def normalize(values):
    centred = values - jnp.mean(values, axis=-1, keepdims=True)
    inverse = lax.rsqrt(jnp.mean(centred * centred, axis=-1, keepdims=True) + EPSILON)
    return (centred * inverse, inverse)


def normalize_back(grad, normed, inverse):
    return inverse * (
        grad
        - jnp.mean(grad, axis=-1, keepdims=True)
        - normed * jnp.mean(grad * normed, axis=-1, keepdims=True)
    )


def row_product(left, right):
    return lax.dot_general(left, right, (((0,), (0,)), ((), ())), preferred_element_type=f32)


def back_product(grad, weight):
    return lax.dot_general(grad, weight, (((1,), (1,)), ((), ())), preferred_element_type=f32)


def product(left, right):
    return jnp.dot(left, right, preferred_element_type=f32)


def total(parts):
    result = parts[0].astype(f32)
    for part in parts[1:]:
        result = result + part.astype(f32)
    return result


def owner_shift(seq_size, owners, share, step):
    return [(d, ((d // share + step) % owners) * share + d % share) for d in range(seq_size)]


def rows_to_owner(blocks, owner, share):
    owners = blocks.shape[0]
    seq_size = lax.axis_size("seq")
    pieces = []
    for step in range(owners):
        block = lax.dynamic_index_in_dim(blocks, (owner + step) % owners, 0, False)
        if step:
            block = lax.ppermute(block, "seq", owner_shift(seq_size, owners, share, step))
        pieces.append(block)
    return pieces


def rows_from_owner(pieces, owner, share):
    owners = len(pieces)
    seq_size = lax.axis_size("seq")
    blocks = jnp.zeros((owners,) + pieces[0].shape, pieces[0].dtype)
    for step in range(owners):
        block = pieces[step]
        if step:
            block = lax.ppermute(block, "seq", owner_shift(seq_size, owners, share, owners - step))
        blocks = lax.dynamic_update_index_in_dim(blocks, block, (owner + step) % owners, 0)
    return blocks


def share_rows(rows, rank, share):
    seq_size = lax.axis_size("seq")
    if share == 2:
        return lax.ppermute(rows, "seq", [(d, d ^ 1) for d in range(seq_size)])
    groups = [list(range(first, first + share)) for first in range(0, seq_size, share)]
    gathered = lax.all_gather(rows, "seq", axis_index_groups=groups)
    gathered = jnp.roll(gathered, -rank, axis=0)[1:]
    return gathered.reshape((share - 1) * rows.shape[0], rows.shape[1])


def return_rows(rest, rank, share):
    seq_size = lax.axis_size("seq")
    if share == 2:
        return lax.ppermute(rest, "seq", [(d, d ^ 1) for d in range(seq_size)]).astype(f32)
    groups = [list(range(first, first + share)) for first in range(0, seq_size, share)]
    parts = rest.reshape(share - 1, rest.shape[0] // (share - 1), rest.shape[1])
    parts = jnp.concatenate([jnp.zeros_like(parts[:1]), parts], axis=0)
    parts = jnp.roll(parts, rank, axis=0)
    return lax.psum_scatter(parts, "seq", scatter_dimension=0, axis_index_groups=groups).astype(f32)


def pair_perm(size, step):
    if size & (size - 1) == 0:
        return [(d, d ^ step) for d in range(size)]
    return [(d, (d + step) % size) for d in range(size)]


def partner(index, size, step):
    return index ^ step if size & (size - 1) == 0 else (index + step) % size


def source(index, size, step):
    return index ^ step if size & (size - 1) == 0 else (index - step) % size


def line_perm(seq_size, step):
    return [(d, (d + 2 * step) % seq_size) for d in range(seq_size)]


def line_sum(values):
    seq_size = lax.axis_size("seq")
    length = seq_size // 2
    if length > 4:
        groups = [list(range(core, seq_size, 2)) for core in range(2)]
        return lax.psum(values, "seq", axis_index_groups=groups)
    received = [lax.ppermute(values, "seq", line_perm(seq_size, step)) for step in range(1, length)]
    return total([values] + received).astype(values.dtype)


def sum_everywhere(values):
    seq_size = lax.axis_size("seq")
    grp_size = lax.axis_size("grp")
    core = lax.axis_index("seq") % 2
    group = lax.axis_index("grp")
    half = values.shape[0] // 2
    quarter = half // grp_size
    take = partial(lax.dynamic_slice_in_dim, axis=0)
    swap = [(d, d ^ 1) for d in range(seq_size)]
    received = lax.ppermute(take(values, (1 - core) * half, half), "seq", swap)
    held = total([take(values, core * half, half), received]).astype(bf16)
    received = [
        lax.ppermute(
            take(held, partner(group, grp_size, step) * quarter, quarter),
            "grp",
            pair_perm(grp_size, step),
        )
        for step in range(1, grp_size)
    ]
    held = total([take(held, group * quarter, quarter)] + received).astype(bf16)
    held = line_sum(held)
    parts = jnp.stack(
        [held] + [lax.ppermute(held, "grp", pair_perm(grp_size, step)) for step in range(1, grp_size)]
    )
    held = jnp.concatenate(
        [
            lax.dynamic_index_in_dim(parts, (group ^ other) if grp_size & (grp_size - 1) == 0 else (group - other) % grp_size, 0, False)
            for other in range(grp_size)
        ],
        axis=0,
    )
    received = lax.ppermute(held, "seq", swap)
    first = core == 0
    return jnp.concatenate(
        [jnp.where(first, held, received), jnp.where(first, received, held)], axis=0
    )


def sum_group(vector):
    seq_size = lax.axis_size("seq")
    swapped = lax.ppermute(vector, "seq", [(d, d ^ 1) for d in range(seq_size)])
    return line_sum(vector + swapped)


def gather_groups(vector):
    grp_size = lax.axis_size("grp")
    group = lax.axis_index("grp")
    parts = jnp.stack(
        [vector]
        + [lax.ppermute(vector, "grp", pair_perm(grp_size, step)) for step in range(1, grp_size)]
    )
    order = [source(jnp.int32(other), grp_size, group) if grp_size & (grp_size - 1) == 0 else (group - other) % grp_size for other in range(grp_size)]
    return jnp.stack([lax.dynamic_index_in_dim(parts, at, 0, False) for at in order])


def on_device(
    tokens,
    cotangent,
    lengths,
    valid_mask,
    lead_index,
    sample_counts,
    lead_table,
    modulation_weight,
    modulation_bias,
    attend_weight,
    output_weight,
    output_bias,
    expand_weight,
    expand_bias,
    shrink_weight,
    shrink_bias,
):
    owners = tokens.shape[1]
    block_rows = tokens.shape[2]
    width = tokens.shape[3]
    seq_size = lax.axis_size("seq")
    share = seq_size // owners
    seq_length = block_rows * seq_size
    rows = owners * block_rows
    head_width = width // HEADS
    score_scale = 1.0 / math.sqrt(head_width)
    place = lax.axis_index("seq")
    owner = place // share
    rank = place % share

    token_pieces = rows_to_owner(tokens[0], owner, share)
    own_tokens = jnp.concatenate(token_pieces, axis=0)
    rest_tokens = share_rows(own_tokens, rank, share)
    grad_pieces = rows_to_owner(cotangent[0], owner, share)
    grad_out = jnp.concatenate(grad_pieces, axis=0).astype(f32)

    steps = jnp.arange(owners, dtype=jnp.int32)
    ranks = (rank + jnp.arange(share, dtype=jnp.int32)) % share
    blocks = ((owner - steps) % owners)[None, :] * share + ranks[:, None]
    key_pos = (blocks[:, :, None] * block_rows + jnp.arange(block_rows, dtype=jnp.int32)).reshape(-1)
    doc_ends = jnp.cumsum(lax.dynamic_index_in_dim(lengths[0], owner, 0, False))
    key_seg = jnp.sum((key_pos[:, None] >= doc_ends[None, :]).astype(jnp.int32), axis=-1)
    key_valid = lax.dynamic_index_in_dim(valid_mask[0], owner, 0, False)[key_pos] > 0
    query_pos = key_pos[:rows]
    query_seg = key_seg[:rows]

    counted = sample_counts.astype(f32)
    shares = counted / jnp.sum(counted) * (counted.shape[0] / math.sqrt(owners * seq_length))
    group_share = lax.dynamic_index_in_dim(shares, lax.axis_index("grp"), 0, False)

    onehot = (jnp.arange(LEADS, dtype=jnp.int32) == lead_index[0]).astype(bf16)
    embedding = product(onehot[None, :], lead_table)[0]
    lifted = jax.nn.silu(embedding).astype(bf16)
    modulation = product(lifted[None, :], modulation_weight)[0] + modulation_bias.astype(f32)
    shift_one, scale_one, gate_one, shift_two, scale_two, gate_two = jnp.split(modulation, 6)

    inputs = own_tokens.astype(f32)
    all_inputs = jnp.concatenate([own_tokens, rest_tokens], axis=0).astype(f32)
    normed_all, inverse_all = normalize(all_inputs)
    mixed_all = (normed_all * (1.0 + scale_one) + shift_one).astype(bf16)
    mixed_one = mixed_all[:rows]
    heads = lambda v: v.reshape(v.shape[0], HEADS, head_width).transpose(1, 0, 2)
    queries = heads(product(mixed_one, attend_weight[:, :width]).astype(bf16))
    key_value = product(mixed_all, attend_weight[:, width:]).astype(bf16)
    keys = heads(key_value[:, :width])
    values = heads(key_value[:, width:])
    allow = (query_seg[:, None] == key_seg[None, :]) & (
        key_valid[None, :] | (query_pos[:, None] == key_pos[None, :])
    )
    scores = jnp.einsum("hqd,hkd->hqk", queries, keys, preferred_element_type=f32) * score_scale
    scores = jnp.where(allow[None], scores, MASKED)
    highest = jnp.max(scores, axis=-1, keepdims=True)
    expo = jnp.exp(scores - highest)
    probs = expo / jnp.sum(expo, axis=-1, keepdims=True)
    probs_low = probs.astype(bf16)
    attended_heads = jnp.einsum("hqk,hkd->hqd", probs_low, values, preferred_element_type=f32)
    attended_full = attended_heads.transpose(1, 0, 2).reshape(rows, width)
    attended = attended_full.astype(bf16)
    branch_one = product(attended, output_weight) + output_bias.astype(f32)
    residual = inputs + gate_one * branch_one
    normed_two, inverse_two = normalize(residual)
    mixed_two = (normed_two * (1.0 + scale_two) + shift_two).astype(bf16)
    hidden = product(mixed_two, expand_weight) + expand_bias.astype(f32)
    activated, gelu_back = jax.vjp(partial(jax.nn.gelu, approximate=True), hidden)
    activated_low = activated.astype(bf16)
    branch_two = product(activated_low, shrink_weight) + shrink_bias.astype(f32)
    output_rows = (residual + gate_two * branch_two).astype(bf16)
    output = rows_from_owner(
        [output_rows[i * block_rows : (i + 1) * block_rows] for i in range(owners)], owner, share
    )

    grad_gate_two = jnp.sum(grad_out * branch_two, axis=0)
    grad_two = (grad_out * gate_two).astype(bf16)
    grad_shrink = row_product(grad_two, activated_low)
    grad_shrink_bias = jnp.sum(grad_two.astype(f32), axis=0)
    grad_hidden = gelu_back(back_product(grad_two, shrink_weight))[0].astype(bf16)
    grad_expand = row_product(mixed_two, grad_hidden)
    grad_expand_bias = jnp.sum(grad_hidden.astype(f32), axis=0)
    packed_ff = (jnp.concatenate([grad_shrink, grad_expand], axis=1) * group_share).astype(bf16)
    summed_ff = sum_everywhere(packed_ff)

    grad_mixed_two = back_product(grad_hidden, expand_weight)
    grad_scale_two = jnp.sum(grad_mixed_two * normed_two, axis=0)
    grad_shift_two = jnp.sum(grad_mixed_two, axis=0)
    grad_residual = grad_out + normalize_back(
        grad_mixed_two * (1.0 + scale_two), normed_two, inverse_two
    )
    grad_gate_one = jnp.sum(grad_residual * branch_one, axis=0)
    grad_one = (grad_residual * gate_one).astype(bf16)
    grad_output = row_product(attended, grad_one)
    grad_output_bias = jnp.sum(grad_one.astype(f32), axis=0)
    grad_attended = back_product(grad_one, output_weight).astype(bf16)
    grad_heads = heads(grad_attended)
    deltas = jnp.sum(grad_heads.astype(f32) * attended_heads, axis=-1, keepdims=True)
    grad_probs = jnp.einsum("hqd,hkd->hqk", grad_heads, values, preferred_element_type=f32)
    grad_scores = (probs_low.astype(f32) * (grad_probs - deltas)).astype(bf16)
    grad_query = jnp.einsum("hqk,hkd->hqd", grad_scores, keys, preferred_element_type=f32)
    grad_key = jnp.einsum("hqk,hqd->hkd", grad_scores, queries, preferred_element_type=f32)
    grad_value = jnp.einsum("hqk,hqd->hkd", probs_low, grad_heads, preferred_element_type=f32)
    flat = lambda v: v.transpose(1, 0, 2).reshape(v.shape[1], width)
    grad_query = (flat(grad_query) * score_scale).astype(bf16)
    grad_kv = jnp.concatenate([flat(grad_key) * score_scale, flat(grad_value)], axis=1).astype(bf16)

    grad_attend = jnp.concatenate(
        [row_product(mixed_one, grad_query), row_product(mixed_all, grad_kv)], axis=1
    )
    packed_at = (jnp.concatenate([grad_attend, grad_output], axis=1) * group_share).astype(bf16)
    summed_at = sum_everywhere(packed_at)
    part_mixed = back_product(grad_kv, attend_weight[:, width:])
    own_part = part_mixed[:rows] + back_product(grad_query, attend_weight[:, :width])
    grad_shift_one = jnp.sum(own_part, axis=0) + jnp.sum(part_mixed[rows:], axis=0)
    grad_scale_one = jnp.sum(own_part * normed_all[:rows], axis=0) + jnp.sum(
        part_mixed[rows:] * normed_all[rows:], axis=0
    )
    grad_mixed_one = own_part + return_rows(part_mixed[rows:].astype(bf16), rank, share)
    grad_rows = grad_residual + normalize_back(
        grad_mixed_one * (1.0 + scale_one), normed_all[:rows], inverse_all[:rows]
    )
    grad_rows = grad_rows.astype(bf16)
    grad_tokens = rows_from_owner(
        [grad_rows[i * block_rows : (i + 1) * block_rows] for i in range(owners)], owner, share
    ).astype(f32)

    vector = jnp.concatenate(
        [
            grad_shift_one,
            grad_scale_one,
            grad_gate_one,
            grad_shift_two,
            grad_scale_two,
            grad_gate_two,
            grad_output_bias,
            grad_expand_bias,
            grad_shrink_bias,
        ]
    )
    vector = sum_group(vector * group_share)
    lead = jnp.broadcast_to(lead_index.astype(f32), (128,))
    gathered = gather_groups(jnp.concatenate([vector, embedding, lead]))
    modulation_grads = gathered[:, : 6 * width]
    ff = expand_bias.shape[0]
    bias_grads = jnp.sum(gathered[:, 6 * width : 8 * width + ff], axis=0)
    embeddings = gathered[:, 8 * width + ff : 9 * width + ff]
    leads = gathered[:, 9 * width + ff].astype(jnp.int32)
    lifted_all, silu_back = jax.vjp(jax.nn.silu, embeddings)
    lifted_all = lifted_all.astype(bf16).astype(f32)
    grad_mod_weight = jnp.sum(lifted_all[:, :, None] * modulation_grads[:, None, :], axis=0)
    grad_mod_bias = jnp.sum(modulation_grads, axis=0)
    grad_lifted = lax.dot_general(
        modulation_grads, modulation_weight.astype(f32), (((1,), (1,)), ((), ())),
        precision=lax.Precision.HIGHEST,
    )
    grad_embedding = silu_back(grad_lifted)[0]
    onehots = (jnp.arange(LEADS, dtype=jnp.int32)[None, :] == leads[:, None]).astype(f32)
    grad_table = jnp.sum(onehots[:, :, None] * grad_embedding[:, None, :], axis=0)
    return (
        output[None],
        grad_tokens[None],
        grad_table,
        grad_mod_weight,
        grad_mod_bias,
        summed_at[:, : 3 * width].astype(f32),
        summed_at[:, 3 * width :].astype(f32),
        bias_grads[:width],
        summed_ff[:, ff:].astype(f32),
        bias_grads[width : width + ff],
        summed_ff[:, :ff].astype(f32).T,
        bias_grads[width + ff :],
    )


def solution(mesh):
    rows = P("grp", None, "seq", None)
    placed = (rows, rows, P("grp", None, None), P("grp", None, None), P("grp")) + (P(),) * 11
    return jax.shard_map(
        on_device,
        mesh=mesh,
        in_specs=placed,
        out_specs=(rows, rows) + (P(),) * 10,
        check_vma=False,
    )
```

```python
from functools import partial
import math

import jax
import jax.numpy as jnp
from jax import lax
from jax.experimental import pallas as pl
from jax.experimental.pallas import tpu as pltpu
from jax.sharding import PartitionSpec as P

HEADS = 6
LEADS = 8

EPSILON = 1e-06
MASKED = -1e30

bf16 = jnp.bfloat16
f32 = jnp.float32


def normalize(values):
    centred = values - jnp.mean(values, axis=-1, keepdims=True)
    inverse = lax.rsqrt(jnp.mean(centred * centred, axis=-1, keepdims=True) + EPSILON)
    return (centred * inverse, inverse)


def normalize_back(grad, normed, inverse):
    return inverse * (
        grad
        - jnp.mean(grad, axis=-1, keepdims=True)
        - normed * jnp.mean(grad * normed, axis=-1, keepdims=True)
    )


def row_product(left, right):
    return lax.dot_general(left, right, (((0,), (0,)), ((), ())), preferred_element_type=f32)


def back_product(grad, weight):
    return lax.dot_general(grad, weight, (((1,), (1,)), ((), ())), preferred_element_type=f32)


def product(left, right):
    return jnp.dot(left, right, preferred_element_type=f32)


def total(parts):
    result = parts[0].astype(f32)
    for part in parts[1:]:
        result = result + part.astype(f32)
    return result


def owner_shift(seq_size, owners, share, step):
    return [(d, ((d // share + step) % owners) * share + d % share) for d in range(seq_size)]


def rows_to_owner(blocks, owner, share):
    owners = blocks.shape[0]
    seq_size = lax.axis_size("seq")
    pieces = []
    for step in range(owners):
        block = lax.dynamic_index_in_dim(blocks, (owner + step) % owners, 0, False)
        if step:
            block = lax.ppermute(block, "seq", owner_shift(seq_size, owners, share, step))
        pieces.append(block)
    return pieces


def rows_from_owner(pieces, share):
    owners = len(pieces)
    seq_size = lax.axis_size("seq")
    return [pieces[0]] + [
        lax.ppermute(pieces[step], "seq", owner_shift(seq_size, owners, share, owners - step))
        for step in range(1, owners)
    ]


def share_rows(rows, rank, share):
    seq_size = lax.axis_size("seq")
    if share == 2:
        return lax.ppermute(rows, "seq", [(d, d ^ 1) for d in range(seq_size)])
    groups = [list(range(first, first + share)) for first in range(0, seq_size, share)]
    gathered = lax.all_gather(rows, "seq", axis_index_groups=groups)
    gathered = jnp.roll(gathered, -rank, axis=0)[1:]
    return gathered.reshape((share - 1) * rows.shape[0], rows.shape[1])


def return_rows(rest, rank, share):
    seq_size = lax.axis_size("seq")
    if share == 2:
        return lax.ppermute(rest, "seq", [(d, d ^ 1) for d in range(seq_size)])
    groups = [list(range(first, first + share)) for first in range(0, seq_size, share)]
    parts = rest.reshape(share - 1, rest.shape[0] // (share - 1), rest.shape[1])
    parts = jnp.concatenate([jnp.zeros_like(parts[:1]), parts], axis=0)
    parts = jnp.roll(parts, rank, axis=0)
    return lax.psum_scatter(parts, "seq", scatter_dimension=0, axis_index_groups=groups)


def swap_cores(values):
    seq_size = lax.axis_size("seq")
    return lax.ppermute(values, "seq", [(d, d ^ 1) for d in range(seq_size)])


def line_size():
    return lax.axis_size("seq") // 2


def line_send(values, step):
    seq_size = lax.axis_size("seq")
    return lax.ppermute(values, "seq", [(d, (d + 2 * step) % seq_size) for d in range(seq_size)])


def plane_send(values, step):
    grp_size = lax.axis_size("grp")
    return lax.ppermute(values, "grp", [(d, plane_at(d, step)) for d in range(grp_size)])


def plane_at(group, step):
    grp_size = lax.axis_size("grp")
    if grp_size & (grp_size - 1) == 0:
        return group ^ step
    return (group + step) % grp_size


def plane_back(group, other):
    grp_size = lax.axis_size("grp")
    if grp_size & (grp_size - 1) == 0:
        return group ^ other
    return (group - other) % grp_size


def rows_at(values, at, count):
    return lax.dynamic_slice_in_dim(values, at * count, count, 0)


def plane_steps():
    return range(1, lax.axis_size("grp"))


def plane_parts(values):
    grp_size = lax.axis_size("grp")
    group = lax.axis_index("grp")
    count = values.shape[0] // grp_size
    return [rows_at(values, plane_at(group, step), count) for step in range(grp_size)]


def send_plane(parts):
    return [parts[0]] + [plane_send(parts[step], step) for step in plane_steps()]


def gather_plane(values):
    return [values] + [plane_send(values, step) for step in plane_steps()]


def line_parts(values):
    length = line_size()
    place = lax.axis_index("seq") // 2
    count = values.shape[0] // length
    return [rows_at(values, (place + step) % length, count) for step in range(length)]


def send_line(parts):
    return [parts[0]] + [line_send(parts[step], step) for step in range(1, len(parts))]


def sum_line(values):
    length = line_size()
    groups = [list(range(core, 2 * length, 2)) for core in range(2)]
    return lax.psum(values, "seq", axis_index_groups=groups)


def low_total(parts):
    return total(parts).astype(bf16)


def after(values, *others):
    return lax.optimization_barrier((values,) + others)[0]


def columns(values, width):
    return [values[:, at : at + width] for at in range(0, values.shape[1], width)]


def sum_share(values, share):
    seq_size = lax.axis_size("seq")
    groups = [list(range(first, first + share)) for first in range(0, seq_size, share)]
    return lax.psum(values, "seq", axis_index_groups=groups)


def after_all(values, *others):
    return lax.optimization_barrier(tuple(values) + others)[: len(values)]


def attention_kernel(
    score_scale, query, key, value, query_seg, query_pos, open_seg, key_pos, probs, attended, bias
):
    @pl.when(pl.program_id(1) == 0)
    def _():
        allow = (query_seg[...] == open_seg[...]) | (query_pos[...] == key_pos[...])
        bias[...] = jnp.where(allow, 0.0, MASKED)

    scaled = (query[0].astype(f32) * score_scale).astype(bf16)
    scores = back_product(scaled, key[0]) + bias[...]
    expo = jnp.exp(scores - jnp.max(scores, axis=1, keepdims=True))
    low = (expo * (1.0 / jnp.sum(expo, axis=1, keepdims=True))).astype(bf16)
    probs[0] = low
    attended[0] = product(low, value[0])


def attention(queries, keys, values, query_seg, query_pos, open_seg, key_pos, score_scale):
    head_count, rows, head_width = queries.shape
    key_count = keys.shape[1]
    step = max(32, min(rows, 2**18 // key_count))
    row_block = lambda i, h: (h, i, 0)
    key_block = lambda i, h: (h, 0, 0)
    size = head_count * rows * key_count
    return pl.pallas_call(
        partial(attention_kernel, score_scale),
        grid=(rows // step, head_count),
        in_specs=[
            pl.BlockSpec((1, step, head_width), row_block),
            pl.BlockSpec((1, key_count, head_width), key_block),
            pl.BlockSpec((1, key_count, head_width), key_block),
            pl.BlockSpec((step, 1), lambda i, h: (i, 0)),
            pl.BlockSpec((step, 1), lambda i, h: (i, 0)),
            pl.BlockSpec((1, key_count), lambda i, h: (0, 0)),
            pl.BlockSpec((1, key_count), lambda i, h: (0, 0)),
        ],
        out_specs=[
            pl.BlockSpec((1, step, key_count), row_block),
            pl.BlockSpec((1, step, head_width), row_block),
        ],
        out_shape=[
            jax.ShapeDtypeStruct((head_count, rows, key_count), bf16),
            jax.ShapeDtypeStruct((head_count, rows, head_width), f32),
        ],
        scratch_shapes=[pltpu.VMEM((step, key_count), f32)],
        compiler_params=pltpu.CompilerParams(vmem_limit_bytes=40 * 2**20),
        cost_estimate=pl.CostEstimate(
            flops=4 * size * head_width, bytes_accessed=2 * size, transcendentals=size
        ),
        name="attention",
    )(queries, keys, values, query_seg, query_pos, open_seg, key_pos)


GELU_RATE = math.sqrt(2.0 / math.pi)
GELU_CUBE = 0.044715
SHIFT_ONE, SCALE_ONE, GATE_ONE, SHIFT_TWO, SCALE_TWO, GATE_TWO, SHARE, EMBEDDING = range(8)


def inner(left, right):
    return row_product(left, right)


def column_sum(values):
    return jnp.sum(values, axis=0, keepdims=True)


def whole(*shape):
    return pl.BlockSpec(shape, lambda *_: (0,) * len(shape))


def kernel_params(mebibytes):
    return pltpu.CompilerParams(vmem_limit_bytes=mebibytes * 2**20)


def prepare_kernel(factor, place, lead, counts, table, weight, bias, attend_weight, mod, turned):
    width = table.shape[1]
    here = lax.broadcasted_iota(jnp.int32, table.shape, 0) == lead[0]
    embedding = column_sum(jnp.where(here, table[...].astype(f32), 0.0))
    lifted = (embedding / (1.0 + jnp.exp(-embedding))).astype(bf16)
    modulation = product(lifted, weight[...]) + bias[:, : weight.shape[1]]
    for part in range(6):
        mod[part : part + 1, :] = modulation[:, part * width : (part + 1) * width]
    every, mine = 0, 0
    for group in range(counts.shape[0]):
        every = every + counts[group]
        mine = mine + jnp.where(place[3] == group, counts[group], 0)
    row = jnp.zeros((1, width), jnp.int32)
    mod[SHARE : SHARE + 1, :] = (row + mine).astype(f32) / (row + every).astype(f32) * factor
    mod[EMBEDDING : EMBEDDING + 1, :] = embedding
    turned[...] = attend_weight[...].T


def prepare(place, lead, counts, table, weight, bias, attend_weight, positions):
    width = table.shape[1]
    operands = (table, weight, bias, attend_weight)
    shapes = [
        jax.ShapeDtypeStruct((8, width), f32),
        jax.ShapeDtypeStruct(attend_weight.shape[::-1], bf16),
    ]
    return pl.pallas_call(
        partial(prepare_kernel, counts.shape[0] / math.sqrt(positions)),
        grid=(1,),
        in_specs=[pl.BlockSpec(memory_space=pltpu.SMEM)] * 3 + [whole(*item.shape) for item in operands],
        out_specs=[whole(*item.shape) for item in shapes],
        out_shape=shapes,
        compiler_params=kernel_params(12),
        name="prepare",
    )(place, lead, counts, *operands)


def forward_kernel(
    head_width, score_scale, owners, place, lengths, own, rest, valid, mod, weight,
    expo, query, key_value, attended_wide, inverse_total, attended, bias,
):
    pair = pl.program_id(0)
    rows, width = own.shape
    key_count = rows + rest.shape[0]

    @pl.when(pair == 0)
    def _():
        shift, scale = mod[SHIFT_ONE : SHIFT_ONE + 1, :], 1.0 + mod[SCALE_ONE : SCALE_ONE + 1, :]
        first = (normalize(own[...].astype(f32))[0] * scale + shift).astype(bf16)
        query[...] = back_product(weight[:width, :], first).astype(bf16)
        key_value[:, :rows] = back_product(weight[width:, :], first).astype(bf16)
        for at in range(0, rest.shape[0], rows):
            part = normalize(rest[at : at + rows, :].astype(f32))[0]
            part = (part * scale + shift).astype(bf16)
            key_value[:, rows + at : 2 * rows + at] = back_product(weight[width:, :], part).astype(bf16)

        owner, rank = place[0], place[1]
        share = key_count // rows
        count = rows // owners
        ends = []
        for doc in range(lengths.shape[1]):
            ends.append(lengths[owner, doc] + (ends[-1] if doc else 0))

        def segment(positions):
            return sum((positions >= end).astype(jnp.int32) for end in ends)

        def block_at(r, step):
            return lax.rem(owner - step + owners, owners) * share + lax.rem(rank + r, share)

        lane = lax.broadcasted_iota(jnp.int32, (1, count), 1)
        query_pos = jnp.concatenate(
            [block_at(0, step) * count + lane for step in range(owners)], axis=1
        )
        query_seg = segment(query_pos)
        down = lax.broadcasted_iota(jnp.int32, (count, 1), 0)
        mine = lax.broadcasted_iota(jnp.int32, (owners, count), 0) == owner
        for r in range(share):
            for step in range(owners):
                block = block_at(r, step)
                key_pos = block * count + down
                open_rows = valid[:, pl.ds(pl.multiple_of(block * count, count), count)]
                open_rows = jnp.where((open_rows > 0) & mine, 1.0, 0.0)
                open_row = jnp.broadcast_to(column_sum(open_rows), (count, count))
                open_key = open_row.T[:, :1] > 0.5
                open_seg = jnp.where(open_key, segment(key_pos), -1)
                allow = (query_seg == open_seg) | (query_pos == key_pos)
                at = (r * owners + step) * count
                bias[at : at + count, :] = jnp.where(allow, 0.0, MASKED)

    for i in range(2):
        first = pl.multiple_of((2 * pair + i) * head_width, head_width)
        here = pl.ds(first, head_width)
        scaled = (query[here, :].astype(f32) * score_scale).astype(bf16)
        scores = inner(key_value[here, :], scaled) + bias[...]
        wide = jnp.exp(scores - jnp.max(scores, axis=0, keepdims=True))
        inverse = 1.0 / column_sum(wide)
        low = wide.astype(bf16)
        expo[i] = low
        inverse_total[i] = inverse
        values = key_value[pl.ds(pl.multiple_of(width + first, head_width), head_width), :]
        attended_wide[here, :] = product(values, low) * inverse

    @pl.when(pair == pl.num_programs(0) - 1)
    def _():
        attended[...] = attended_wide[...].T.astype(bf16)


def forward_attention(place, lengths, valid, own, rest, mod, weight):
    rows, width = own.shape
    key_count = rows + rest.shape[0]
    head_width = width // HEADS
    size = HEADS * rows * key_count
    scalars = pl.BlockSpec(memory_space=pltpu.SMEM)
    return pl.pallas_call(
        partial(forward_kernel, head_width, 1.0 / math.sqrt(head_width), lengths.shape[0]),
        grid=(HEADS // 2,),
        in_specs=[scalars, scalars] + [whole(*item.shape) for item in (own, rest, valid, mod, weight)],
        out_specs=[
            pl.BlockSpec((2, key_count, rows), lambda p: (p, 0, 0)),
            whole(width, rows),
            whole(2 * width, key_count),
            whole(width, rows),
            pl.BlockSpec((2, 1, rows), lambda p: (p, 0, 0)),
            whole(rows, width),
        ],
        out_shape=[
            pltpu.HBM((HEADS, key_count, rows), bf16),
            jax.ShapeDtypeStruct((width, rows), bf16),
            jax.ShapeDtypeStruct((2 * width, key_count), bf16),
            jax.ShapeDtypeStruct((width, rows), f32),
            jax.ShapeDtypeStruct((HEADS, 1, rows), f32),
            jax.ShapeDtypeStruct((rows, width), bf16),
        ],
        scratch_shapes=[pltpu.VMEM((key_count, rows), f32)],
        compiler_params=kernel_params(20),
        cost_estimate=pl.CostEstimate(
            flops=16 * size * head_width, bytes_accessed=2 * size, transcendentals=size
        ),
        name="forward_attention",
    )(place, lengths, own, rest, valid, mod, weight)


def middle_kernel(
    place, own, attended, cotangent, mod, bias, output_weight, expand_weight, shrink_weight,
    keep, send, packed_output, grad_attended, grad_residual, sums, *output,
):
    first_core = place[2] == 0
    rows, width = own.shape
    blocks = expand_weight.shape[1] // width
    row = lambda at: mod[at : at + 1, :]
    bias_row = lambda at: bias[:, at * width : (at + 1) * width]
    share = row(SHARE)
    scale_two = 1.0 + row(SCALE_TWO)
    branch_one = product(attended[...], output_weight[...]) + bias_row(6)
    residual = own[...].astype(f32) + row(GATE_ONE) * branch_one
    normed, inverse = normalize(residual)
    mixed = (normed * scale_two + row(SHIFT_TWO)).astype(bf16)
    wide = cotangent[...].astype(f32)
    grad_two = (wide * row(GATE_TWO)).astype(bf16)
    sums[...] = jnp.zeros_like(sums)
    branch_two = jnp.zeros((rows, width), f32) + bias_row(7 + blocks)
    grad_mixed = jnp.zeros((rows, width), f32)
    for block in range(blocks):
        part = slice(block * width, (block + 1) * width)
        hidden = product(mixed, expand_weight[:, part]) + bias_row(7 + block)
        square = hidden * hidden
        bent = jnp.tanh(GELU_RATE * hidden * (1.0 + GELU_CUBE * square))
        half = 0.5 + 0.5 * bent
        slope = half + 0.5 * hidden * (1.0 - bent * bent) * (
            GELU_RATE + (3.0 * GELU_CUBE * GELU_RATE) * square
        )
        active = (hidden * half).astype(bf16)
        branch_two = branch_two + product(active, shrink_weight[part, :])
        grad_hidden = (back_product(grad_two, shrink_weight[part, :]) * slope).astype(bf16)
        grad_shrink = inner(active, grad_two) * share
        grad_expand = inner(mixed, grad_hidden) * share
        keep[part, :] = jnp.where(first_core, grad_shrink, grad_expand).astype(bf16)
        send[part, :] = jnp.where(first_core, grad_expand, grad_shrink).astype(bf16)
        sums[7 + block : 8 + block, :] = column_sum(grad_hidden.astype(f32)) * share
        grad_mixed = grad_mixed + back_product(grad_hidden, expand_weight[:, part])
    result = (residual + row(GATE_TWO) * branch_two).astype(bf16)
    count = rows // len(output)
    for step in range(len(output)):
        output[step][...] = result[step * count : (step + 1) * count, :]
    sums[5:6, :] = column_sum(wide * branch_two) * share
    sums[7 + blocks : 8 + blocks, :] = column_sum(grad_two.astype(f32)) * share
    sums[4:5, :] = column_sum(grad_mixed * normed) * share
    sums[3:4, :] = column_sum(grad_mixed) * share
    grad_wide = wide + normalize_back(grad_mixed * scale_two, normed, inverse)
    grad_residual[...] = grad_wide
    sums[2:3, :] = column_sum(grad_wide * branch_one) * share
    grad_one = (grad_wide * row(GATE_ONE)).astype(bf16)
    sums[6:7, :] = column_sum(grad_one.astype(f32)) * share
    packed_output[...] = (inner(attended[...], grad_one) * share).astype(bf16)
    grad_attended[...] = back_product(output_weight[...], grad_one).astype(bf16)


def middle(
    owners, place, own, attended, cotangent, mod, bias, output_weight, expand_weight, shrink_weight
):
    rows, width = own.shape
    hidden = expand_weight.shape[1]
    operands = (
        own, attended, cotangent, mod, bias, output_weight, expand_weight, shrink_weight
    )
    shapes = [
        jax.ShapeDtypeStruct((hidden, width), bf16),
        jax.ShapeDtypeStruct((hidden, width), bf16),
        pltpu.HBM((width, width), bf16),
        pltpu.HBM((width, rows), bf16),
        pltpu.HBM((rows, width), f32),
        jax.ShapeDtypeStruct((16, width), f32),
    ] + [jax.ShapeDtypeStruct((rows // owners, width), bf16)] * owners
    return pl.pallas_call(
        middle_kernel,
        grid=(1,),
        in_specs=[pl.BlockSpec(memory_space=pltpu.SMEM)] + [whole(*item.shape) for item in operands],
        out_specs=[whole(*item.shape) for item in shapes],
        out_shape=shapes,
        compiler_params=kernel_params(16),
        cost_estimate=pl.CostEstimate(
            flops=16 * rows * width * hidden, bytes_accessed=2**24, transcendentals=rows * hidden
        ),
        name="middle",
    )(place, *operands)


def backward_kernel(
    head_width, score_scale, place, expo, query, key_value, attended_wide, inverse_total,
    grad_attended, own, rest, mod, weight, packed_output, sums_in, keep, send, own_part, sums,
    grad_query, grad_key, grad_value,
):
    pair = pl.program_id(0)
    rows, width = own.shape
    grad_keys, grad_values = [], []
    for i in range(2):
        first = pl.multiple_of((2 * pair + i) * head_width, head_width)
        here = pl.ds(first, head_width)
        scaled = (query[here, :].astype(f32) * score_scale).astype(bf16)
        keys = key_value[here, :]
        values = key_value[pl.ds(pl.multiple_of(width + first, head_width), head_width), :]
        grads = (grad_attended[here, :].astype(f32) * inverse_total[i]).astype(bf16)
        delta = column_sum(grads.astype(f32) * attended_wide[here, :])
        low = expo[i]
        grad_scores = (low.astype(f32) * (inner(values, grads) - delta)).astype(bf16)
        grad_values.append(back_product(low, grads))
        grad_keys.append(back_product(grad_scores, scaled))
        grad_query[here, :] = (product(keys, grad_scores) * score_scale).astype(bf16)
    grad_key[pair] = jnp.concatenate(grad_keys, axis=1).astype(bf16)
    grad_value[pair] = jnp.concatenate(grad_values, axis=1).astype(bf16)

    @pl.when(pair == pl.num_programs(0) - 1)
    def _():
        row = lambda at: mod[at : at + 1, :]
        share = row(SHARE)
        shift, scale = row(SHIFT_ONE), 1.0 + row(SCALE_ONE)
        pairs = range(HEADS // 2)
        packed_key = jnp.zeros((width, width), f32)
        packed_value = jnp.zeros((width, width), f32)
        total_shift = jnp.zeros((1, width), f32)
        total_scale = jnp.zeros((1, width), f32)
        for at in range(0, rows + rest.shape[0], rows):
            here = slice(at, at + rows)
            source = own[...] if at == 0 else rest[at - rows : at, :]
            normed = normalize(source.astype(f32))[0]
            mixed = (normed * scale + shift).astype(bf16)
            keys = jnp.concatenate([grad_key[pair, here, :] for pair in pairs], axis=1)
            values = jnp.concatenate([grad_value[pair, here, :] for pair in pairs], axis=1)
            part = product(keys, weight[width : 2 * width, :]) + product(
                values, weight[2 * width :, :]
            )
            if at == 0:
                part = part + inner(grad_query[...], weight[:width, :])
                own_part[...] = part
                packed_query = product(grad_query[...], mixed).T
            else:
                send[2 * width + at - rows : 2 * width + at, :] = part.astype(bf16)
            packed_key = packed_key + inner(mixed, keys)
            packed_value = packed_value + inner(mixed, values)
            total_shift = total_shift + column_sum(part)
            total_scale = total_scale + column_sum(part * normed)
        first_core = place[2] == 0
        packed = [packed_query * share, packed_key * share, packed_value * share, packed_output[...].astype(f32)]
        for half in range(2):
            here = slice(half * width, (half + 1) * width)
            keep[here, :] = jnp.where(first_core, packed[half], packed[2 + half]).astype(bf16)
            send[here, :] = jnp.where(first_core, packed[2 + half], packed[half]).astype(bf16)
        sums[...] = sums_in[...]
        sums[0:1, :] = total_shift * share
        sums[1:2, :] = total_scale * share
        send[2 * width + rest.shape[0] :, :] = sums[...].astype(bf16)


def backward_attention(place, saved, grad_attended, own, rest, mod, weight, packed_output, sums):
    expo, query, key_value, attended_wide, inverse_total = saved
    rows, width = own.shape
    key_count = rows + rest.shape[0]
    head_width = width // HEADS
    size = HEADS * rows * key_count
    operands = (
        query, key_value, attended_wide, inverse_total, grad_attended, own, rest, mod, weight,
        packed_output, sums,
    )
    specs = [whole(*item.shape) for item in operands]
    specs[3] = pl.BlockSpec((2, 1, rows), lambda p: (p, 0, 0))
    shapes = [
        jax.ShapeDtypeStruct((2 * width, width), bf16),
        jax.ShapeDtypeStruct((2 * width + rest.shape[0] + sums.shape[0], width), bf16),
        jax.ShapeDtypeStruct((rows, width), f32),
        jax.ShapeDtypeStruct(sums.shape, f32),
    ]
    return pl.pallas_call(
        partial(backward_kernel, head_width, 1.0 / math.sqrt(head_width)),
        grid=(HEADS // 2,),
        in_specs=[
            pl.BlockSpec(memory_space=pltpu.SMEM),
            pl.BlockSpec((2, key_count, rows), lambda p: (p, 0, 0)),
        ]
        + specs,
        out_specs=[whole(*item.shape) for item in shapes],
        out_shape=shapes,
        scratch_shapes=[
            pltpu.VMEM((width, rows), bf16),
            pltpu.VMEM((HEADS // 2, key_count, 2 * head_width), bf16),
            pltpu.VMEM((HEADS // 2, key_count, 2 * head_width), bf16),
        ],
        compiler_params=kernel_params(16),
        cost_estimate=pl.CostEstimate(
            flops=32 * size * head_width, bytes_accessed=2 * size, transcendentals=0
        ),
        name="backward_attention",
    )(place, pltpu.with_memory_space_constraint(expo, pltpu.HBM), *operands)


def finish_kernel(own, part, received, grad_residual, mod, sums, *results):
    rows, width = own.shape
    count = rows // len(results)
    normed, inverse = normalize(own[...].astype(f32))
    first = received.shape[0] - rows - sums.shape[0]
    grad = (part[...] + received[first : first + rows, :].astype(f32)) * (1.0 + mod[SCALE_ONE : SCALE_ONE + 1, :])
    grad = (grad_residual[...] + normalize_back(grad, normed, inverse)).astype(bf16)
    both = (sums[...] + received[first + rows :, :].astype(f32)).astype(bf16)
    for step, result in enumerate(results):
        result[:count, :] = grad[step * count : (step + 1) * count, :]
        result[count:, :] = both


def finish_rows(owners, own, part, received, grad_residual, mod, sums):
    operands = (own, part, received, grad_residual, mod, sums)
    shape = (own.shape[0] // owners + sums.shape[0], own.shape[1])
    return pl.pallas_call(
        finish_kernel,
        grid=(1,),
        in_specs=[whole(*item.shape) for item in operands],
        out_specs=[whole(*shape)] * owners,
        out_shape=[jax.ShapeDtypeStruct(shape, bf16)] * owners,
        compiler_params=kernel_params(12),
        name="finish_rows",
    )(*operands)


def placed_kernel(owners, place, *refs):
    pieces, result = refs[:owners], refs[owners]
    for step in range(owners):
        result[lax.rem(place[0] + step, owners)] = pieces[step][...]


def placed(place, pieces):
    owners = len(pieces)
    shape = (owners,) + pieces[0].shape
    return pl.pallas_call(
        partial(placed_kernel, owners),
        grid=(1,),
        in_specs=[pl.BlockSpec(memory_space=pltpu.SMEM)] + [whole(*item.shape) for item in pieces],
        out_specs=whole(*shape),
        out_shape=jax.ShapeDtypeStruct(shape, pieces[0].dtype),
        compiler_params=kernel_params(8),
        name="placed",
    )(place, *pieces)


def placed_sums_kernel(owners, place, lead, mod, *refs):
    pieces, (result, vector) = refs[:owners], refs[owners:]
    count = result.shape[1]
    for step in range(owners):
        result[lax.rem(place[0] + step, owners)] = pieces[step][:count, :].astype(f32)
    below = total([piece[count:, :] for piece in pieces])
    row = lax.broadcasted_iota(jnp.int32, below.shape, 0)
    below = jnp.where(row == 12, mod[EMBEDDING : EMBEDDING + 1, :], below)
    below = jnp.where(row == 13, jnp.full(below.shape, lead[0]).astype(f32), below)
    vector[...] = below.astype(bf16)


def placed_sums(place, lead, mod, pieces):
    owners = len(pieces)
    below, width = 16, mod.shape[1]
    shapes = [
        jax.ShapeDtypeStruct((owners, pieces[0].shape[0] - below, width), f32),
        jax.ShapeDtypeStruct((below, width), bf16),
    ]
    return pl.pallas_call(
        partial(placed_sums_kernel, owners),
        grid=(1,),
        in_specs=[pl.BlockSpec(memory_space=pltpu.SMEM)] * 2
        + [whole(*mod.shape)]
        + [whole(*item.shape) for item in pieces],
        out_specs=[whole(*item.shape) for item in shapes],
        out_shape=shapes,
        compiler_params=kernel_params(8),
        name="placed_sums",
    )(place, lead, mod, *pieces)


def ordered_kernel(grp_size, line, count, targets, place, *refs):
    own, received, outputs = refs[:grp_size], refs[grp_size : 2 * grp_size], refs[2 * grp_size :]
    width = own[0].shape[1]
    core, group, at_line = place[2], place[3], place[4]

    def write(side, ref, b):
        for c in range(line):
            from_c = lax.rem(at_line - c + line, line)
            here = pl.ds(pl.multiple_of(from_c * count, count), count)
            first = ((side * grp_size + b) * line + c) * count
            output, row, column = targets[first // width]
            row = row + first % width
            outputs[output][row : row + count, column : column + width] = ref[here, :].astype(f32)

    def choose(side, refs_here):
        for step in range(grp_size):
            for g in range(grp_size):
                b = g ^ step if grp_size & (grp_size - 1) == 0 else (g - step) % grp_size

                @pl.when(group == g)
                def _():
                    write(side, refs_here[step], b)

    for side in range(2):

        @pl.when(core == side)
        def _():
            choose(side, own)
            choose(1 - side, received)


def ordered(place, own, rows, targets, shapes):
    line = 1 if line_size() > 4 else line_size()
    received = [swap_cores(part) for part in own]
    shapes = [jax.ShapeDtypeStruct(shape, f32) for shape in shapes]
    return pl.pallas_call(
        partial(ordered_kernel, len(own), line, rows // line, targets),
        grid=(1,),
        in_specs=[pl.BlockSpec(memory_space=pltpu.SMEM)]
        + [whole(rows, part.shape[1]) for part in own + received],
        out_specs=[whole(*item.shape) for item in shapes],
        out_shape=shapes,
        compiler_params=kernel_params(16),
        name="ordered",
    )(place, *own, *received)


def vectors_kernel(parts_count, *refs):
    parts = [ref[...].astype(f32) for ref in refs[:parts_count]]
    weight = refs[parts_count]
    grad_weight, grad_bias, table, biases = refs[parts_count + 1 :]
    width = parts[0].shape[1]
    biases[...] = total([part[6:12] for part in parts])
    stacked = jnp.concatenate([part[12:13] for part in parts] + [jnp.zeros((8 - parts_count, width), f32)])
    gate = 1.0 / (1.0 + jnp.exp(-stacked))
    lifted = (stacked * gate).astype(bf16).astype(f32).T
    grad_lifted = jnp.zeros((8, width), f32)
    for block in range(6):
        rows = [part[block : block + 1] for part in parts]
        here = slice(block * width, (block + 1) * width)
        grad_weight[:, here] = total([lifted[:, p : p + 1] * row for p, row in enumerate(rows)])
        grad_bias[:, here] = total(rows)
        rows = jnp.concatenate(rows + [jnp.zeros((8 - parts_count, width), f32)])
        high = rows.astype(bf16)
        low = (rows - high.astype(f32)).astype(bf16)
        grad_lifted = grad_lifted + back_product(high, weight[:, here]) + back_product(low, weight[:, here])
    grad_embedding = grad_lifted * gate * (1.0 + stacked * (1.0 - gate))
    lead = lax.broadcasted_iota(jnp.int32, (LEADS, width), 0).astype(f32)
    table[...] = total(
        [
            jnp.where(lead == parts[p][13:14], grad_embedding[p : p + 1], 0.0)
            for p in range(parts_count)
        ]
    )


def vectors(parts, first, weight):
    width = weight.shape[0]
    shapes = [weight.shape, (1, weight.shape[1]), (LEADS, width), (6, width)]
    shapes = [jax.ShapeDtypeStruct(shape, f32) for shape in shapes]
    return pl.pallas_call(
        partial(vectors_kernel, len(parts)),
        grid=(1,),
        in_specs=[pl.BlockSpec((16, width), lambda i: (first // 16, 0)) for _ in parts]
        + [whole(*weight.shape)],
        out_specs=[whole(*item.shape) for item in shapes],
        out_shape=shapes,
        compiler_params=kernel_params(16),
        name="vectors",
    )(*parts, weight)


def long_forward(owner, rank, share, lengths, valid, own, rest, mod, weight):
    rows, width = own.shape
    owners = lengths.shape[0]
    count = rows // owners
    steps = jnp.arange(owners, dtype=jnp.int32)
    ranks = (rank + jnp.arange(share, dtype=jnp.int32)) % share
    blocks = (((owner - steps) % owners)[None, :] * share + ranks[:, None]).reshape(-1, 1)
    key_pos = blocks * count + jnp.arange(count, dtype=jnp.int32)[None, :]
    doc_ends = jnp.cumsum(lax.dynamic_index_in_dim(lengths, owner, 0, False))
    key_seg = sum((key_pos >= doc_ends[doc]).astype(jnp.int32) for doc in range(doc_ends.shape[0]))
    own_valid = lax.dynamic_index_in_dim(valid, owner, 0, False).reshape(-1, count)
    key_valid = own_valid[blocks[:, 0]] > 0
    open_seg = jnp.where(key_valid, key_seg, -1).reshape(1, -1)
    key_pos = key_pos.reshape(1, -1)
    query_seg = key_seg.reshape(-1, 1)[:rows]
    query_pos = key_pos.reshape(-1, 1)[:rows]
    head_width = width // HEADS
    normed = normalize(jnp.concatenate([own, rest], axis=0).astype(f32))[0]
    mixed = (normed * (1.0 + mod[SCALE_ONE]) + mod[SHIFT_ONE]).astype(bf16)
    heads = lambda v: v.reshape(v.shape[0], HEADS, head_width).transpose(1, 0, 2)
    queries = heads(back_product(mixed[:rows], weight[:width]).astype(bf16))
    key_value = back_product(mixed, weight[width:]).astype(bf16)
    keys = heads(key_value[:, :width])
    values = heads(key_value[:, width:])
    probs, attended = attention(
        queries, keys, values, query_seg, query_pos, open_seg, key_pos, 1.0 / math.sqrt(head_width)
    )
    flat = attended.transpose(1, 0, 2).reshape(rows, width).astype(bf16)
    return ((probs, queries, keys, values, attended, normed, mixed), flat)


def long_backward(place, saved, grad_attended, own, rest, mod, weight, packed_output, sums):
    probs, queries, keys, values, attended, normed, mixed = saved
    rows, width = own.shape
    head_width = width // HEADS
    score_scale = 1.0 / math.sqrt(head_width)
    grad_heads = grad_attended.reshape(HEADS, head_width, rows).transpose(0, 2, 1)
    deltas = jnp.sum(grad_heads.astype(f32) * attended, axis=-1, keepdims=True)
    grad_probs = jnp.einsum("hqd,hkd->hqk", grad_heads, values, preferred_element_type=f32)
    grad_scores = (probs.astype(f32) * (grad_probs - deltas)).astype(bf16)
    grad_query = jnp.einsum("hqk,hkd->hqd", grad_scores, keys, preferred_element_type=f32)
    grad_key = jnp.einsum("hqk,hqd->hkd", grad_scores, queries, preferred_element_type=f32)
    grad_value = jnp.einsum("hqk,hqd->hkd", probs, grad_heads, preferred_element_type=f32)
    flat = lambda v: v.transpose(1, 0, 2).reshape(v.shape[1], width)
    grad_query = (flat(grad_query) * score_scale).astype(bf16)
    grad_key = (flat(grad_key) * score_scale).astype(bf16)
    grad_value = flat(grad_value).astype(bf16)
    part = product(grad_key, weight[width : 2 * width]) + product(grad_value, weight[2 * width :])
    part = jnp.concatenate([part[:rows] + product(grad_query, weight[:width]), part[rows:]], axis=0)
    share = mod[SHARE]
    first = jnp.concatenate([row_product(mixed[:rows], grad_query), row_product(mixed, grad_key)])
    first = (first * share).astype(bf16)
    second = jnp.concatenate(
        [(row_product(mixed, grad_value) * share).astype(bf16), packed_output]
    )
    first_core = place[2] == 0
    keep = jnp.where(first_core, first, second)
    send = jnp.where(first_core, second, first)
    total_rows = jnp.stack([jnp.sum(part, axis=0), jnp.sum(part * normed, axis=0)]) * share
    sums = jnp.concatenate([total_rows, sums[2:]], axis=0)
    send = jnp.concatenate([send, part[rows:].astype(bf16), sums.astype(bf16)])
    return (keep, send, part[:rows], sums)


def on_device(
    tokens,
    cotangent,
    lengths,
    valid_mask,
    lead_index,
    sample_counts,
    lead_table,
    modulation_weight,
    modulation_bias,
    attend_weight,
    output_weight,
    output_bias,
    expand_weight,
    expand_bias,
    shrink_weight,
    shrink_bias,
):
    owners = tokens.shape[1]
    block_rows = tokens.shape[2]
    width = tokens.shape[3]
    hidden_width = expand_bias.shape[0]
    seq_size = lax.axis_size("seq")
    share = seq_size // owners
    seq_length = block_rows * seq_size
    rows = owners * block_rows
    place = lax.axis_index("seq")
    owner = place // share
    rank = place % share

    where = jnp.stack([owner, rank, place % 2, lax.axis_index("grp"), place // 2]).astype(jnp.int32)

    token_pieces = rows_to_owner(tokens[0], owner, share)

    bias = [modulation_bias, output_bias, expand_bias, shrink_bias]
    bias = jnp.concatenate(bias).astype(f32)[None]
    mod, weight = prepare(
        where, lead_index, sample_counts, lead_table, modulation_weight, bias, attend_weight,
        owners * seq_length,
    )
    grad_pieces = rows_to_owner(after(cotangent[0], mod), owner, share)
    token_pieces = after_all(token_pieces, mod)
    own_tokens = jnp.concatenate(token_pieces, axis=0)
    rest_tokens = share_rows(own_tokens, rank, share)
    short = seq_length <= 2048
    if short:
        *saved, attended = forward_attention(
            where, lengths[0], valid_mask[0], own_tokens, rest_tokens, mod, weight
        )
    else:
        saved, attended = long_forward(
            owner, rank, share, lengths[0], valid_mask[0], own_tokens, rest_tokens, mod, weight
        )
    grad_out = jnp.concatenate(after_all(grad_pieces, attended), axis=0)
    ff_keep, ff_send, packed_output, grad_attended, grad_residual, sums, *output_pieces = middle(
        owners, where, own_tokens, attended, grad_out, mod, bias, output_weight, expand_weight,
        shrink_weight,
    )
    output_pieces = rows_from_owner(output_pieces, share)
    ff_core = low_total([ff_keep, swap_cores(ff_send)])
    ff_parts = send_plane(plane_parts(ff_core))
    grad_attended = after(grad_attended, ff_core)
    backward = backward_attention if short else long_backward
    held = backward(
        where, saved, grad_attended, own_tokens, rest_tokens, mod, weight, packed_output, sums
    )
    at_keep, send, own_part, sums = after_all(held, *ff_parts[1:], *output_pieces)
    ff_plane = low_total(ff_parts)
    line = line_size() <= 4
    if line:
        ff_parts = send_line(line_parts(ff_plane))
    if share == 2:
        received = swap_cores(send)
    else:
        received = swap_cores(send[: 2 * width])
        vector = sum_share(sums, share)
        rest_part = return_rows(send[2 * width : -sums.shape[0]], rank, share)
        received = jnp.concatenate([received, rest_part, (vector - sums).astype(bf16)])
    at_core = low_total([at_keep, received[: 2 * width]])
    at_slices = plane_parts(at_core)
    if line:
        ff_parts = after_all(ff_parts, *at_slices)
    at_parts = send_plane(at_slices)
    at_plane = low_total(at_parts)
    if line:
        ff_line = low_total(ff_parts)
        ff_pieces = send_line([ff_line] * line_size())
        at_line = low_total(send_line(line_parts(at_plane)))
        at_pieces = send_line([at_line] * line_size())
    else:
        ff_pieces = [sum_line(ff_plane)]
        at_pieces = [sum_line(at_plane)]
    finished = finish_rows(
        owners, own_tokens, own_part, after(received, *ff_pieces), grad_residual, mod, sums
    )
    grad_pieces = rows_from_owner(finished, share)
    ff_parts = gather_plane(jnp.concatenate(ff_pieces))
    grad_tokens, vector = placed_sums(where, lead_index, mod, grad_pieces)
    at_parts = gather_plane(jnp.concatenate(at_pieces + [vector]))
    ff_parts = list(after_all(ff_parts, vector, *at_pieces))
    ff_blocks = hidden_width // width
    targets = [(0, i * width, 0) for i in range(ff_blocks)] + [(1, 0, i * width) for i in range(ff_blocks)]
    grad_shrink, grad_expand = ordered(
        where, ff_parts, ff_parts[0].shape[0], targets, [shrink_weight.shape, expand_weight.shape]
    )
    output = placed(where, after_all(output_pieces, vector))
    at_parts = list(after_all(at_parts, grad_shrink, output))
    targets = [(0, 0, i * width) for i in range(3)] + [(1, 0, 0)]
    count = at_parts[0].shape[0] - vector.shape[0]
    grad_attend, grad_output = ordered(
        where, at_parts, count, targets, [attend_weight.shape, output_weight.shape]
    )
    grad_mod_weight, grad_mod_bias, grad_table, biases = vectors(at_parts, count, modulation_weight)
    return (
        output[None],
        grad_tokens[None],
        grad_table,
        grad_mod_weight,
        grad_mod_bias.reshape(-1),
        grad_attend,
        grad_output,
        biases[0],
        grad_expand,
        biases[1 : 1 + ff_blocks].reshape(-1),
        grad_shrink,
        biases[1 + ff_blocks],
    )


def solution(mesh):
    rows = P("grp", None, "seq", None)
    placed = (rows, rows, P("grp", None, None), P("grp", None, None), P("grp")) + (P(),) * 11
    return jax.shard_map(
        on_device,
        mesh=mesh,
        in_specs=placed,
        out_specs=(rows, rows) + (P(),) * 10,
        check_vma=False,
    )
```

```python
from functools import partial
import math

import jax
import jax.numpy as jnp
from jax import lax
from jax.experimental import pallas as pl
from jax.experimental.pallas import tpu as pltpu
from jax.sharding import PartitionSpec as P

HEADS = 6
LEADS = 8

EPSILON = 1e-06
MASKED = -1e30

bf16 = jnp.bfloat16
f32 = jnp.float32


def normalize(values):
    centred = values - jnp.mean(values, axis=-1, keepdims=True)
    inverse = lax.rsqrt(jnp.mean(centred * centred, axis=-1, keepdims=True) + EPSILON)
    return (centred * inverse, inverse)


def normalize_back(grad, normed, inverse):
    return inverse * (
        grad
        - jnp.mean(grad, axis=-1, keepdims=True)
        - normed * jnp.mean(grad * normed, axis=-1, keepdims=True)
    )


def row_product(left, right):
    return lax.dot_general(left, right, (((0,), (0,)), ((), ())), preferred_element_type=f32)


def back_product(grad, weight):
    return lax.dot_general(grad, weight, (((1,), (1,)), ((), ())), preferred_element_type=f32)


def product(left, right):
    return jnp.dot(left, right, preferred_element_type=f32)


def total(parts):
    result = parts[0].astype(f32)
    for part in parts[1:]:
        result = result + part.astype(f32)
    return result


def owner_shift(seq_size, owners, share, step):
    return [(d, ((d // share + step) % owners) * share + d % share) for d in range(seq_size)]


def rows_to_owner(blocks, owner, share):
    owners = blocks.shape[0]
    seq_size = lax.axis_size("seq")
    pieces = []
    for step in range(owners):
        block = lax.dynamic_index_in_dim(blocks, (owner + step) % owners, 0, False)
        if step:
            block = lax.ppermute(block, "seq", owner_shift(seq_size, owners, share, step))
        pieces.append(block)
    return pieces


def rows_from_owner(blocks, share):
    owners = blocks.shape[0]
    groups = [[owner * share + rank for owner in range(owners)] for rank in range(share)]
    return lax.all_to_all(blocks, "seq", 0, 0, axis_index_groups=groups)


def share_rows(rows, rank, share):
    seq_size = lax.axis_size("seq")
    if share == 2:
        return lax.ppermute(rows, "seq", [(d, d ^ 1) for d in range(seq_size)])
    groups = [list(range(first, first + share)) for first in range(0, seq_size, share)]
    gathered = lax.all_gather(rows, "seq", axis_index_groups=groups)
    gathered = jnp.roll(gathered, -rank, axis=0)[1:]
    return gathered.reshape((share - 1) * rows.shape[0], rows.shape[1])


def return_rows(rest, rank, share):
    seq_size = lax.axis_size("seq")
    if share == 2:
        return lax.ppermute(rest, "seq", [(d, d ^ 1) for d in range(seq_size)])
    groups = [list(range(first, first + share)) for first in range(0, seq_size, share)]
    parts = rest.reshape(share - 1, rest.shape[0] // (share - 1), rest.shape[1])
    parts = jnp.concatenate([jnp.zeros_like(parts[:1]), parts], axis=0)
    parts = jnp.roll(parts, rank, axis=0)
    return lax.psum_scatter(parts, "seq", scatter_dimension=0, axis_index_groups=groups)


def swap_cores(values):
    seq_size = lax.axis_size("seq")
    return lax.ppermute(values, "seq", [(d, d ^ 1) for d in range(seq_size)])


def line_size():
    return lax.axis_size("seq") // 2


def line_send(values, step):
    seq_size = lax.axis_size("seq")
    return lax.ppermute(values, "seq", [(d, (d + 2 * step) % seq_size) for d in range(seq_size)])


def plane_send(values, step):
    grp_size = lax.axis_size("grp")
    return lax.ppermute(values, "grp", [(d, plane_at(d, step)) for d in range(grp_size)])


def plane_at(group, step):
    grp_size = lax.axis_size("grp")
    if grp_size & (grp_size - 1) == 0:
        return group ^ step
    return (group + step) % grp_size


def plane_back(group, other):
    grp_size = lax.axis_size("grp")
    if grp_size & (grp_size - 1) == 0:
        return group ^ other
    return (group - other) % grp_size


def rows_at(values, at, count):
    return lax.dynamic_slice_in_dim(values, at * count, count, 0)


def plane_steps():
    return range(1, lax.axis_size("grp"))


def plane_parts(values):
    grp_size = lax.axis_size("grp")
    group = lax.axis_index("grp")
    count = values.shape[0] // grp_size
    return [rows_at(values, plane_at(group, step), count) for step in range(grp_size)]


def send_plane(parts):
    return [parts[0]] + [plane_send(parts[step], step) for step in plane_steps()]


def gather_plane(values):
    return [values] + [plane_send(values, step) for step in plane_steps()]


def line_parts(values):
    length = line_size()
    place = lax.axis_index("seq") // 2
    count = values.shape[0] // length
    return [rows_at(values, (place + step) % length, count) for step in range(length)]


def send_line(parts):
    return [parts[0]] + [line_send(parts[step], step) for step in range(1, len(parts))]


def line_exchange(values):
    length = line_size()
    groups = [list(range(core, 2 * length, 2)) for core in range(2)]
    return lax.all_to_all(values, "seq", 0, 0, axis_index_groups=groups)


def sum_line(values):
    length = line_size()
    groups = [list(range(core, 2 * length, 2)) for core in range(2)]
    return lax.psum(values, "seq", axis_index_groups=groups)


def low_total(parts):
    return total(parts).astype(bf16)


def after(values, *others):
    return lax.optimization_barrier((values,) + others)[0]


def columns(values, width):
    return [values[:, at : at + width] for at in range(0, values.shape[1], width)]


def sum_share(values, share):
    seq_size = lax.axis_size("seq")
    groups = [list(range(first, first + share)) for first in range(0, seq_size, share)]
    return lax.psum(values, "seq", axis_index_groups=groups)


def after_all(values, *others):
    return lax.optimization_barrier(tuple(values) + others)[: len(values)]


def attention_kernel(
    score_scale, query, key, value, query_seg, query_pos, open_seg, key_pos, probs, attended, bias
):
    @pl.when(pl.program_id(1) == 0)
    def _():
        allow = (query_seg[...] == open_seg[...]) | (query_pos[...] == key_pos[...])
        bias[...] = jnp.where(allow, 0.0, MASKED)

    scaled = (query[0].astype(f32) * score_scale).astype(bf16)
    scores = back_product(scaled, key[0]) + bias[...]
    expo = jnp.exp(scores - jnp.max(scores, axis=1, keepdims=True))
    low = (expo * (1.0 / jnp.sum(expo, axis=1, keepdims=True))).astype(bf16)
    probs[0] = low
    attended[0] = product(low, value[0])


def attention(queries, keys, values, query_seg, query_pos, open_seg, key_pos, score_scale):
    head_count, rows, head_width = queries.shape
    key_count = keys.shape[1]
    step = max(32, min(rows, 2**18 // key_count))
    row_block = lambda i, h: (h, i, 0)
    key_block = lambda i, h: (h, 0, 0)
    size = head_count * rows * key_count
    return pl.pallas_call(
        partial(attention_kernel, score_scale),
        grid=(rows // step, head_count),
        in_specs=[
            pl.BlockSpec((1, step, head_width), row_block),
            pl.BlockSpec((1, key_count, head_width), key_block),
            pl.BlockSpec((1, key_count, head_width), key_block),
            pl.BlockSpec((step, 1), lambda i, h: (i, 0)),
            pl.BlockSpec((step, 1), lambda i, h: (i, 0)),
            pl.BlockSpec((1, key_count), lambda i, h: (0, 0)),
            pl.BlockSpec((1, key_count), lambda i, h: (0, 0)),
        ],
        out_specs=[
            pl.BlockSpec((1, step, key_count), row_block),
            pl.BlockSpec((1, step, head_width), row_block),
        ],
        out_shape=[
            jax.ShapeDtypeStruct((head_count, rows, key_count), bf16),
            jax.ShapeDtypeStruct((head_count, rows, head_width), f32),
        ],
        scratch_shapes=[pltpu.VMEM((step, key_count), f32)],
        compiler_params=pltpu.CompilerParams(vmem_limit_bytes=40 * 2**20),
        cost_estimate=pl.CostEstimate(
            flops=4 * size * head_width, bytes_accessed=2 * size, transcendentals=size
        ),
        name="attention",
    )(queries, keys, values, query_seg, query_pos, open_seg, key_pos)


GELU_RATE = math.sqrt(2.0 / math.pi)
GELU_CUBE = 0.044715
SHIFT_ONE, SCALE_ONE, GATE_ONE, SHIFT_TWO, SCALE_TWO, GATE_TWO, SHARE, EMBEDDING = range(8)


def inner(left, right):
    return row_product(left, right)


def column_sum(values):
    return jnp.sum(values, axis=0, keepdims=True)


def whole(*shape):
    return pl.BlockSpec(shape, lambda *_: (0,) * len(shape))


def kernel_params(mebibytes):
    return pltpu.CompilerParams(vmem_limit_bytes=mebibytes * 2**20)


def prepare_kernel(factor, place, lead, counts, table, weight, bias, attend_weight, mod, turned):
    width = table.shape[1]
    here = lax.broadcasted_iota(jnp.int32, table.shape, 0) == lead[0]
    embedding = column_sum(jnp.where(here, table[...].astype(f32), 0.0))
    lifted = (embedding / (1.0 + jnp.exp(-embedding))).astype(bf16)
    modulation = product(lifted, weight[...]) + bias[:, : weight.shape[1]]
    for part in range(6):
        mod[part : part + 1, :] = modulation[:, part * width : (part + 1) * width]
    every, mine = 0, 0
    for group in range(counts.shape[0]):
        every = every + counts[group]
        mine = mine + jnp.where(place[3] == group, counts[group], 0)
    row = jnp.zeros((1, width), jnp.int32)
    mod[SHARE : SHARE + 1, :] = (row + mine).astype(f32) / (row + every).astype(f32) * factor
    mod[EMBEDDING : EMBEDDING + 1, :] = embedding
    turned[...] = attend_weight[...].T


def prepare(place, lead, counts, table, weight, bias, attend_weight, positions):
    width = table.shape[1]
    operands = (table, weight, bias, attend_weight)
    shapes = [
        jax.ShapeDtypeStruct((8, width), f32),
        jax.ShapeDtypeStruct(attend_weight.shape[::-1], bf16),
    ]
    return pl.pallas_call(
        partial(prepare_kernel, counts.shape[0] / math.sqrt(positions)),
        grid=(1,),
        in_specs=[pl.BlockSpec(memory_space=pltpu.SMEM)] * 3 + [whole(*item.shape) for item in operands],
        out_specs=[whole(*item.shape) for item in shapes],
        out_shape=shapes,
        compiler_params=kernel_params(12),
        name="prepare",
    )(place, lead, counts, *operands)


def forward_kernel(
    head_width, score_scale, owners, place, lengths, own, rest, valid, mod, weight,
    expo, query, key_value, attended_wide, inverse_total, attended, bias,
):
    pair = pl.program_id(0)
    rows, width = own.shape
    key_count = rows + rest.shape[0]

    @pl.when(pair == 0)
    def _():
        shift, scale = mod[SHIFT_ONE : SHIFT_ONE + 1, :], 1.0 + mod[SCALE_ONE : SCALE_ONE + 1, :]
        first = (normalize(own[...].astype(f32))[0] * scale + shift).astype(bf16)
        query[...] = back_product(weight[:width, :], first).astype(bf16)
        key_value[:, :rows] = back_product(weight[width:, :], first).astype(bf16)
        for at in range(0, rest.shape[0], rows):
            part = normalize(rest[at : at + rows, :].astype(f32))[0]
            part = (part * scale + shift).astype(bf16)
            key_value[:, rows + at : 2 * rows + at] = back_product(weight[width:, :], part).astype(bf16)

        owner, rank = place[0], place[1]
        share = key_count // rows
        count = rows // owners
        ends = []
        for doc in range(lengths.shape[1]):
            ends.append(lengths[owner, doc] + (ends[-1] if doc else 0))

        def segment(positions):
            return sum((positions >= end).astype(jnp.int32) for end in ends)

        def block_at(r, step):
            return lax.rem(owner - step + owners, owners) * share + lax.rem(rank + r, share)

        lane = lax.broadcasted_iota(jnp.int32, (1, count), 1)
        query_pos = jnp.concatenate(
            [block_at(0, step) * count + lane for step in range(owners)], axis=1
        )
        query_seg = segment(query_pos)
        down = lax.broadcasted_iota(jnp.int32, (count, 1), 0)
        mine = lax.broadcasted_iota(jnp.int32, (owners, count), 0) == owner
        for r in range(share):
            for step in range(owners):
                block = block_at(r, step)
                key_pos = block * count + down
                open_rows = valid[:, pl.ds(pl.multiple_of(block * count, count), count)]
                open_rows = jnp.where((open_rows > 0) & mine, 1.0, 0.0)
                open_row = jnp.broadcast_to(column_sum(open_rows), (count, count))
                open_key = open_row.T[:, :1] > 0.5
                open_seg = jnp.where(open_key, segment(key_pos), -1)
                allow = (query_seg == open_seg) | (query_pos == key_pos)
                at = (r * owners + step) * count
                bias[at : at + count, :] = jnp.where(allow, 0.0, MASKED)

    for i in range(2):
        first = pl.multiple_of((2 * pair + i) * head_width, head_width)
        here = pl.ds(first, head_width)
        scaled = (query[here, :].astype(f32) * score_scale).astype(bf16)
        scores = inner(key_value[here, :], scaled) + bias[...]
        wide = jnp.exp(scores - jnp.max(scores, axis=0, keepdims=True))
        inverse = 1.0 / column_sum(wide)
        low = wide.astype(bf16)
        expo[i] = low
        inverse_total[i] = inverse
        values = key_value[pl.ds(pl.multiple_of(width + first, head_width), head_width), :]
        attended_wide[here, :] = product(values, low) * inverse

    @pl.when(pair == pl.num_programs(0) - 1)
    def _():
        attended[...] = attended_wide[...].T.astype(bf16)


def forward_attention(place, lengths, valid, own, rest, mod, weight):
    rows, width = own.shape
    key_count = rows + rest.shape[0]
    head_width = width // HEADS
    size = HEADS * rows * key_count
    scalars = pl.BlockSpec(memory_space=pltpu.SMEM)
    return pl.pallas_call(
        partial(forward_kernel, head_width, 1.0 / math.sqrt(head_width), lengths.shape[0]),
        grid=(HEADS // 2,),
        in_specs=[scalars, scalars] + [whole(*item.shape) for item in (own, rest, valid, mod, weight)],
        out_specs=[
            pl.BlockSpec((2, key_count, rows), lambda p: (p, 0, 0)),
            whole(width, rows),
            whole(2 * width, key_count),
            whole(width, rows),
            pl.BlockSpec((2, 1, rows), lambda p: (p, 0, 0)),
            whole(rows, width),
        ],
        out_shape=[
            pltpu.HBM((HEADS, key_count, rows), bf16),
            jax.ShapeDtypeStruct((width, rows), bf16),
            jax.ShapeDtypeStruct((2 * width, key_count), bf16),
            jax.ShapeDtypeStruct((width, rows), f32),
            jax.ShapeDtypeStruct((HEADS, 1, rows), f32),
            jax.ShapeDtypeStruct((rows, width), bf16),
        ],
        scratch_shapes=[pltpu.VMEM((key_count, rows), f32)],
        compiler_params=kernel_params(20),
        cost_estimate=pl.CostEstimate(
            flops=16 * size * head_width, bytes_accessed=2 * size, transcendentals=size
        ),
        name="forward_attention",
    )(place, lengths, own, rest, valid, mod, weight)


def middle_kernel(
    place, own, attended, cotangent, mod, bias, output_weight, expand_weight, shrink_weight,
    keep, send, packed_output, grad_attended, grad_residual, sums, output,
):
    first_core = place[2] == 0
    rows, width = own.shape
    blocks = expand_weight.shape[1] // width
    row = lambda at: mod[at : at + 1, :]
    bias_row = lambda at: bias[:, at * width : (at + 1) * width]
    share = row(SHARE)
    scale_two = 1.0 + row(SCALE_TWO)
    branch_one = product(attended[...], output_weight[...]) + bias_row(6)
    residual = own[...].astype(f32) + row(GATE_ONE) * branch_one
    normed, inverse = normalize(residual)
    mixed = (normed * scale_two + row(SHIFT_TWO)).astype(bf16)
    wide = cotangent[...].astype(f32)
    grad_two = (wide * row(GATE_TWO)).astype(bf16)
    sums[...] = jnp.zeros_like(sums)
    branch_two = jnp.zeros((rows, width), f32) + bias_row(7 + blocks)
    grad_mixed = jnp.zeros((rows, width), f32)
    for block in range(blocks):
        part = slice(block * width, (block + 1) * width)
        hidden = product(mixed, expand_weight[:, part]) + bias_row(7 + block)
        square = hidden * hidden
        bent = jnp.tanh(GELU_RATE * hidden * (1.0 + GELU_CUBE * square))
        half = 0.5 + 0.5 * bent
        slope = half + 0.5 * hidden * (1.0 - bent * bent) * (
            GELU_RATE + (3.0 * GELU_CUBE * GELU_RATE) * square
        )
        active = (hidden * half).astype(bf16)
        branch_two = branch_two + product(active, shrink_weight[part, :])
        grad_hidden = (back_product(grad_two, shrink_weight[part, :]) * slope).astype(bf16)
        grad_shrink = inner(active, grad_two) * share
        grad_expand = inner(mixed, grad_hidden) * share
        keep[part, :] = jnp.where(first_core, grad_shrink, grad_expand).astype(bf16)
        send[part, :] = jnp.where(first_core, grad_expand, grad_shrink).astype(bf16)
        sums[7 + block : 8 + block, :] = column_sum(grad_hidden.astype(f32)) * share
        grad_mixed = grad_mixed + back_product(grad_hidden, expand_weight[:, part])
    result = (residual + row(GATE_TWO) * branch_two).astype(bf16)
    owners, count = output.shape[:2]
    for step in range(owners):
        output[lax.rem(place[0] - step + owners, owners)] = result[step * count : (step + 1) * count, :]
    sums[5:6, :] = column_sum(wide * branch_two) * share
    sums[7 + blocks : 8 + blocks, :] = column_sum(grad_two.astype(f32)) * share
    sums[4:5, :] = column_sum(grad_mixed * normed) * share
    sums[3:4, :] = column_sum(grad_mixed) * share
    grad_wide = wide + normalize_back(grad_mixed * scale_two, normed, inverse)
    grad_residual[...] = grad_wide
    sums[2:3, :] = column_sum(grad_wide * branch_one) * share
    grad_one = (grad_wide * row(GATE_ONE)).astype(bf16)
    sums[6:7, :] = column_sum(grad_one.astype(f32)) * share
    packed_output[...] = (inner(attended[...], grad_one) * share).astype(bf16)
    grad_attended[...] = back_product(output_weight[...], grad_one).astype(bf16)


def middle(
    owners, place, own, attended, cotangent, mod, bias, output_weight, expand_weight, shrink_weight
):
    rows, width = own.shape
    hidden = expand_weight.shape[1]
    operands = (
        own, attended, cotangent, mod, bias, output_weight, expand_weight, shrink_weight
    )
    shapes = [
        jax.ShapeDtypeStruct((hidden, width), bf16),
        jax.ShapeDtypeStruct((hidden, width), bf16),
        pltpu.HBM((width, width), bf16),
        pltpu.HBM((width, rows), bf16),
        pltpu.HBM((rows, width), f32),
        jax.ShapeDtypeStruct((16, width), f32),
        jax.ShapeDtypeStruct((owners, rows // owners, width), bf16),
    ]
    return pl.pallas_call(
        middle_kernel,
        grid=(1,),
        in_specs=[pl.BlockSpec(memory_space=pltpu.SMEM)] + [whole(*item.shape) for item in operands],
        out_specs=[whole(*item.shape) for item in shapes],
        out_shape=shapes,
        compiler_params=kernel_params(16),
        cost_estimate=pl.CostEstimate(
            flops=16 * rows * width * hidden, bytes_accessed=2**24, transcendentals=rows * hidden
        ),
        name="middle",
    )(place, *operands)


def backward_kernel(
    head_width, score_scale, place, expo, query, key_value, attended_wide, inverse_total,
    grad_attended, own, rest, mod, weight, packed_output, grad_residual, sums_in, keep, send,
    rest_part, own_part, sums,
    grad_query, grad_key, grad_value,
):
    pair = pl.program_id(0)
    rows, width = own.shape
    grad_keys, grad_values = [], []
    for i in range(2):
        first = pl.multiple_of((2 * pair + i) * head_width, head_width)
        here = pl.ds(first, head_width)
        scaled = (query[here, :].astype(f32) * score_scale).astype(bf16)
        keys = key_value[here, :]
        values = key_value[pl.ds(pl.multiple_of(width + first, head_width), head_width), :]
        grads = (grad_attended[here, :].astype(f32) * inverse_total[i]).astype(bf16)
        delta = column_sum(grads.astype(f32) * attended_wide[here, :])
        low = expo[i]
        grad_scores = (low.astype(f32) * (inner(values, grads) - delta)).astype(bf16)
        grad_values.append(back_product(low, grads))
        grad_keys.append(back_product(grad_scores, scaled))
        grad_query[here, :] = (product(keys, grad_scores) * score_scale).astype(bf16)
    grad_key[pair] = jnp.concatenate(grad_keys, axis=1).astype(bf16)
    grad_value[pair] = jnp.concatenate(grad_values, axis=1).astype(bf16)

    @pl.when(pair == pl.num_programs(0) - 1)
    def _():
        row = lambda at: mod[at : at + 1, :]
        share = row(SHARE)
        shift, scale = row(SHIFT_ONE), 1.0 + row(SCALE_ONE)
        pairs = range(HEADS // 2)
        packed_key = jnp.zeros((width, width), f32)
        packed_value = jnp.zeros((width, width), f32)
        total_shift = jnp.zeros((1, width), f32)
        total_scale = jnp.zeros((1, width), f32)
        for at in range(0, rows + rest.shape[0], rows):
            here = slice(at, at + rows)
            source = own[...] if at == 0 else rest[at - rows : at, :]
            normed, inverse = normalize(source.astype(f32))
            mixed = (normed * scale + shift).astype(bf16)
            keys = jnp.concatenate([grad_key[pair, here, :] for pair in pairs], axis=1)
            values = jnp.concatenate([grad_value[pair, here, :] for pair in pairs], axis=1)
            part = product(keys, weight[width : 2 * width, :]) + product(
                values, weight[2 * width :, :]
            )
            if at == 0:
                part = part + inner(grad_query[...], weight[:width, :])
                back = normalize_back(part * scale, normed, inverse)
                own_part[...] = (grad_residual[...] + back).astype(bf16)
                packed_query = product(grad_query[...], mixed).T
            else:
                rest_part[at - rows : at, :] = part.astype(bf16)
            packed_key = packed_key + inner(mixed, keys)
            packed_value = packed_value + inner(mixed, values)
            total_shift = total_shift + column_sum(part)
            total_scale = total_scale + column_sum(part * normed)
        first_core = place[2] == 0
        packed = [packed_query * share, packed_key * share, packed_value * share, packed_output[...].astype(f32)]
        half = width // 2
        for at, matrix in enumerate(packed):
            here = slice(at * half, (at + 1) * half)
            keep[here, :] = jnp.where(first_core, matrix[:half], matrix[half:]).astype(bf16)
            send[here, :] = jnp.where(first_core, matrix[half:], matrix[:half]).astype(bf16)
        sums[...] = sums_in[...]
        sums[0:1, :] = total_shift * share
        sums[1:2, :] = total_scale * share
        rest_part[rest.shape[0] :, :] = sums[...].astype(bf16)


def backward_attention(
    place, saved, grad_attended, own, rest, mod, weight, packed_output, grad_residual, sums
):
    expo, query, key_value, attended_wide, inverse_total = saved
    rows, width = own.shape
    key_count = rows + rest.shape[0]
    head_width = width // HEADS
    size = HEADS * rows * key_count
    operands = (
        query, key_value, attended_wide, inverse_total, grad_attended, own, rest, mod, weight,
        packed_output, grad_residual, sums,
    )
    specs = [whole(*item.shape) for item in operands]
    specs[3] = pl.BlockSpec((2, 1, rows), lambda p: (p, 0, 0))
    shapes = [
        jax.ShapeDtypeStruct((2 * width, width), bf16),
        jax.ShapeDtypeStruct((2 * width, width), bf16),
        jax.ShapeDtypeStruct((rest.shape[0] + sums.shape[0], width), bf16),
        jax.ShapeDtypeStruct((rows, width), bf16),
        jax.ShapeDtypeStruct(sums.shape, f32),
    ]
    return pl.pallas_call(
        partial(backward_kernel, head_width, 1.0 / math.sqrt(head_width)),
        grid=(HEADS // 2,),
        in_specs=[
            pl.BlockSpec(memory_space=pltpu.SMEM),
            pl.BlockSpec((2, key_count, rows), lambda p: (p, 0, 0)),
        ]
        + specs,
        out_specs=[whole(*item.shape) for item in shapes],
        out_shape=shapes,
        scratch_shapes=[
            pltpu.VMEM((width, rows), bf16),
            pltpu.VMEM((HEADS // 2, key_count, 2 * head_width), bf16),
            pltpu.VMEM((HEADS // 2, key_count, 2 * head_width), bf16),
        ],
        compiler_params=kernel_params(16),
        cost_estimate=pl.CostEstimate(
            flops=32 * size * head_width, bytes_accessed=2 * size, transcendentals=0
        ),
        name="backward_attention",
    )(place, pltpu.with_memory_space_constraint(expo, pltpu.HBM), *operands)


def finish_kernel(place, own, part, received, mod, result):
    rows, width = own.shape
    owners, count = result.shape[:2]
    normed, inverse = normalize(own[...].astype(f32))
    grad = received[:rows, :].astype(f32) * (1.0 + mod[SCALE_ONE : SCALE_ONE + 1, :])
    grad = (part[...].astype(f32) + normalize_back(grad, normed, inverse)).astype(bf16)
    for step in range(owners):
        at = lax.rem(place[0] - step + owners, owners)
        result[at] = grad[step * count : (step + 1) * count, :]


def finish_rows(owners, place, own, part, received, mod):
    operands = (own, part, received, mod)
    shape = (owners, own.shape[0] // owners, own.shape[1])
    return pl.pallas_call(
        finish_kernel,
        grid=(1,),
        in_specs=[pl.BlockSpec(memory_space=pltpu.SMEM)] + [whole(*item.shape) for item in operands],
        out_specs=whole(*shape),
        out_shape=jax.ShapeDtypeStruct(shape, bf16),
        compiler_params=kernel_params(12),
        name="finish_rows",
    )(place, *operands)


def line_total_kernel(sums, received, *refs):
    parts, result = refs[:-1], refs[-1]
    count = parts[0].shape[0]
    result[:count, :] = total([part[...] for part in parts]).astype(bf16)
    below = received[received.shape[0] - sums.shape[0] :, :].astype(f32)
    result[count:, :] = (sums[...] + below).astype(bf16)


def line_total(parts, sums, received):
    count, width = parts[0].shape
    below = sums.shape[0]
    return pl.pallas_call(
        line_total_kernel,
        grid=(1,),
        in_specs=[whole(*item.shape) for item in [sums, received] + parts],
        out_specs=whole(count + below, width),
        out_shape=jax.ShapeDtypeStruct((count + below, width), bf16),
        compiler_params=kernel_params(8),
        name="line_total",
    )(sums, received, *parts)


def with_lead(below, lead, mod):
    row = lax.broadcasted_iota(jnp.int32, below.shape, 0)
    below = jnp.where(row == 12, mod[EMBEDDING : EMBEDDING + 1, :], below)
    return jnp.where(row == 13, jnp.full(below.shape, lead).astype(f32), below).astype(bf16)


def line_join_kernel(lead, mod, *refs):
    parts, result = refs[:-1], refs[-1]
    count = (result.shape[0] - 16) // len(parts)
    for at, part in enumerate(parts):
        result[at * count : (at + 1) * count, :] = part[:count, :]
    below = total([part[count:, :] for part in parts])
    result[len(parts) * count :, :] = with_lead(below, lead[0], mod)


def line_join(lead, mod, parts):
    rows, width = parts[0].shape
    shape = (len(parts) * (rows - 16) + 16, width)
    return pl.pallas_call(
        line_join_kernel,
        grid=(1,),
        in_specs=[pl.BlockSpec(memory_space=pltpu.SMEM)]
        + [whole(*item.shape) for item in [mod] + parts],
        out_specs=whole(*shape),
        out_shape=jax.ShapeDtypeStruct(shape, bf16),
        compiler_params=kernel_params(8),
        name="line_join",
    )(lead, mod, *parts)


def picked(place, grp_size, own, received, side, b, write):
    group = place[3]
    for step in range(grp_size):
        here = (group ^ b if grp_size & (grp_size - 1) == 0 else lax.rem(group - b + grp_size, grp_size)) == step
        for ref, mine in ((own[step], True), (received[step], False)):

            @pl.when(here & ((place[2] == side) == mine))
            def _():
                write(ref)


def copy_line(place, line, count, ref, output, first):
    for c in range(line):
        from_c = lax.rem(place[4] - c + line, line)
        here = pl.ds(pl.multiple_of(from_c * count, count), count)
        output[first + c * count : first + (c + 1) * count, :] = ref[here, :].astype(f32)


def first_sums_kernel(grp_size, line, place, *refs):
    own, received = refs[:grp_size], refs[grp_size : 2 * grp_size]
    refs = refs[2 * grp_size :]
    weight, output, blocks = refs[:3]
    shrink, expand, grad_weight, copied, rows, table, grad_bias = refs[3:10]
    output_bias, expand_bias, shrink_bias, grad_lifted, sums = refs[10:]
    b = pl.program_id(0)
    width = table.shape[1]
    count = own[0].shape[0] - 16
    copied[...] = output[...]
    rows[...] = blocks[...].astype(f32)
    for side, target in enumerate((shrink, expand)):
        write = lambda ref: copy_line(place, line, count // line, ref, target, 0)
        picked(place, grp_size, own, received, side, b, write)

    parts = [part[count:, :].astype(f32) for part in own]
    pad = jnp.zeros((8 - grp_size, width), f32)
    stacked = jnp.concatenate([part[12:13] for part in parts] + [pad])
    gate = 1.0 / (1.0 + jnp.exp(-stacked))

    @pl.when(b == 0)
    def _():
        sums[...] = total(parts)
        grad_lifted[...] = jnp.zeros_like(grad_lifted)

    @pl.when(b < 3)
    def _():
        lifted = (stacked * gate).astype(bf16)
        line_of = lax.broadcasted_iota(jnp.int32, parts[0].shape, 0)
        for i in range(2):
            here = slice(i * width, (i + 1) * width)
            picks = [column_sum(jnp.where(line_of == 2 * b + i, part, 0.0)) for part in parts]
            picks = jnp.concatenate(picks + [pad]).astype(bf16)
            grad_weight[:, here] = inner(lifted, picks)
            grad_lifted[...] += back_product(picks, weight[:, here])

    @pl.when(b == pl.num_programs(0) - 1)
    def _():
        for at in range(6):
            grad_bias[at * width : (at + 1) * width] = sums[at]
        output_bias[...] = sums[6]
        for at in range(expand_bias.shape[0] // width):
            expand_bias[at * width : (at + 1) * width] = sums[7 + at]
        shrink_bias[...] = sums[7 + expand_bias.shape[0] // width]
        grad_embedding = grad_lifted[...] * gate * (1.0 + stacked * (1.0 - gate))
        lead = lax.broadcasted_iota(jnp.int32, (LEADS, width), 0).astype(f32)
        table[...] = total(
            [
                jnp.where(lead == part[13:14], grad_embedding[p : p + 1], 0.0)
                for p, part in enumerate(parts)
            ]
        )


def first_sums(place, own, weight, output, blocks):
    grp_size = len(own)
    line = 1 if line_size() > 4 else line_size()
    received = [swap_cores(part) for part in own]
    width = weight.shape[0]
    hidden = grp_size * width
    owners = blocks.shape[0]
    block = pl.BlockSpec((owners // grp_size,) + blocks.shape[1:], lambda b: (b, 0, 0))
    wide = pl.BlockSpec((width, 2 * width), lambda b: (0, jnp.minimum(b, 2)))
    return pl.pallas_call(
        partial(first_sums_kernel, grp_size, line),
        grid=(grp_size,),
        in_specs=[pl.BlockSpec(memory_space=pltpu.SMEM)]
        + [whole(*own[0].shape)] * (2 * grp_size)
        + [wide, block, block],
        out_specs=[
            pl.BlockSpec((width, width), lambda b: (b, 0)),
            pl.BlockSpec((width, width), lambda b: (0, b)),
            wide,
            block,
            block,
            whole(LEADS, width),
            whole(6 * width),
            whole(width),
            whole(hidden),
            whole(width),
        ],
        out_shape=[
            jax.ShapeDtypeStruct((hidden, width), f32),
            jax.ShapeDtypeStruct((width, hidden), f32),
            jax.ShapeDtypeStruct(weight.shape, f32),
            jax.ShapeDtypeStruct(output.shape, output.dtype),
            jax.ShapeDtypeStruct(blocks.shape, f32),
            jax.ShapeDtypeStruct((LEADS, width), f32),
            jax.ShapeDtypeStruct((6 * width,), f32),
            jax.ShapeDtypeStruct((width,), f32),
            jax.ShapeDtypeStruct((hidden,), f32),
            jax.ShapeDtypeStruct((width,), f32),
        ],
        scratch_shapes=[pltpu.VMEM((8, width), f32), pltpu.VMEM((16, width), f32)],
        compiler_params=kernel_params(20),
        name="first_sums",
    )(place, *own, *received, weight, output, blocks)


def second_sums_kernel(grp_size, line, place, *refs):
    own, received = refs[:grp_size], refs[grp_size : 2 * grp_size]
    attend, output = refs[2 * grp_size :]
    b = pl.program_id(0)
    half = output.shape[0] // 2
    for target, chosen in ((attend, b < grp_size - 1), (output, b == grp_size - 1)):

        @pl.when(chosen)
        def _():
            for side in range(2):
                write = lambda ref: copy_line(place, line, half // line, ref, target, side * half)
                picked(place, grp_size, own, received, side, b, write)


def second_sums(place, own):
    grp_size, width = len(own), own[0].shape[1]
    line = 1 if line_size() > 4 else line_size()
    received = [swap_cores(part) for part in own]
    return pl.pallas_call(
        partial(second_sums_kernel, grp_size, line),
        grid=(grp_size,),
        in_specs=[pl.BlockSpec(memory_space=pltpu.SMEM)] + [whole(*own[0].shape)] * (2 * grp_size),
        out_specs=[
            pl.BlockSpec((width, width), lambda b: (0, jnp.minimum(b, grp_size - 2))),
            whole(width, width),
        ],
        out_shape=[
            jax.ShapeDtypeStruct((width, 3 * width), f32),
            jax.ShapeDtypeStruct((width, width), f32),
        ],
        compiler_params=kernel_params(16),
        name="second_sums",
    )(place, *own, *received)


def long_forward(owner, rank, share, lengths, valid, own, rest, mod, weight):
    rows, width = own.shape
    owners = lengths.shape[0]
    count = rows // owners
    steps = jnp.arange(owners, dtype=jnp.int32)
    ranks = (rank + jnp.arange(share, dtype=jnp.int32)) % share
    blocks = (((owner - steps) % owners)[None, :] * share + ranks[:, None]).reshape(-1, 1)
    key_pos = blocks * count + jnp.arange(count, dtype=jnp.int32)[None, :]
    doc_ends = jnp.cumsum(lax.dynamic_index_in_dim(lengths, owner, 0, False))
    key_seg = sum((key_pos >= doc_ends[doc]).astype(jnp.int32) for doc in range(doc_ends.shape[0]))
    own_valid = lax.dynamic_index_in_dim(valid, owner, 0, False).reshape(-1, count)
    key_valid = own_valid[blocks[:, 0]] > 0
    open_seg = jnp.where(key_valid, key_seg, -1).reshape(1, -1)
    key_pos = key_pos.reshape(1, -1)
    query_seg = key_seg.reshape(-1, 1)[:rows]
    query_pos = key_pos.reshape(-1, 1)[:rows]
    head_width = width // HEADS
    normed = normalize(jnp.concatenate([own, rest], axis=0).astype(f32))[0]
    mixed = (normed * (1.0 + mod[SCALE_ONE]) + mod[SHIFT_ONE]).astype(bf16)
    heads = lambda v: v.reshape(v.shape[0], HEADS, head_width).transpose(1, 0, 2)
    queries = heads(back_product(mixed[:rows], weight[:width]).astype(bf16))
    key_value = back_product(mixed, weight[width:]).astype(bf16)
    keys = heads(key_value[:, :width])
    values = heads(key_value[:, width:])
    probs, attended = attention(
        queries, keys, values, query_seg, query_pos, open_seg, key_pos, 1.0 / math.sqrt(head_width)
    )
    flat = attended.transpose(1, 0, 2).reshape(rows, width).astype(bf16)
    return ((probs, queries, keys, values, attended, normed, mixed), flat)


def long_backward(
    place, saved, grad_attended, own, rest, mod, weight, packed_output, grad_residual, sums
):
    probs, queries, keys, values, attended, normed, mixed = saved
    rows, width = own.shape
    head_width = width // HEADS
    score_scale = 1.0 / math.sqrt(head_width)
    grad_heads = grad_attended.reshape(HEADS, head_width, rows).transpose(0, 2, 1)
    deltas = jnp.sum(grad_heads.astype(f32) * attended, axis=-1, keepdims=True)
    grad_probs = jnp.einsum("hqd,hkd->hqk", grad_heads, values, preferred_element_type=f32)
    grad_scores = (probs.astype(f32) * (grad_probs - deltas)).astype(bf16)
    grad_query = jnp.einsum("hqk,hkd->hqd", grad_scores, keys, preferred_element_type=f32)
    grad_key = jnp.einsum("hqk,hqd->hkd", grad_scores, queries, preferred_element_type=f32)
    grad_value = jnp.einsum("hqk,hqd->hkd", probs, grad_heads, preferred_element_type=f32)
    flat = lambda v: v.transpose(1, 0, 2).reshape(v.shape[1], width)
    grad_query = (flat(grad_query) * score_scale).astype(bf16)
    grad_key = (flat(grad_key) * score_scale).astype(bf16)
    grad_value = flat(grad_value).astype(bf16)
    part = product(grad_key, weight[width : 2 * width]) + product(grad_value, weight[2 * width :])
    part = jnp.concatenate([part[:rows] + product(grad_query, weight[:width]), part[rows:]], axis=0)
    share = mod[SHARE]
    packed = [row_product(mixed[:rows], grad_query), row_product(mixed, grad_key), row_product(mixed, grad_value)]
    packed = [(matrix * share).astype(bf16) for matrix in packed] + [packed_output]
    half = width // 2
    top = jnp.concatenate([matrix[:half] for matrix in packed])
    bottom = jnp.concatenate([matrix[half:] for matrix in packed])
    first_core = place[2] == 0
    keep = jnp.where(first_core, top, bottom)
    send = jnp.where(first_core, bottom, top)
    total_rows = jnp.stack([jnp.sum(part, axis=0), jnp.sum(part * normed, axis=0)]) * share
    sums = jnp.concatenate([total_rows, sums[2:]], axis=0)
    normed, inverse = normalize(own.astype(f32))
    own_part = grad_residual + normalize_back(part[:rows] * (1.0 + mod[SCALE_ONE]), normed, inverse)
    return (keep, send, part[rows:].astype(bf16), own_part.astype(bf16), sums)


def on_device(
    tokens,
    cotangent,
    lengths,
    valid_mask,
    lead_index,
    sample_counts,
    lead_table,
    modulation_weight,
    modulation_bias,
    attend_weight,
    output_weight,
    output_bias,
    expand_weight,
    expand_bias,
    shrink_weight,
    shrink_bias,
):
    owners = tokens.shape[1]
    block_rows = tokens.shape[2]
    width = tokens.shape[3]
    hidden_width = expand_bias.shape[0]
    seq_size = lax.axis_size("seq")
    share = seq_size // owners
    seq_length = block_rows * seq_size
    rows = owners * block_rows
    place = lax.axis_index("seq")
    owner = place // share
    rank = place % share

    where = jnp.stack([owner, rank, place % 2, lax.axis_index("grp"), place // 2]).astype(jnp.int32)

    token_pieces = rows_to_owner(tokens[0], owner, share)

    bias = [modulation_bias, output_bias, expand_bias, shrink_bias]
    bias = jnp.concatenate(bias).astype(f32)[None]
    mod, weight = prepare(
        where, lead_index, sample_counts, lead_table, modulation_weight, bias, attend_weight,
        owners * seq_length,
    )
    grad_pieces = rows_to_owner(after(cotangent[0], mod), owner, share)
    token_pieces = after_all(token_pieces, mod)
    own_tokens = jnp.concatenate(token_pieces, axis=0)
    rest_tokens = share_rows(own_tokens, rank, share)
    short = seq_length <= 2048
    if short:
        *saved, attended = forward_attention(
            where, lengths[0], valid_mask[0], own_tokens, rest_tokens, mod, weight
        )
    else:
        saved, attended = long_forward(
            owner, rank, share, lengths[0], valid_mask[0], own_tokens, rest_tokens, mod, weight
        )
    grad_out = jnp.concatenate(after_all(grad_pieces, attended), axis=0)
    ff_keep, ff_send, packed_output, grad_attended, grad_residual, sums, output = middle(
        owners, where, own_tokens, attended, grad_out, mod, bias, output_weight, expand_weight,
        shrink_weight,
    )
    output = rows_from_owner(output, share)
    ff_core = low_total([ff_keep, swap_cores(ff_send)])
    ff_parts = send_plane(plane_parts(ff_core))
    grad_attended = after(grad_attended, ff_core)
    backward = backward_attention if short else long_backward
    held = backward(
        where, saved, grad_attended, own_tokens, rest_tokens, mod, weight, packed_output,
        grad_residual, sums,
    )
    at_keep, at_send, rest_part, own_part, sums = after_all(held, *ff_parts[1:], output)
    ff_plane = low_total(ff_parts)
    line = line_size() <= 4
    if line:
        ff_parts = send_line(line_parts(ff_plane))
    at_core = low_total([at_keep, swap_cores(at_send)])
    if share == 2:
        received = swap_cores(rest_part)
    else:
        received = return_rows(rest_part, rank, share)
    at_slices = plane_parts(at_core)
    finished = finish_rows(owners, where, own_tokens, own_part, after(received, ff_plane), mod)
    finished = rows_from_owner(finished, share)
    at_parts = send_plane(at_slices)
    at_plane = low_total(at_parts)
    if line:
        ff_parts = list(after_all(ff_parts, *at_slices))
        ff_line = line_total(ff_parts, sums, received)
        ff_pieces = send_line([ff_line] * line_size())
        ff_plane = line_join(lead_index, mod, ff_pieces)
        at_line = low_total(after_all(send_line(line_parts(at_plane)), finished))
        at_pieces = send_line([at_line] * line_size())
    else:
        vector = with_lead(lax.psum(sums, "seq"), lead_index[0], mod)
        ff_pieces = [sum_line(ff_plane)]
        ff_plane = jnp.concatenate(ff_pieces + [vector])
        at_line = sum_line(at_plane)
        at_pieces = [at_line]
    ff_parts = gather_plane(ff_plane)
    at_parts = gather_plane(jnp.concatenate(at_pieces))
    ff_parts = list(after_all(ff_parts, *at_pieces))
    grad_shrink, grad_expand, grad_mod_weight, output, grad_tokens, grad_table, grad_mod_bias, *biases = (
        first_sums(where, ff_parts, modulation_weight, output, finished)
    )
    at_parts = list(after_all(at_parts, grad_shrink))
    grad_attend, grad_output = second_sums(where, at_parts)
    return (
        output[None],
        grad_tokens[None],
        grad_table,
        grad_mod_weight,
        grad_mod_bias,
        grad_attend,
        grad_output,
        biases[0],
        grad_expand,
        biases[1],
        grad_shrink,
        biases[2],
    )


def solution(mesh):
    rows = P("grp", None, "seq", None)
    placed = (rows, rows, P("grp", None, None), P("grp", None, None), P("grp")) + (P(),) * 11
    return jax.shard_map(
        on_device,
        mesh=mesh,
        in_specs=placed,
        out_specs=(rows, rows) + (P(),) * 10,
        check_vma=False,
    )
```

```python
from functools import partial
import math

import jax
import jax.numpy as jnp
from jax import lax
from jax.experimental import pallas as pl
from jax.experimental.pallas import tpu as pltpu
from jax.sharding import PartitionSpec as P

HEADS = 6
LEADS = 8

EPSILON = 1e-06
MASKED = -1e30

bf16 = jnp.bfloat16
f32 = jnp.float32


def normalize(values):
    centred = values - jnp.mean(values, axis=-1, keepdims=True)
    inverse = lax.rsqrt(jnp.mean(centred * centred, axis=-1, keepdims=True) + EPSILON)
    return (centred * inverse, inverse)


def normalize_back(grad, normed, inverse):
    return inverse * (
        grad
        - jnp.mean(grad, axis=-1, keepdims=True)
        - normed * jnp.mean(grad * normed, axis=-1, keepdims=True)
    )


def row_product(left, right):
    return lax.dot_general(left, right, (((0,), (0,)), ((), ())), preferred_element_type=f32)


def back_product(grad, weight):
    return lax.dot_general(grad, weight, (((1,), (1,)), ((), ())), preferred_element_type=f32)


def product(left, right):
    return jnp.dot(left, right, preferred_element_type=f32)


def total(parts):
    result = parts[0].astype(f32)
    for part in parts[1:]:
        result = result + part.astype(f32)
    return result


def away(index, size, step):
    return index ^ step if size & (size - 1) == 0 else (index + step) % size


def back(index, size, step):
    return index ^ step if size & (size - 1) == 0 else (index - step) % size


def owner_pairs(seq_size, owners, share, step):
    return [(d, away(d // share, owners, step) * share + d % share) for d in range(seq_size)]


def rows_to_owner(blocks, owner, share):
    owners = blocks.shape[0]
    seq_size = lax.axis_size("seq")
    pieces = []
    for step in range(owners):
        block = lax.dynamic_index_in_dim(blocks, away(owner, owners, step), 0, False)
        if step:
            block = lax.ppermute(block, "seq", owner_pairs(seq_size, owners, share, step))
        pieces.append(block)
    return pieces


def pieces_from_owner(pieces, share):
    owners, seq_size = len(pieces), lax.axis_size("seq")
    return [pieces[0]] + [
        lax.ppermute(pieces[step], "seq", owner_pairs(seq_size, owners, share, step))
        for step in range(1, owners)
    ]


def rows_from_owner(blocks, share):
    owners = blocks.shape[0]
    groups = [[owner * share + rank for owner in range(owners)] for rank in range(share)]
    return lax.all_to_all(blocks, "seq", 0, 0, axis_index_groups=groups)


def share_rows(rows, rank, share):
    seq_size = lax.axis_size("seq")
    if share == 2:
        return lax.ppermute(rows, "seq", [(d, d ^ 1) for d in range(seq_size)])
    groups = [list(range(first, first + share)) for first in range(0, seq_size, share)]
    gathered = lax.all_gather(rows, "seq", axis_index_groups=groups)
    gathered = jnp.roll(gathered, -rank, axis=0)[1:]
    return gathered.reshape((share - 1) * rows.shape[0], rows.shape[1])


def return_rows(rest, rank, share):
    seq_size = lax.axis_size("seq")
    if share == 2:
        return lax.ppermute(rest, "seq", [(d, d ^ 1) for d in range(seq_size)])
    groups = [list(range(first, first + share)) for first in range(0, seq_size, share)]
    parts = rest.reshape(share - 1, rest.shape[0] // (share - 1), rest.shape[1])
    parts = jnp.concatenate([jnp.zeros_like(parts[:1]), parts], axis=0)
    parts = jnp.roll(parts, rank, axis=0)
    return lax.psum_scatter(parts, "seq", scatter_dimension=0, axis_index_groups=groups)


def swap_cores(values):
    seq_size = lax.axis_size("seq")
    return lax.ppermute(values, "seq", [(d, d ^ 1) for d in range(seq_size)])


def line_size():
    return lax.axis_size("seq") // 2


def line_send(values, step):
    seq_size = lax.axis_size("seq")
    return lax.ppermute(values, "seq", owner_pairs(seq_size, seq_size // 2, 2, step))


def plane_send(values, step):
    grp_size = lax.axis_size("grp")
    return lax.ppermute(values, "grp", [(d, away(d, grp_size, step)) for d in range(grp_size)])


def rows_at(values, at, count):
    return lax.dynamic_slice_in_dim(values, at * count, count, 0)


def plane_steps():
    return range(1, lax.axis_size("grp"))


def plane_parts(values):
    grp_size = lax.axis_size("grp")
    group = lax.axis_index("grp")
    count = values.shape[0] // grp_size
    return [rows_at(values, away(group, grp_size, step), count) for step in range(grp_size)]


def send_plane(parts):
    return [parts[0]] + [plane_send(parts[step], step) for step in plane_steps()]


def gather_plane(values):
    return [values] + [plane_send(values, step) for step in plane_steps()]


def line_parts(values):
    length = line_size()
    place = lax.axis_index("seq") // 2
    count = values.shape[0] // length
    return [rows_at(values, away(place, length, step), count) for step in range(length)]


def send_line(parts):
    return [parts[0]] + [line_send(parts[step], step) for step in range(1, len(parts))]


def line_exchange(values):
    length = line_size()
    groups = [list(range(core, 2 * length, 2)) for core in range(2)]
    return lax.all_to_all(values, "seq", 0, 0, axis_index_groups=groups)


def sum_line(values):
    length = line_size()
    groups = [list(range(core, 2 * length, 2)) for core in range(2)]
    return lax.psum(values, "seq", axis_index_groups=groups)


def low_total(parts):
    return total(parts).astype(bf16)


def after(values, *others):
    return lax.optimization_barrier((values,) + others)[0]


def columns(values, width):
    return [values[:, at : at + width] for at in range(0, values.shape[1], width)]


def sum_share(values, share):
    seq_size = lax.axis_size("seq")
    groups = [list(range(first, first + share)) for first in range(0, seq_size, share)]
    return lax.psum(values, "seq", axis_index_groups=groups)


def after_all(values, *others):
    return lax.optimization_barrier(tuple(values) + others)[: len(values)]


def attention_kernel(
    score_scale, query, key, value, query_seg, query_pos, open_seg, key_pos, probs, attended, bias
):
    @pl.when(pl.program_id(1) == 0)
    def _():
        allow = (query_seg[...] == open_seg[...]) | (query_pos[...] == key_pos[...])
        bias[...] = jnp.where(allow, 0.0, MASKED)

    scaled = (query[0].astype(f32) * score_scale).astype(bf16)
    scores = back_product(scaled, key[0]) + bias[...]
    expo = jnp.exp(scores - jnp.max(scores, axis=1, keepdims=True))
    low = (expo * (1.0 / jnp.sum(expo, axis=1, keepdims=True))).astype(bf16)
    probs[0] = low
    attended[0] = product(low, value[0])


def attention(queries, keys, values, query_seg, query_pos, open_seg, key_pos, score_scale):
    head_count, rows, head_width = queries.shape
    key_count = keys.shape[1]
    step = max(32, min(rows, 2**18 // key_count))
    row_block = lambda i, h: (h, i, 0)
    key_block = lambda i, h: (h, 0, 0)
    size = head_count * rows * key_count
    return pl.pallas_call(
        partial(attention_kernel, score_scale),
        grid=(rows // step, head_count),
        in_specs=[
            pl.BlockSpec((1, step, head_width), row_block),
            pl.BlockSpec((1, key_count, head_width), key_block),
            pl.BlockSpec((1, key_count, head_width), key_block),
            pl.BlockSpec((step, 1), lambda i, h: (i, 0)),
            pl.BlockSpec((step, 1), lambda i, h: (i, 0)),
            pl.BlockSpec((1, key_count), lambda i, h: (0, 0)),
            pl.BlockSpec((1, key_count), lambda i, h: (0, 0)),
        ],
        out_specs=[
            pl.BlockSpec((1, step, key_count), row_block),
            pl.BlockSpec((1, step, head_width), row_block),
        ],
        out_shape=[
            jax.ShapeDtypeStruct((head_count, rows, key_count), bf16),
            jax.ShapeDtypeStruct((head_count, rows, head_width), f32),
        ],
        scratch_shapes=[pltpu.VMEM((step, key_count), f32)],
        compiler_params=pltpu.CompilerParams(vmem_limit_bytes=40 * 2**20),
        cost_estimate=pl.CostEstimate(
            flops=4 * size * head_width, bytes_accessed=2 * size, transcendentals=size
        ),
        name="attention",
    )(queries, keys, values, query_seg, query_pos, open_seg, key_pos)


GELU_RATE = math.sqrt(2.0 / math.pi)
GELU_CUBE = 0.044715
SHIFT_ONE, SCALE_ONE, GATE_ONE, SHIFT_TWO, SCALE_TWO, GATE_TWO, SHARE, EMBEDDING = range(8)


def inner(left, right):
    return row_product(left, right)


def column_sum(values):
    return jnp.sum(values, axis=0, keepdims=True)


def whole(*shape):
    return pl.BlockSpec(shape, lambda *_: (0,) * len(shape))


def kernel_params(mebibytes):
    return pltpu.CompilerParams(vmem_limit_bytes=mebibytes * 2**20)


def prepare_kernel(factor, place, lead, counts, table, weight, bias, attend_weight, mod, turned):
    width = table.shape[1]
    here = lax.broadcasted_iota(jnp.int32, table.shape, 0) == lead[0]
    embedding = column_sum(jnp.where(here, table[...].astype(f32), 0.0))
    lifted = (embedding / (1.0 + jnp.exp(-embedding))).astype(bf16)
    modulation = product(lifted, weight[...]) + bias[:, : weight.shape[1]]
    for part in range(6):
        mod[part : part + 1, :] = modulation[:, part * width : (part + 1) * width]
    every, mine = 0, 0
    for group in range(counts.shape[0]):
        every = every + counts[group]
        mine = mine + jnp.where(place[3] == group, counts[group], 0)
    row = jnp.zeros((1, width), jnp.int32)
    mod[SHARE : SHARE + 1, :] = (row + mine).astype(f32) / (row + every).astype(f32) * factor
    mod[EMBEDDING : EMBEDDING + 1, :] = embedding
    turned[...] = attend_weight[...].T


def prepare(place, lead, counts, table, weight, bias, attend_weight, positions):
    width = table.shape[1]
    operands = (table, weight, bias, attend_weight)
    shapes = [
        jax.ShapeDtypeStruct((8, width), f32),
        jax.ShapeDtypeStruct(attend_weight.shape[::-1], bf16),
    ]
    return pl.pallas_call(
        partial(prepare_kernel, counts.shape[0] / math.sqrt(positions)),
        grid=(1,),
        in_specs=[pl.BlockSpec(memory_space=pltpu.SMEM)] * 3 + [whole(*item.shape) for item in operands],
        out_specs=[whole(*item.shape) for item in shapes],
        out_shape=shapes,
        compiler_params=kernel_params(12),
        name="prepare",
    )(place, lead, counts, *operands)


def forward_kernel(
    head_width, score_scale, owners, place, lengths, own, rest, valid, mod, weight,
    expo, query, key_value, attended_wide, inverse_total, attended, bias,
):
    pair = pl.program_id(0)
    rows, width = own.shape
    key_count = rows + rest.shape[0]

    @pl.when(pair == 0)
    def _():
        shift, scale = mod[SHIFT_ONE : SHIFT_ONE + 1, :], 1.0 + mod[SCALE_ONE : SCALE_ONE + 1, :]
        first = (normalize(own[...].astype(f32))[0] * scale + shift).astype(bf16)
        query[...] = back_product(weight[:width, :], first).astype(bf16)
        key_value[:, :rows] = back_product(weight[width:, :], first).astype(bf16)
        for at in range(0, rest.shape[0], rows):
            part = normalize(rest[at : at + rows, :].astype(f32))[0]
            part = (part * scale + shift).astype(bf16)
            key_value[:, rows + at : 2 * rows + at] = back_product(weight[width:, :], part).astype(bf16)

        owner, rank = place[0], place[1]
        share = key_count // rows
        count = rows // owners
        ends = []
        for doc in range(lengths.shape[1]):
            ends.append(lengths[owner, doc] + (ends[-1] if doc else 0))

        def segment(positions):
            return sum((positions >= end).astype(jnp.int32) for end in ends)

        def block_at(r, step):
            return back(owner, owners, step) * share + lax.rem(rank + r, share)

        lane = lax.broadcasted_iota(jnp.int32, (1, count), 1)
        query_pos = jnp.concatenate(
            [block_at(0, step) * count + lane for step in range(owners)], axis=1
        )
        query_seg = segment(query_pos)
        down = lax.broadcasted_iota(jnp.int32, (count, 1), 0)
        mine = lax.broadcasted_iota(jnp.int32, (owners, count), 0) == owner
        for r in range(share):
            for step in range(owners):
                block = block_at(r, step)
                key_pos = block * count + down
                open_rows = valid[:, pl.ds(pl.multiple_of(block * count, count), count)]
                open_rows = jnp.where((open_rows > 0) & mine, 1.0, 0.0)
                open_row = jnp.broadcast_to(column_sum(open_rows), (count, count))
                open_key = open_row.T[:, :1] > 0.5
                open_seg = jnp.where(open_key, segment(key_pos), -1)
                allow = (query_seg == open_seg) | (query_pos == key_pos)
                at = (r * owners + step) * count
                bias[at : at + count, :] = jnp.where(allow, 0.0, MASKED)

    heads = [pl.multiple_of((2 * pair + i) * head_width, head_width) for i in range(2)]
    scores = []
    for first in heads:
        here = pl.ds(first, head_width)
        scaled = (query[here, :].astype(f32) * score_scale).astype(bf16)
        scores.append(inner(key_value[here, :], scaled) + bias[...])
    for i, first in enumerate(heads):
        wide = jnp.exp(scores[i] - jnp.max(scores[i], axis=0, keepdims=True))
        inverse = 1.0 / column_sum(wide)
        low = wide.astype(bf16)
        expo[i] = low
        inverse_total[i] = inverse
        values = key_value[pl.ds(pl.multiple_of(width + first, head_width), head_width), :]
        attended_wide[pl.ds(first, head_width), :] = product(values, low) * inverse

    @pl.when(pair == pl.num_programs(0) - 1)
    def _():
        attended[...] = attended_wide[...].T.astype(bf16)


def forward_attention(place, lengths, valid, own, rest, mod, weight):
    rows, width = own.shape
    key_count = rows + rest.shape[0]
    head_width = width // HEADS
    size = HEADS * rows * key_count
    scalars = pl.BlockSpec(memory_space=pltpu.SMEM)
    return pl.pallas_call(
        partial(forward_kernel, head_width, 1.0 / math.sqrt(head_width), lengths.shape[0]),
        grid=(HEADS // 2,),
        in_specs=[scalars, scalars] + [whole(*item.shape) for item in (own, rest, valid, mod, weight)],
        out_specs=[
            pl.BlockSpec((2, key_count, rows), lambda p: (p, 0, 0)),
            whole(width, rows),
            whole(2 * width, key_count),
            whole(width, rows),
            pl.BlockSpec((2, 1, rows), lambda p: (p, 0, 0)),
            whole(rows, width),
        ],
        out_shape=[
            pltpu.HBM((HEADS, key_count, rows), bf16),
            jax.ShapeDtypeStruct((width, rows), bf16),
            jax.ShapeDtypeStruct((2 * width, key_count), bf16),
            jax.ShapeDtypeStruct((width, rows), f32),
            jax.ShapeDtypeStruct((HEADS, 1, rows), f32),
            jax.ShapeDtypeStruct((rows, width), bf16),
        ],
        scratch_shapes=[pltpu.VMEM((key_count, rows), f32)],
        compiler_params=kernel_params(20),
        cost_estimate=pl.CostEstimate(
            flops=16 * size * head_width, bytes_accessed=2 * size, transcendentals=size
        ),
        name="forward_attention",
    )(place, lengths, own, rest, valid, mod, weight)


def middle_kernel(
    place, own, attended, cotangent, mod, bias, output_weight, expand_weight, shrink_weight,
    keep, send, packed_output, grad_attended, grad_residual, sums, output,
):
    first_core = place[2] == 0
    rows, width = own.shape
    blocks = expand_weight.shape[1] // width
    row = lambda at: mod[at : at + 1, :]
    bias_row = lambda at: bias[:, at * width : (at + 1) * width]
    share = row(SHARE)
    scale_two = 1.0 + row(SCALE_TWO)
    branch_one = product(attended[...], output_weight[...]) + bias_row(6)
    residual = own[...].astype(f32) + row(GATE_ONE) * branch_one
    normed, inverse = normalize(residual)
    mixed = (normed * scale_two + row(SHIFT_TWO)).astype(bf16)
    wide = cotangent[...].astype(f32)
    grad_two = (wide * row(GATE_TWO)).astype(bf16)
    sums[...] = jnp.zeros_like(sums)
    branch_two = jnp.zeros((rows, width), f32) + bias_row(7 + blocks)
    grad_mixed = jnp.zeros((rows, width), f32)
    for block in range(blocks):
        part = slice(block * width, (block + 1) * width)
        hidden = product(mixed, expand_weight[:, part]) + bias_row(7 + block)
        square = hidden * hidden
        bent = jnp.tanh(GELU_RATE * hidden * (1.0 + GELU_CUBE * square))
        half = 0.5 + 0.5 * bent
        slope = half + 0.5 * hidden * (1.0 - bent * bent) * (
            GELU_RATE + (3.0 * GELU_CUBE * GELU_RATE) * square
        )
        active = (hidden * half).astype(bf16)
        branch_two = branch_two + product(active, shrink_weight[part, :])
        grad_hidden = (back_product(grad_two, shrink_weight[part, :]) * slope).astype(bf16)
        grad_shrink = inner(active, grad_two) * share
        grad_expand = inner(mixed, grad_hidden) * share
        keep[part, :] = jnp.where(first_core, grad_shrink, grad_expand).astype(bf16)
        send[part, :] = jnp.where(first_core, grad_expand, grad_shrink).astype(bf16)
        sums[7 + block : 8 + block, :] = column_sum(grad_hidden.astype(f32)) * share
        grad_mixed = grad_mixed + back_product(grad_hidden, expand_weight[:, part])
    result = (residual + row(GATE_TWO) * branch_two).astype(bf16)
    owners, count = output.shape[:2]
    for step in range(owners):
        output[back(place[0], owners, step)] = result[step * count : (step + 1) * count, :]
    sums[5:6, :] = column_sum(wide * branch_two) * share
    sums[7 + blocks : 8 + blocks, :] = column_sum(grad_two.astype(f32)) * share
    sums[4:5, :] = column_sum(grad_mixed * normed) * share
    sums[3:4, :] = column_sum(grad_mixed) * share
    grad_wide = wide + normalize_back(grad_mixed * scale_two, normed, inverse)
    grad_residual[...] = grad_wide
    sums[2:3, :] = column_sum(grad_wide * branch_one) * share
    grad_one = (grad_wide * row(GATE_ONE)).astype(bf16)
    sums[6:7, :] = column_sum(grad_one.astype(f32)) * share
    packed_output[...] = (inner(attended[...], grad_one) * share).astype(bf16)
    grad_attended[...] = back_product(output_weight[...], grad_one).astype(bf16)


def middle(
    owners, place, own, attended, cotangent, mod, bias, output_weight, expand_weight, shrink_weight
):
    rows, width = own.shape
    hidden = expand_weight.shape[1]
    operands = (
        own, attended, cotangent, mod, bias, output_weight, expand_weight, shrink_weight
    )
    shapes = [
        jax.ShapeDtypeStruct((hidden, width), bf16),
        jax.ShapeDtypeStruct((hidden, width), bf16),
        pltpu.HBM((width, width), bf16),
        pltpu.HBM((width, rows), bf16),
        pltpu.HBM((rows, width), f32),
        jax.ShapeDtypeStruct((16, width), f32),
        jax.ShapeDtypeStruct((owners, rows // owners, width), bf16),
    ]
    return pl.pallas_call(
        middle_kernel,
        grid=(1,),
        in_specs=[pl.BlockSpec(memory_space=pltpu.SMEM)] + [whole(*item.shape) for item in operands],
        out_specs=[whole(*item.shape) for item in shapes],
        out_shape=shapes,
        compiler_params=kernel_params(16),
        cost_estimate=pl.CostEstimate(
            flops=16 * rows * width * hidden, bytes_accessed=2**24, transcendentals=rows * hidden
        ),
        name="middle",
    )(place, *operands)


def backward_kernel(
    head_width, score_scale, place, expo, query, key_value, attended_wide, inverse_total,
    grad_attended, own, rest, mod, weight, packed_output, grad_residual, sums_in, keep, send,
    rest_part, own_part, sums,
    grad_query, grad_key, grad_value,
):
    pair = pl.program_id(0)
    rows, width = own.shape
    grad_keys, grad_values = [], []
    for i in range(2):
        first = pl.multiple_of((2 * pair + i) * head_width, head_width)
        here = pl.ds(first, head_width)
        scaled = (query[here, :].astype(f32) * score_scale).astype(bf16)
        keys = key_value[here, :]
        values = key_value[pl.ds(pl.multiple_of(width + first, head_width), head_width), :]
        grads = (grad_attended[here, :].astype(f32) * inverse_total[i]).astype(bf16)
        delta = column_sum(grads.astype(f32) * attended_wide[here, :])
        low = expo[i]
        grad_scores = (low.astype(f32) * (inner(values, grads) - delta)).astype(bf16)
        grad_values.append(back_product(low, grads))
        grad_keys.append(back_product(grad_scores, scaled))
        grad_query[here, :] = (product(keys, grad_scores) * score_scale).astype(bf16)
    grad_key[pair] = jnp.concatenate(grad_keys, axis=1).astype(bf16)
    grad_value[pair] = jnp.concatenate(grad_values, axis=1).astype(bf16)

    @pl.when(pair == pl.num_programs(0) - 1)
    def _():
        row = lambda at: mod[at : at + 1, :]
        share = row(SHARE)
        shift, scale = row(SHIFT_ONE), 1.0 + row(SCALE_ONE)
        pairs = range(HEADS // 2)
        packed_key = jnp.zeros((width, width), f32)
        packed_value = jnp.zeros((width, width), f32)
        total_shift = jnp.zeros((1, width), f32)
        total_scale = jnp.zeros((1, width), f32)
        for at in range(0, rows + rest.shape[0], rows):
            here = slice(at, at + rows)
            source = own[...] if at == 0 else rest[at - rows : at, :]
            normed, inverse = normalize(source.astype(f32))
            mixed = (normed * scale + shift).astype(bf16)
            keys = jnp.concatenate([grad_key[pair, here, :] for pair in pairs], axis=1)
            values = jnp.concatenate([grad_value[pair, here, :] for pair in pairs], axis=1)
            part = product(keys, weight[width : 2 * width, :]) + product(
                values, weight[2 * width :, :]
            )
            if at == 0:
                part = part + inner(grad_query[...], weight[:width, :])
                back = normalize_back(part * scale, normed, inverse)
                own_part[...] = (grad_residual[...] + back).astype(bf16)
                packed_query = product(grad_query[...], mixed).T
            else:
                rest_part[at - rows : at, :] = part.astype(bf16)
            packed_key = packed_key + inner(mixed, keys)
            packed_value = packed_value + inner(mixed, values)
            total_shift = total_shift + column_sum(part)
            total_scale = total_scale + column_sum(part * normed)
        first_core = place[2] == 0
        packed = [packed_query * share, packed_key * share, packed_value * share, packed_output[...].astype(f32)]
        half = width // 2
        for at, matrix in enumerate(packed):
            here = slice(at * half, (at + 1) * half)
            keep[here, :] = jnp.where(first_core, matrix[:half], matrix[half:]).astype(bf16)
            send[here, :] = jnp.where(first_core, matrix[half:], matrix[:half]).astype(bf16)
        sums[...] = sums_in[...]
        sums[0:1, :] = total_shift * share
        sums[1:2, :] = total_scale * share
        rest_part[rest.shape[0] :, :] = sums[...].astype(bf16)


def backward_attention(
    place, saved, grad_attended, own, rest, mod, weight, packed_output, grad_residual, sums
):
    expo, query, key_value, attended_wide, inverse_total = saved
    rows, width = own.shape
    key_count = rows + rest.shape[0]
    head_width = width // HEADS
    size = HEADS * rows * key_count
    operands = (
        query, key_value, attended_wide, inverse_total, grad_attended, own, rest, mod, weight,
        packed_output, grad_residual, sums,
    )
    specs = [whole(*item.shape) for item in operands]
    specs[3] = pl.BlockSpec((2, 1, rows), lambda p: (p, 0, 0))
    shapes = [
        jax.ShapeDtypeStruct((2 * width, width), bf16),
        jax.ShapeDtypeStruct((2 * width, width), bf16),
        jax.ShapeDtypeStruct((rest.shape[0] + sums.shape[0], width), bf16),
        jax.ShapeDtypeStruct((rows, width), bf16),
        jax.ShapeDtypeStruct(sums.shape, f32),
    ]
    return pl.pallas_call(
        partial(backward_kernel, head_width, 1.0 / math.sqrt(head_width)),
        grid=(HEADS // 2,),
        in_specs=[
            pl.BlockSpec(memory_space=pltpu.SMEM),
            pl.BlockSpec((2, key_count, rows), lambda p: (p, 0, 0)),
        ]
        + specs,
        out_specs=[whole(*item.shape) for item in shapes],
        out_shape=shapes,
        scratch_shapes=[
            pltpu.VMEM((width, rows), bf16),
            pltpu.VMEM((HEADS // 2, key_count, 2 * head_width), bf16),
            pltpu.VMEM((HEADS // 2, key_count, 2 * head_width), bf16),
        ],
        compiler_params=kernel_params(16),
        cost_estimate=pl.CostEstimate(
            flops=32 * size * head_width, bytes_accessed=2 * size, transcendentals=0
        ),
        name="backward_attention",
    )(place, pltpu.with_memory_space_constraint(expo, pltpu.HBM), *operands)


def finish_kernel(owners, own, part, received, mod, *refs):
    parts, results = refs[:-owners], refs[-owners:]
    rows, width = own.shape
    count = rows // owners
    normed, inverse = normalize(own[...].astype(f32))
    grad = received[:rows, :].astype(f32) * (1.0 + mod[SCALE_ONE : SCALE_ONE + 1, :])
    grad = (part[...].astype(f32) + normalize_back(grad, normed, inverse)).astype(bf16)
    for step, result in enumerate(results):
        result[:count, :] = grad[step * count : (step + 1) * count, :]
    if parts:
        summed = total([ref[...] for ref in parts]).astype(bf16)
        for result in results:
            result[count:, :] = summed


def finish_rows(owners, own, part, received, mod, parts):
    operands = [own, part, received, mod] + parts
    shape = (own.shape[0] // owners + (parts[0].shape[0] if parts else 0), own.shape[1])
    return pl.pallas_call(
        partial(finish_kernel, owners),
        grid=(1,),
        in_specs=[whole(*item.shape) for item in operands],
        out_specs=[whole(*shape)] * owners,
        out_shape=[jax.ShapeDtypeStruct(shape, bf16)] * owners,
        compiler_params=kernel_params(12),
        name="finish_rows",
    )(*operands)


def line_total_kernel(sums, received, *refs):
    parts, result = refs[:-1], refs[-1]
    count = parts[0].shape[-2]
    if len(parts[0].shape) == 3:
        parts = [parts[0].at[at] for at in range(parts[0].shape[0])]
    result[:count, :] = total([part[...] for part in parts]).astype(bf16)
    below = received[received.shape[0] - sums.shape[0] :, :].astype(f32)
    result[count:, :] = (sums[...] + below).astype(bf16)


def line_total(parts, sums, received):
    count, width = parts[0].shape[-2:]
    below = sums.shape[0]
    return pl.pallas_call(
        line_total_kernel,
        grid=(1,),
        in_specs=[whole(*item.shape) for item in [sums, received] + parts],
        out_specs=whole(count + below, width),
        out_shape=jax.ShapeDtypeStruct((count + below, width), bf16),
        compiler_params=kernel_params(8),
        name="line_total",
    )(sums, received, *parts)


def with_lead(below, lead, mod):
    row = lax.broadcasted_iota(jnp.int32, below.shape, 0)
    below = jnp.where(row == 12, mod[EMBEDDING : EMBEDDING + 1, :], below)
    return jnp.where(row == 13, jnp.full(below.shape, lead).astype(f32), below).astype(bf16)


def line_join_kernel(lead, mod, *refs):
    parts, result = refs[:-1], refs[-1]
    count = (result.shape[0] - 16) // len(parts)
    for at, part in enumerate(parts):
        result[at * count : (at + 1) * count, :] = part[:count, :]
    below = total([part[count:, :] for part in parts])
    result[len(parts) * count :, :] = with_lead(below, lead[0], mod)


def line_join(lead, mod, parts):
    rows, width = parts[0].shape
    shape = (len(parts) * (rows - 16) + 16, width)
    return pl.pallas_call(
        line_join_kernel,
        grid=(1,),
        in_specs=[pl.BlockSpec(memory_space=pltpu.SMEM)]
        + [whole(*item.shape) for item in [mod] + parts],
        out_specs=whole(*shape),
        out_shape=jax.ShapeDtypeStruct(shape, bf16),
        compiler_params=kernel_params(8),
        name="line_join",
    )(lead, mod, *parts)


def picked(place, grp_size, own, received, side, b, write):
    group = place[3]
    for step in range(grp_size):
        here = back(group, grp_size, b) == step
        for ref, mine in ((own[step], True), (received[step], False)):

            @pl.when(here & ((place[2] == side) == mine))
            def _():
                write(ref)


def copy_line(place, line, count, ref, output, first):
    for c in range(line):
        from_c = back(place[4], line, c) if line > 1 else 0
        here = pl.ds(pl.multiple_of(from_c * count, count), count) if line > 1 else slice(0, count)
        output[first + c * count : first + (c + 1) * count, :] = ref[here, :].astype(f32)


def first_sums_kernel(grp_size, line, place, *refs):
    own, received = refs[:grp_size], refs[grp_size : 2 * grp_size]
    refs = refs[2 * grp_size :]
    weight, output = refs[:2]
    owners = len(refs) - 14
    pieces, refs = refs[2 : 2 + owners], refs[2 + owners :]
    shrink, expand, grad_weight, copied, rows, table, grad_bias = refs[:7]
    output_bias, expand_bias, shrink_bias, grad_lifted, sums = refs[7:]
    b = pl.program_id(0)
    width = table.shape[1]
    count = own[0].shape[0] - 16
    copied[...] = output[...]
    for step, piece in enumerate(pieces):

        @pl.when(back(place[0], owners, step) == b)
        def _():
            rows[0] = piece[: rows.shape[1], :].astype(f32)

    for side, target in enumerate((shrink, expand)):
        write = lambda ref: copy_line(place, line, count // line, ref, target, 0)
        picked(place, grp_size, own, received, side, b, write)

    parts = [part[count:, :].astype(f32) for part in own]
    pad = jnp.zeros((8 - grp_size, width), f32)
    stacked = jnp.concatenate([part[12:13] for part in parts] + [pad])
    gate = 1.0 / (1.0 + jnp.exp(-stacked))

    @pl.when(b == 0)
    def _():
        sums[...] = total(parts)
        grad_lifted[...] = jnp.zeros_like(grad_lifted)

    @pl.when(b < 3)
    def _():
        lifted = (stacked * gate).astype(bf16)
        line_of = lax.broadcasted_iota(jnp.int32, parts[0].shape, 0)
        for i in range(2):
            here = slice(i * width, (i + 1) * width)
            picks = [column_sum(jnp.where(line_of == 2 * b + i, part, 0.0)) for part in parts]
            picks = jnp.concatenate(picks + [pad]).astype(bf16)
            grad_weight[:, here] = inner(lifted, picks)
            grad_lifted[...] += back_product(picks, weight[:, here])

    @pl.when(b == pl.num_programs(0) - 1)
    def _():
        for at in range(6):
            grad_bias[at * width : (at + 1) * width] = sums[at]
        output_bias[...] = sums[6]
        for at in range(expand_bias.shape[0] // width):
            expand_bias[at * width : (at + 1) * width] = sums[7 + at]
        shrink_bias[...] = sums[7 + expand_bias.shape[0] // width]
        grad_embedding = grad_lifted[...] * gate * (1.0 + stacked * (1.0 - gate))
        lead = lax.broadcasted_iota(jnp.int32, (LEADS, width), 0).astype(f32)
        table[...] = total(
            [
                jnp.where(lead == part[13:14], grad_embedding[p : p + 1], 0.0)
                for p, part in enumerate(parts)
            ]
        )


def first_sums(place, own, weight, output, pieces):
    grp_size = len(own)
    line = 1 if line_size() > 4 else line_size()
    received = [swap_cores(part) for part in own]
    width = weight.shape[0]
    hidden = grp_size * width
    block = pl.BlockSpec((1,) + output.shape[1:], lambda b: (b, 0, 0))
    wide = pl.BlockSpec((width, 2 * width), lambda b: (0, jnp.minimum(b, 2)))
    return pl.pallas_call(
        partial(first_sums_kernel, grp_size, line),
        grid=(grp_size,),
        in_specs=[pl.BlockSpec(memory_space=pltpu.SMEM)]
        + [whole(*own[0].shape)] * (2 * grp_size)
        + [wide, block]
        + [whole(*item.shape) for item in pieces],
        out_specs=[
            pl.BlockSpec((width, width), lambda b: (b, 0)),
            pl.BlockSpec((width, width), lambda b: (0, b)),
            wide,
            block,
            block,
            whole(LEADS, width),
            whole(6 * width),
            whole(width),
            whole(hidden),
            whole(width),
        ],
        out_shape=[
            jax.ShapeDtypeStruct((hidden, width), f32),
            jax.ShapeDtypeStruct((width, hidden), f32),
            jax.ShapeDtypeStruct(weight.shape, f32),
            jax.ShapeDtypeStruct(output.shape, output.dtype),
            jax.ShapeDtypeStruct(output.shape, f32),
            jax.ShapeDtypeStruct((LEADS, width), f32),
            jax.ShapeDtypeStruct((6 * width,), f32),
            jax.ShapeDtypeStruct((width,), f32),
            jax.ShapeDtypeStruct((hidden,), f32),
            jax.ShapeDtypeStruct((width,), f32),
        ],
        scratch_shapes=[pltpu.VMEM((8, width), f32), pltpu.VMEM((16, width), f32)],
        compiler_params=kernel_params(20),
        name="first_sums",
    )(place, *own, *received, weight, output, *pieces)


def second_sums_kernel(grp_size, line, place, *refs):
    own, received = refs[:grp_size], refs[grp_size : 2 * grp_size]
    attend, output = refs[2 * grp_size :]
    b = pl.program_id(0)
    half = output.shape[0] // 2
    for target, chosen in ((attend, b < grp_size - 1), (output, b == grp_size - 1)):

        @pl.when(chosen)
        def _():
            for side in range(2):
                write = lambda ref: copy_line(place, line, half // line, ref, target, side * half)
                picked(place, grp_size, own, received, side, b, write)


def second_sums(place, own):
    grp_size, width = len(own), own[0].shape[1]
    line = 1 if line_size() > 4 else line_size()
    received = [swap_cores(part) for part in own]
    return pl.pallas_call(
        partial(second_sums_kernel, grp_size, line),
        grid=(grp_size,),
        in_specs=[pl.BlockSpec(memory_space=pltpu.SMEM)] + [whole(*own[0].shape)] * (2 * grp_size),
        out_specs=[
            pl.BlockSpec((width, width), lambda b: (0, jnp.minimum(b, grp_size - 2))),
            whole(width, width),
        ],
        out_shape=[
            jax.ShapeDtypeStruct((width, 3 * width), f32),
            jax.ShapeDtypeStruct((width, width), f32),
        ],
        compiler_params=kernel_params(16),
        name="second_sums",
    )(place, *own, *received)


def long_forward(owner, rank, share, lengths, valid, own, rest, mod, weight):
    rows, width = own.shape
    owners = lengths.shape[0]
    count = rows // owners
    steps = jnp.arange(owners, dtype=jnp.int32)
    ranks = (rank + jnp.arange(share, dtype=jnp.int32)) % share
    blocks = (back(owner, owners, steps)[None, :] * share + ranks[:, None]).reshape(-1, 1)
    key_pos = blocks * count + jnp.arange(count, dtype=jnp.int32)[None, :]
    doc_ends = jnp.cumsum(lax.dynamic_index_in_dim(lengths, owner, 0, False))
    key_seg = sum((key_pos >= doc_ends[doc]).astype(jnp.int32) for doc in range(doc_ends.shape[0]))
    own_valid = lax.dynamic_index_in_dim(valid, owner, 0, False).reshape(-1, count)
    key_valid = own_valid[blocks[:, 0]] > 0
    open_seg = jnp.where(key_valid, key_seg, -1).reshape(1, -1)
    key_pos = key_pos.reshape(1, -1)
    query_seg = key_seg.reshape(-1, 1)[:rows]
    query_pos = key_pos.reshape(-1, 1)[:rows]
    head_width = width // HEADS
    normed = normalize(jnp.concatenate([own, rest], axis=0).astype(f32))[0]
    mixed = (normed * (1.0 + mod[SCALE_ONE]) + mod[SHIFT_ONE]).astype(bf16)
    heads = lambda v: v.reshape(v.shape[0], HEADS, head_width).transpose(1, 0, 2)
    queries = heads(back_product(mixed[:rows], weight[:width]).astype(bf16))
    key_value = back_product(mixed, weight[width:]).astype(bf16)
    keys = heads(key_value[:, :width])
    values = heads(key_value[:, width:])
    probs, attended = attention(
        queries, keys, values, query_seg, query_pos, open_seg, key_pos, 1.0 / math.sqrt(head_width)
    )
    flat = attended.transpose(1, 0, 2).reshape(rows, width).astype(bf16)
    return ((probs, queries, keys, values, attended, normed, mixed), flat)


def long_backward(
    place, saved, grad_attended, own, rest, mod, weight, packed_output, grad_residual, sums
):
    probs, queries, keys, values, attended, normed, mixed = saved
    rows, width = own.shape
    head_width = width // HEADS
    score_scale = 1.0 / math.sqrt(head_width)
    grad_heads = grad_attended.reshape(HEADS, head_width, rows).transpose(0, 2, 1)
    deltas = jnp.sum(grad_heads.astype(f32) * attended, axis=-1, keepdims=True)
    grad_probs = jnp.einsum("hqd,hkd->hqk", grad_heads, values, preferred_element_type=f32)
    grad_scores = (probs.astype(f32) * (grad_probs - deltas)).astype(bf16)
    grad_query = jnp.einsum("hqk,hkd->hqd", grad_scores, keys, preferred_element_type=f32)
    grad_key = jnp.einsum("hqk,hqd->hkd", grad_scores, queries, preferred_element_type=f32)
    grad_value = jnp.einsum("hqk,hqd->hkd", probs, grad_heads, preferred_element_type=f32)
    flat = lambda v: v.transpose(1, 0, 2).reshape(v.shape[1], width)
    grad_query = (flat(grad_query) * score_scale).astype(bf16)
    grad_key = (flat(grad_key) * score_scale).astype(bf16)
    grad_value = flat(grad_value).astype(bf16)
    part = product(grad_key, weight[width : 2 * width]) + product(grad_value, weight[2 * width :])
    part = jnp.concatenate([part[:rows] + product(grad_query, weight[:width]), part[rows:]], axis=0)
    share = mod[SHARE]
    packed = [row_product(mixed[:rows], grad_query), row_product(mixed, grad_key), row_product(mixed, grad_value)]
    packed = [(matrix * share).astype(bf16) for matrix in packed] + [packed_output]
    half = width // 2
    top = jnp.concatenate([matrix[:half] for matrix in packed])
    bottom = jnp.concatenate([matrix[half:] for matrix in packed])
    first_core = place[2] == 0
    keep = jnp.where(first_core, top, bottom)
    send = jnp.where(first_core, bottom, top)
    total_rows = jnp.stack([jnp.sum(part, axis=0), jnp.sum(part * normed, axis=0)]) * share
    sums = jnp.concatenate([total_rows, sums[2:]], axis=0)
    normed, inverse = normalize(own.astype(f32))
    own_part = grad_residual + normalize_back(part[:rows] * (1.0 + mod[SCALE_ONE]), normed, inverse)
    return (keep, send, part[rows:].astype(bf16), own_part.astype(bf16), sums)


def on_device(
    tokens,
    cotangent,
    lengths,
    valid_mask,
    lead_index,
    sample_counts,
    lead_table,
    modulation_weight,
    modulation_bias,
    attend_weight,
    output_weight,
    output_bias,
    expand_weight,
    expand_bias,
    shrink_weight,
    shrink_bias,
):
    owners = tokens.shape[1]
    block_rows = tokens.shape[2]
    width = tokens.shape[3]
    hidden_width = expand_bias.shape[0]
    seq_size = lax.axis_size("seq")
    share = seq_size // owners
    seq_length = block_rows * seq_size
    rows = owners * block_rows
    place = lax.axis_index("seq")
    owner = place // share
    rank = place % share

    where = jnp.stack([owner, rank, place % 2, lax.axis_index("grp"), place // 2]).astype(jnp.int32)

    token_pieces = rows_to_owner(tokens[0], owner, share)

    bias = [modulation_bias, output_bias, expand_bias, shrink_bias]
    bias = jnp.concatenate(bias).astype(f32)[None]
    mod, weight = prepare(
        where, lead_index, sample_counts, lead_table, modulation_weight, bias, attend_weight,
        owners * seq_length,
    )
    grad_pieces = rows_to_owner(after(cotangent[0], mod), owner, share)
    token_pieces = after_all(token_pieces, mod)
    own_tokens = jnp.concatenate(token_pieces, axis=0)
    rest_tokens = share_rows(own_tokens, rank, share)
    short = seq_length <= 2048
    if short:
        *saved, attended = forward_attention(
            where, lengths[0], valid_mask[0], own_tokens, rest_tokens, mod, weight
        )
    else:
        saved, attended = long_forward(
            owner, rank, share, lengths[0], valid_mask[0], own_tokens, rest_tokens, mod, weight
        )
    grad_out = jnp.concatenate(after_all(grad_pieces, attended), axis=0)
    ff_keep, ff_send, packed_output, grad_attended, grad_residual, sums, output = middle(
        owners, where, own_tokens, attended, grad_out, mod, bias, output_weight, expand_weight,
        shrink_weight,
    )
    output = rows_from_owner(output, share)
    ff_core = low_total([ff_keep, swap_cores(ff_send)])
    ff_parts = send_plane(plane_parts(ff_core))
    grad_attended = after(grad_attended, ff_core)
    backward = backward_attention if short else long_backward
    held = backward(
        where, saved, grad_attended, own_tokens, rest_tokens, mod, weight, packed_output,
        grad_residual, sums,
    )
    at_keep, at_send, rest_part, own_part, sums = after_all(held, *ff_parts[1:], output)
    ff_plane = low_total(ff_parts)
    line = line_size() <= 4
    if line:
        ff_parts = [line_exchange(ff_plane.reshape(line_size(), -1, width))]
    at_core = low_total([at_keep, swap_cores(at_send)])
    if share == 2:
        received = swap_cores(rest_part)
    else:
        received = return_rows(rest_part, rank, share)
    at_slices = plane_parts(at_core)
    at_parts = send_plane(at_slices)
    if line:
        ff_parts = list(after_all(ff_parts, *at_slices))
        ff_line = line_total(ff_parts, sums, received)
        at_parts = after_all(at_parts, ff_line)
    at_plane = low_total(at_parts)
    if line:
        ff_pieces = send_line([ff_line] * line_size())
        ff_plane = line_join(lead_index, mod, ff_pieces)
        at_line = send_line(line_parts(at_plane))
    else:
        vector = with_lead(lax.psum(sums, "seq"), lead_index[0], mod)
        ff_pieces = [sum_line(ff_plane)]
        ff_plane = jnp.concatenate(ff_pieces + [vector])
        at_line = []
    pieces = finish_rows(owners, own_tokens, own_part, received, mod, at_line)
    pieces = pieces_from_owner(pieces, share)
    at_pieces = [piece[block_rows:] for piece in pieces] if line else [sum_line(at_plane)]
    ff_parts = gather_plane(ff_plane)
    at_parts = gather_plane(jnp.concatenate(at_pieces))
    ff_parts = list(after_all(ff_parts, *pieces))
    grad_shrink, grad_expand, grad_mod_weight, output, grad_tokens, grad_table, grad_mod_bias, *biases = (
        first_sums(where, ff_parts, modulation_weight, output, pieces)
    )
    at_parts = list(after_all(at_parts, grad_shrink))
    grad_attend, grad_output = second_sums(where, at_parts)
    return (
        output[None],
        grad_tokens[None],
        grad_table,
        grad_mod_weight,
        grad_mod_bias,
        grad_attend,
        grad_output,
        biases[0],
        grad_expand,
        biases[1],
        grad_shrink,
        biases[2],
    )


def solution(mesh):
    rows = P("grp", None, "seq", None)
    placed = (rows, rows, P("grp", None, None), P("grp", None, None), P("grp")) + (P(),) * 11
    return jax.shard_map(
        on_device,
        mesh=mesh,
        in_specs=placed,
        out_specs=(rows, rows) + (P(),) * 10,
        check_vma=False,
    )
```

```python
from functools import partial
import math

import jax
import jax.numpy as jnp
from jax import lax
from jax.experimental import pallas as pl
from jax.experimental.pallas import tpu as pltpu
from jax.sharding import PartitionSpec as P

HEADS = 6
LEADS = 8

EPSILON = 1e-06
MASKED = -1e30

bf16 = jnp.bfloat16
f32 = jnp.float32


def normalize(values):
    centred = values - jnp.mean(values, axis=-1, keepdims=True)
    inverse = lax.rsqrt(jnp.mean(centred * centred, axis=-1, keepdims=True) + EPSILON)
    return (centred * inverse, inverse)


def normalize_back(grad, normed, inverse):
    return inverse * (
        grad
        - jnp.mean(grad, axis=-1, keepdims=True)
        - normed * jnp.mean(grad * normed, axis=-1, keepdims=True)
    )


def row_product(left, right):
    return lax.dot_general(left, right, (((0,), (0,)), ((), ())), preferred_element_type=f32)


def back_product(grad, weight):
    return lax.dot_general(grad, weight, (((1,), (1,)), ((), ())), preferred_element_type=f32)


def product(left, right):
    return jnp.dot(left, right, preferred_element_type=f32)


def total(parts):
    result = parts[0].astype(f32)
    for part in parts[1:]:
        result = result + part.astype(f32)
    return result


def away(index, size, step):
    return index ^ step if size & (size - 1) == 0 else (index + step) % size


def back(index, size, step):
    return index ^ step if size & (size - 1) == 0 else (index - step) % size


def owner_pairs(seq_size, owners, share, step):
    return [(d, away(d // share, owners, step) * share + d % share) for d in range(seq_size)]


def rows_to_owner(blocks, owner, share):
    owners = blocks.shape[0]
    seq_size = lax.axis_size("seq")
    pieces = []
    for step in range(owners):
        block = lax.dynamic_index_in_dim(blocks, away(owner, owners, step), 0, False)
        if step:
            block = lax.ppermute(block, "seq", owner_pairs(seq_size, owners, share, step))
        pieces.append(block)
    return pieces


def pieces_from_owner(pieces, share):
    owners, seq_size = len(pieces), lax.axis_size("seq")
    return [pieces[0]] + [
        lax.ppermute(pieces[step], "seq", owner_pairs(seq_size, owners, share, step))
        for step in range(1, owners)
    ]


def rows_from_owner(blocks, share):
    owners = blocks.shape[0]
    groups = [[owner * share + rank for owner in range(owners)] for rank in range(share)]
    return lax.all_to_all(blocks, "seq", 0, 0, axis_index_groups=groups)


def share_rows(rows, rank, share):
    seq_size = lax.axis_size("seq")
    if share == 2:
        return lax.ppermute(rows, "seq", [(d, d ^ 1) for d in range(seq_size)])
    groups = [list(range(first, first + share)) for first in range(0, seq_size, share)]
    gathered = lax.all_gather(rows, "seq", axis_index_groups=groups)
    gathered = jnp.roll(gathered, -rank, axis=0)[1:]
    return gathered.reshape((share - 1) * rows.shape[0], rows.shape[1])


def return_rows(rest, rank, share):
    seq_size = lax.axis_size("seq")
    if share == 2:
        return lax.ppermute(rest, "seq", [(d, d ^ 1) for d in range(seq_size)])
    groups = [list(range(first, first + share)) for first in range(0, seq_size, share)]
    parts = rest.reshape(share - 1, rest.shape[0] // (share - 1), rest.shape[1])
    parts = jnp.concatenate([jnp.zeros_like(parts[:1]), parts], axis=0)
    parts = jnp.roll(parts, rank, axis=0)
    return lax.psum_scatter(parts, "seq", scatter_dimension=0, axis_index_groups=groups)


def swap_cores(values):
    seq_size = lax.axis_size("seq")
    return lax.ppermute(values, "seq", [(d, d ^ 1) for d in range(seq_size)])


def line_size():
    return lax.axis_size("seq") // 2


def line_send(values, step):
    seq_size = lax.axis_size("seq")
    return lax.ppermute(values, "seq", owner_pairs(seq_size, seq_size // 2, 2, step))


def plane_send(values, step):
    grp_size = lax.axis_size("grp")
    return lax.ppermute(values, "grp", [(d, away(d, grp_size, step)) for d in range(grp_size)])


def rows_at(values, at, count):
    return lax.dynamic_slice_in_dim(values, at * count, count, 0)


def plane_steps():
    return range(1, lax.axis_size("grp"))


def plane_parts(values):
    grp_size = lax.axis_size("grp")
    group = lax.axis_index("grp")
    count = values.shape[0] // grp_size
    return [rows_at(values, away(group, grp_size, step), count) for step in range(grp_size)]


def send_plane(parts):
    return [parts[0]] + [plane_send(parts[step], step) for step in plane_steps()]


def gather_plane(values):
    return [values] + [plane_send(values, step) for step in plane_steps()]


def line_parts(values):
    length = line_size()
    place = lax.axis_index("seq") // 2
    count = values.shape[0] // length
    return [rows_at(values, away(place, length, step), count) for step in range(length)]


def send_line(parts):
    return [parts[0]] + [line_send(parts[step], step) for step in range(1, len(parts))]


def line_exchange(values):
    length = line_size()
    groups = [list(range(core, 2 * length, 2)) for core in range(2)]
    return lax.all_to_all(values, "seq", 0, 0, axis_index_groups=groups)


def sum_line(values):
    length = line_size()
    groups = [list(range(core, 2 * length, 2)) for core in range(2)]
    return lax.psum(values, "seq", axis_index_groups=groups)


def low_total(parts):
    return total(parts).astype(bf16)


def after(values, *others):
    return lax.optimization_barrier((values,) + others)[0]


def columns(values, width):
    return [values[:, at : at + width] for at in range(0, values.shape[1], width)]


def sum_share(values, share):
    seq_size = lax.axis_size("seq")
    groups = [list(range(first, first + share)) for first in range(0, seq_size, share)]
    return lax.psum(values, "seq", axis_index_groups=groups)


def after_all(values, *others):
    return lax.optimization_barrier(tuple(values) + others)[: len(values)]


def attention_kernel(
    score_scale, query, key, value, query_seg, query_pos, open_seg, key_pos, probs, attended, bias
):
    @pl.when(pl.program_id(1) == 0)
    def _():
        allow = (query_seg[...] == open_seg[...]) | (query_pos[...] == key_pos[...])
        bias[...] = jnp.where(allow, 0.0, MASKED)

    scaled = (query[0].astype(f32) * score_scale).astype(bf16)
    scores = back_product(scaled, key[0]) + bias[...]
    expo = jnp.exp(scores - jnp.max(scores, axis=1, keepdims=True))
    low = (expo * (1.0 / jnp.sum(expo, axis=1, keepdims=True))).astype(bf16)
    probs[0] = low
    attended[0] = product(low, value[0])


def attention(queries, keys, values, query_seg, query_pos, open_seg, key_pos, score_scale):
    head_count, rows, head_width = queries.shape
    key_count = keys.shape[1]
    step = max(32, min(rows, 2**18 // key_count))
    row_block = lambda i, h: (h, i, 0)
    key_block = lambda i, h: (h, 0, 0)
    size = head_count * rows * key_count
    return pl.pallas_call(
        partial(attention_kernel, score_scale),
        grid=(rows // step, head_count),
        in_specs=[
            pl.BlockSpec((1, step, head_width), row_block),
            pl.BlockSpec((1, key_count, head_width), key_block),
            pl.BlockSpec((1, key_count, head_width), key_block),
            pl.BlockSpec((step, 1), lambda i, h: (i, 0)),
            pl.BlockSpec((step, 1), lambda i, h: (i, 0)),
            pl.BlockSpec((1, key_count), lambda i, h: (0, 0)),
            pl.BlockSpec((1, key_count), lambda i, h: (0, 0)),
        ],
        out_specs=[
            pl.BlockSpec((1, step, key_count), row_block),
            pl.BlockSpec((1, step, head_width), row_block),
        ],
        out_shape=[
            jax.ShapeDtypeStruct((head_count, rows, key_count), bf16),
            jax.ShapeDtypeStruct((head_count, rows, head_width), f32),
        ],
        scratch_shapes=[pltpu.VMEM((step, key_count), f32)],
        compiler_params=pltpu.CompilerParams(vmem_limit_bytes=40 * 2**20),
        cost_estimate=pl.CostEstimate(
            flops=4 * size * head_width, bytes_accessed=2 * size, transcendentals=size
        ),
        name="attention",
    )(queries, keys, values, query_seg, query_pos, open_seg, key_pos)


GELU_RATE = math.sqrt(2.0 / math.pi)
GELU_CUBE = 0.044715
SHIFT_ONE, SCALE_ONE, GATE_ONE, SHIFT_TWO, SCALE_TWO, GATE_TWO, SHARE, EMBEDDING = range(8)


def inner(left, right):
    return row_product(left, right)


def column_sum(values):
    return jnp.sum(values, axis=0, keepdims=True)


def whole(*shape):
    return pl.BlockSpec(shape, lambda *_: (0,) * len(shape))


def kernel_params(mebibytes):
    return pltpu.CompilerParams(vmem_limit_bytes=mebibytes * 2**20)


def prepare_kernel(factor, place, lead, counts, table, weight, bias, attend_weight, mod, turned):
    width = table.shape[1]
    here = lax.broadcasted_iota(jnp.int32, table.shape, 0) == lead[0]
    embedding = column_sum(jnp.where(here, table[...].astype(f32), 0.0))
    lifted = (embedding / (1.0 + jnp.exp(-embedding))).astype(bf16)
    modulation = product(lifted, weight[...]) + bias[:, : weight.shape[1]]
    for part in range(6):
        mod[part : part + 1, :] = modulation[:, part * width : (part + 1) * width]
    every, mine = 0, 0
    for group in range(counts.shape[0]):
        every = every + counts[group]
        mine = mine + jnp.where(place[3] == group, counts[group], 0)
    row = jnp.zeros((1, width), jnp.int32)
    mod[SHARE : SHARE + 1, :] = (row + mine).astype(f32) / (row + every).astype(f32) * factor
    mod[EMBEDDING : EMBEDDING + 1, :] = embedding
    turned[...] = attend_weight[...].T


def prepare(place, lead, counts, table, weight, bias, attend_weight, positions):
    width = table.shape[1]
    operands = (table, weight, bias, attend_weight)
    shapes = [
        jax.ShapeDtypeStruct((8, width), f32),
        jax.ShapeDtypeStruct(attend_weight.shape[::-1], bf16),
    ]
    return pl.pallas_call(
        partial(prepare_kernel, counts.shape[0] / math.sqrt(positions)),
        grid=(1,),
        in_specs=[pl.BlockSpec(memory_space=pltpu.SMEM)] * 3 + [whole(*item.shape) for item in operands],
        out_specs=[whole(*item.shape) for item in shapes],
        out_shape=shapes,
        compiler_params=kernel_params(8),
        name="prepare",
    )(place, lead, counts, *operands)


def forward_kernel(
    head_width, score_scale, owners, place, lengths, own, rest, valid, mod, weight,
    expo, query, key_value, attended_wide, inverse_total, attended, bias,
):
    pair = pl.program_id(0)
    rows, width = own.shape
    key_count = rows + rest.shape[0]

    @pl.when(pair == 0)
    def _():
        shift, scale = mod[SHIFT_ONE : SHIFT_ONE + 1, :], 1.0 + mod[SCALE_ONE : SCALE_ONE + 1, :]
        first = (normalize(own[...].astype(f32))[0] * scale + shift).astype(bf16)
        query[...] = back_product(weight[:width, :], first).astype(bf16)
        key_value[:, :rows] = back_product(weight[width:, :], first).astype(bf16)
        for at in range(0, rest.shape[0], rows):
            part = normalize(rest[at : at + rows, :].astype(f32))[0]
            part = (part * scale + shift).astype(bf16)
            key_value[:, rows + at : 2 * rows + at] = back_product(weight[width:, :], part).astype(bf16)

        owner, rank = place[0], place[1]
        share = key_count // rows
        count = rows // owners
        ends = []
        for doc in range(lengths.shape[1]):
            ends.append(lengths[owner, doc] + (ends[-1] if doc else 0))

        def segment(positions):
            return sum((positions >= end).astype(jnp.int32) for end in ends)

        def block_at(r, step):
            return back(owner, owners, step) * share + lax.rem(rank + r, share)

        lane = lax.broadcasted_iota(jnp.int32, (1, count), 1)
        query_pos = jnp.concatenate(
            [block_at(0, step) * count + lane for step in range(owners)], axis=1
        )
        query_seg = segment(query_pos)
        down = lax.broadcasted_iota(jnp.int32, (count, 1), 0)
        mine = lax.broadcasted_iota(jnp.int32, (owners, count), 0) == owner
        for r in range(share):
            for step in range(owners):
                block = block_at(r, step)
                key_pos = block * count + down
                open_rows = valid[:, pl.ds(pl.multiple_of(block * count, count), count)]
                open_rows = jnp.where((open_rows > 0) & mine, 1.0, 0.0)
                open_row = jnp.broadcast_to(column_sum(open_rows), (count, count))
                open_key = open_row.T[:, :1] > 0.5
                open_seg = jnp.where(open_key, segment(key_pos), -1)
                allow = (query_seg == open_seg) | (query_pos == key_pos)
                at = (r * owners + step) * count
                bias[at : at + count, :] = jnp.where(allow, 0.0, MASKED)

    heads = [pl.multiple_of((2 * pair + i) * head_width, head_width) for i in range(2)]
    scores = []
    for first in heads:
        here = pl.ds(first, head_width)
        scaled = (query[here, :].astype(f32) * score_scale).astype(bf16)
        scores.append(inner(key_value[here, :], scaled) + bias[...])
    for i, first in enumerate(heads):
        wide = jnp.exp(scores[i] - jnp.max(scores[i], axis=0, keepdims=True))
        inverse = 1.0 / column_sum(wide)
        low = wide.astype(bf16)
        expo[i] = low
        inverse_total[i] = inverse
        values = key_value[pl.ds(pl.multiple_of(width + first, head_width), head_width), :]
        attended_wide[pl.ds(first, head_width), :] = product(values, low) * inverse

    @pl.when(pair == pl.num_programs(0) - 1)
    def _():
        attended[...] = attended_wide[...].T.astype(bf16)


def forward_attention(place, lengths, valid, own, rest, mod, weight):
    rows, width = own.shape
    key_count = rows + rest.shape[0]
    head_width = width // HEADS
    size = HEADS * rows * key_count
    scalars = pl.BlockSpec(memory_space=pltpu.SMEM)
    return pl.pallas_call(
        partial(forward_kernel, head_width, 1.0 / math.sqrt(head_width), lengths.shape[0]),
        grid=(HEADS // 2,),
        in_specs=[scalars, scalars] + [whole(*item.shape) for item in (own, rest, valid, mod, weight)],
        out_specs=[
            pl.BlockSpec((2, key_count, rows), lambda p: (p, 0, 0)),
            whole(width, rows),
            whole(2 * width, key_count),
            whole(width, rows),
            pl.BlockSpec((2, 1, rows), lambda p: (p, 0, 0)),
            whole(rows, width),
        ],
        out_shape=[
            pltpu.HBM((HEADS, key_count, rows), bf16),
            jax.ShapeDtypeStruct((width, rows), bf16),
            jax.ShapeDtypeStruct((2 * width, key_count), bf16),
            jax.ShapeDtypeStruct((width, rows), f32),
            jax.ShapeDtypeStruct((HEADS, 1, rows), f32),
            jax.ShapeDtypeStruct((rows, width), bf16),
        ],
        scratch_shapes=[pltpu.VMEM((key_count, rows), f32)],
        compiler_params=kernel_params(22),
        cost_estimate=pl.CostEstimate(
            flops=16 * size * head_width, bytes_accessed=2 * size, transcendentals=size
        ),
        name="forward_attention",
    )(place, lengths, own, rest, valid, mod, weight)


def middle_kernel(
    place, own, attended, cotangent, mod, bias, output_weight, expand_weight, shrink_weight,
    keep, send, packed_output, grad_attended, grad_residual, sums, output,
):
    first_core = place[2] == 0
    rows, width = own.shape
    blocks = expand_weight.shape[1] // width
    row = lambda at: mod[at : at + 1, :]
    bias_row = lambda at: bias[:, at * width : (at + 1) * width]
    share = row(SHARE)
    scale_two = 1.0 + row(SCALE_TWO)
    branch_one = product(attended[...], output_weight[...]) + bias_row(6)
    residual = own[...].astype(f32) + row(GATE_ONE) * branch_one
    normed, inverse = normalize(residual)
    mixed = (normed * scale_two + row(SHIFT_TWO)).astype(bf16)
    wide = cotangent[...].astype(f32)
    grad_two = (wide * row(GATE_TWO)).astype(bf16)
    sums[...] = jnp.zeros_like(sums)
    hidden = product(mixed, expand_weight[...]) + bias[:, 7 * width : (7 + blocks) * width]
    square = hidden * hidden
    bent = jnp.tanh(GELU_RATE * hidden * (1.0 + GELU_CUBE * square))
    half = 0.5 + 0.5 * bent
    slope = half + 0.5 * hidden * (1.0 - bent * bent) * (
        GELU_RATE + (3.0 * GELU_CUBE * GELU_RATE) * square
    )
    active = (hidden * half).astype(bf16)
    branch_two = product(active, shrink_weight[...]) + bias_row(7 + blocks)
    grad_hidden = (back_product(grad_two, shrink_weight[...]) * slope).astype(bf16)
    grad_mixed = back_product(grad_hidden, expand_weight[...])
    hidden_sum = column_sum(grad_hidden.astype(f32))
    for block in range(blocks):
        part = slice(block * width, (block + 1) * width)
        grad_shrink = inner(active[:, part], grad_two) * share
        grad_expand = inner(mixed, grad_hidden[:, part]) * share
        keep[part, :] = jnp.where(first_core, grad_shrink, grad_expand).astype(bf16)
        send[part, :] = jnp.where(first_core, grad_expand, grad_shrink).astype(bf16)
        sums[7 + block : 8 + block, :] = hidden_sum[:, part] * share
    result = (residual + row(GATE_TWO) * branch_two).astype(bf16)
    owners, count = output.shape[:2]
    for step in range(owners):
        output[back(place[0], owners, step)] = result[step * count : (step + 1) * count, :]
    sums[5:6, :] = column_sum(wide * branch_two) * share
    sums[7 + blocks : 8 + blocks, :] = column_sum(grad_two.astype(f32)) * share
    sums[4:5, :] = column_sum(grad_mixed * normed) * share
    sums[3:4, :] = column_sum(grad_mixed) * share
    grad_wide = wide + normalize_back(grad_mixed * scale_two, normed, inverse)
    grad_residual[...] = grad_wide
    sums[2:3, :] = column_sum(grad_wide * branch_one) * share
    grad_one = (grad_wide * row(GATE_ONE)).astype(bf16)
    sums[6:7, :] = column_sum(grad_one.astype(f32)) * share
    packed_output[...] = (inner(attended[...], grad_one) * share).astype(bf16)
    grad_attended[...] = back_product(output_weight[...], grad_one).astype(bf16)


def middle(
    owners, place, own, attended, cotangent, mod, bias, output_weight, expand_weight, shrink_weight
):
    rows, width = own.shape
    hidden = expand_weight.shape[1]
    operands = (
        own, attended, cotangent, mod, bias, output_weight, expand_weight, shrink_weight
    )
    shapes = [
        jax.ShapeDtypeStruct((hidden, width), bf16),
        jax.ShapeDtypeStruct((hidden, width), bf16),
        pltpu.HBM((width, width), bf16),
        pltpu.HBM((width, rows), bf16),
        pltpu.HBM((rows, width), f32),
        jax.ShapeDtypeStruct((16, width), f32),
        jax.ShapeDtypeStruct((owners, rows // owners, width), bf16),
    ]
    return pl.pallas_call(
        middle_kernel,
        grid=(1,),
        in_specs=[pl.BlockSpec(memory_space=pltpu.SMEM)] + [whole(*item.shape) for item in operands],
        out_specs=[whole(*item.shape) for item in shapes],
        out_shape=shapes,
        compiler_params=kernel_params(20),
        cost_estimate=pl.CostEstimate(
            flops=16 * rows * width * hidden, bytes_accessed=2**24, transcendentals=rows * hidden
        ),
        name="middle",
    )(place, *operands)


def backward_kernel(
    head_width, score_scale, place, expo, query, key_value, attended_wide, inverse_total,
    grad_attended, own, rest, mod, weight, packed_output, grad_residual, sums_in, keep, send,
    rest_part, own_part, sums,
    grad_query, grad_key, grad_value,
):
    pair = pl.program_id(0)
    rows, width = own.shape
    grad_keys, grad_values = [], []
    for i in range(2):
        first = pl.multiple_of((2 * pair + i) * head_width, head_width)
        here = pl.ds(first, head_width)
        scaled = (query[here, :].astype(f32) * score_scale).astype(bf16)
        keys = key_value[here, :]
        values = key_value[pl.ds(pl.multiple_of(width + first, head_width), head_width), :]
        grads = (grad_attended[here, :].astype(f32) * inverse_total[i]).astype(bf16)
        delta = column_sum(grads.astype(f32) * attended_wide[here, :])
        low = expo[i]
        grad_scores = (low.astype(f32) * (inner(values, grads) - delta)).astype(bf16)
        grad_values.append(back_product(low, grads))
        grad_keys.append(back_product(grad_scores, scaled))
        grad_query[here, :] = (product(keys, grad_scores) * score_scale).astype(bf16)
    grad_key[pair] = jnp.concatenate(grad_keys, axis=1).astype(bf16)
    grad_value[pair] = jnp.concatenate(grad_values, axis=1).astype(bf16)

    @pl.when(pair == pl.num_programs(0) - 1)
    def _():
        row = lambda at: mod[at : at + 1, :]
        share = row(SHARE)
        shift, scale = row(SHIFT_ONE), 1.0 + row(SCALE_ONE)
        pairs = range(HEADS // 2)
        packed_key = jnp.zeros((width, width), f32)
        packed_value = jnp.zeros((width, width), f32)
        total_shift = jnp.zeros((1, width), f32)
        total_scale = jnp.zeros((1, width), f32)
        for at in range(0, rows + rest.shape[0], rows):
            here = slice(at, at + rows)
            source = own[...] if at == 0 else rest[at - rows : at, :]
            normed, inverse = normalize(source.astype(f32))
            mixed = (normed * scale + shift).astype(bf16)
            keys = jnp.concatenate([grad_key[pair, here, :] for pair in pairs], axis=1)
            values = jnp.concatenate([grad_value[pair, here, :] for pair in pairs], axis=1)
            part = product(keys, weight[width : 2 * width, :]) + product(
                values, weight[2 * width :, :]
            )
            if at == 0:
                part = part + inner(grad_query[...], weight[:width, :])
                back = normalize_back(part * scale, normed, inverse)
                own_part[...] = (grad_residual[...] + back).astype(bf16)
                packed_query = product(grad_query[...], mixed).T
            else:
                rest_part[at - rows : at, :] = part.astype(bf16)
            packed_key = packed_key + inner(mixed, keys)
            packed_value = packed_value + inner(mixed, values)
            total_shift = total_shift + column_sum(part)
            total_scale = total_scale + column_sum(part * normed)
        first_core = place[2] == 0
        packed = [packed_query * share, packed_key * share, packed_value * share, packed_output[...].astype(f32)]
        half = width // 2
        for at, matrix in enumerate(packed):
            here = slice(at * half, (at + 1) * half)
            keep[here, :] = jnp.where(first_core, matrix[:half], matrix[half:]).astype(bf16)
            send[here, :] = jnp.where(first_core, matrix[half:], matrix[:half]).astype(bf16)
        sums[...] = sums_in[...]
        sums[0:1, :] = total_shift * share
        sums[1:2, :] = total_scale * share
        rest_part[rest.shape[0] :, :] = sums[...].astype(bf16)


def backward_attention(
    place, saved, grad_attended, own, rest, mod, weight, packed_output, grad_residual, sums
):
    expo, query, key_value, attended_wide, inverse_total = saved
    rows, width = own.shape
    key_count = rows + rest.shape[0]
    head_width = width // HEADS
    size = HEADS * rows * key_count
    operands = (
        query, key_value, attended_wide, inverse_total, grad_attended, own, rest, mod, weight,
        packed_output, grad_residual, sums,
    )
    specs = [whole(*item.shape) for item in operands]
    specs[3] = pl.BlockSpec((2, 1, rows), lambda p: (p, 0, 0))
    shapes = [
        pltpu.HBM((2 * width, width), bf16),
        jax.ShapeDtypeStruct((2 * width, width), bf16),
        pltpu.HBM((rest.shape[0] + sums.shape[0], width), bf16),
        jax.ShapeDtypeStruct((rows, width), bf16),
        jax.ShapeDtypeStruct(sums.shape, f32),
    ]
    return pl.pallas_call(
        partial(backward_kernel, head_width, 1.0 / math.sqrt(head_width)),
        grid=(HEADS // 2,),
        in_specs=[
            pl.BlockSpec(memory_space=pltpu.SMEM),
            pl.BlockSpec((2, key_count, rows), lambda p: (p, 0, 0)),
        ]
        + specs,
        out_specs=[whole(*item.shape) for item in shapes],
        out_shape=shapes,
        scratch_shapes=[
            pltpu.VMEM((width, rows), bf16),
            pltpu.VMEM((HEADS // 2, key_count, 2 * head_width), bf16),
            pltpu.VMEM((HEADS // 2, key_count, 2 * head_width), bf16),
        ],
        compiler_params=kernel_params(16),
        cost_estimate=pl.CostEstimate(
            flops=32 * size * head_width, bytes_accessed=2 * size, transcendentals=0
        ),
        name="backward_attention",
    )(place, pltpu.with_memory_space_constraint(expo, pltpu.HBM), *operands)


def finish_kernel(owners, own, part, received, mod, *refs):
    parts, results = refs[:-owners], refs[-owners:]
    rows, width = own.shape
    count = rows // owners
    normed, inverse = normalize(own[...].astype(f32))
    grad = received[:rows, :].astype(f32) * (1.0 + mod[SCALE_ONE : SCALE_ONE + 1, :])
    grad = (part[...].astype(f32) + normalize_back(grad, normed, inverse)).astype(bf16)
    for step, result in enumerate(results):
        result[:count, :] = grad[step * count : (step + 1) * count, :]
    if parts:
        summed = total([ref[...] for ref in parts]).astype(bf16)
        for result in results:
            result[count:, :] = summed


def finish_rows(owners, own, part, received, mod, parts):
    operands = [own, part, received, mod] + parts
    shape = (own.shape[0] // owners + (parts[0].shape[0] if parts else 0), own.shape[1])
    return pl.pallas_call(
        partial(finish_kernel, owners),
        grid=(1,),
        in_specs=[whole(*item.shape) for item in operands],
        out_specs=[whole(*shape)] * owners,
        out_shape=[jax.ShapeDtypeStruct(shape, bf16)] * owners,
        compiler_params=kernel_params(12),
        name="finish_rows",
    )(*operands)


def pair_parts_kernel(grp_size, place, kept, received, *results):
    count = results[0].shape[0]
    for step, result in enumerate(results):
        here = pl.ds(pl.multiple_of(away(place[3], grp_size, step) * count, count), count)
        result[...] = total([kept[here, :], received[here, :]]).astype(bf16)


def pair_parts(place, kept, received):
    grp_size = lax.axis_size("grp")
    shape = (kept.shape[0] // grp_size, kept.shape[1])
    return pl.pallas_call(
        partial(pair_parts_kernel, grp_size),
        grid=(1,),
        in_specs=[pl.BlockSpec(memory_space=pltpu.SMEM)] + [whole(*kept.shape)] * 2,
        out_specs=[whole(*shape)] * grp_size,
        out_shape=[jax.ShapeDtypeStruct(shape, bf16)] * grp_size,
        compiler_params=kernel_params(12),
        name="pair_parts",
    )(place, kept, received)


def sum_parts_kernel(*refs):
    refs[-1][...] = total([ref[...] for ref in refs[:-1]]).astype(bf16)


def sum_parts(parts):
    return pl.pallas_call(
        sum_parts_kernel,
        grid=(1,),
        in_specs=[whole(*parts[0].shape)] * len(parts),
        out_specs=whole(*parts[0].shape),
        out_shape=jax.ShapeDtypeStruct(parts[0].shape, bf16),
        compiler_params=kernel_params(8),
        name="sum_parts",
    )(*parts)


def line_total_kernel(sums, received, *refs):
    parts, result = refs[:-1], refs[-1]
    count = parts[0].shape[-2]
    if len(parts[0].shape) == 3:
        parts = [parts[0].at[at] for at in range(parts[0].shape[0])]
    result[:count, :] = total([part[...] for part in parts]).astype(bf16)
    below = received[received.shape[0] - sums.shape[0] :, :].astype(f32)
    result[count:, :] = (sums[...] + below).astype(bf16)


def line_total(parts, sums, received):
    count, width = parts[0].shape[-2:]
    below = sums.shape[0]
    return pl.pallas_call(
        line_total_kernel,
        grid=(1,),
        in_specs=[whole(*item.shape) for item in [sums, received] + parts],
        out_specs=whole(count + below, width),
        out_shape=jax.ShapeDtypeStruct((count + below, width), bf16),
        compiler_params=kernel_params(4),
        name="line_total",
    )(sums, received, *parts)


def with_lead(below, lead, mod):
    row = lax.broadcasted_iota(jnp.int32, below.shape, 0)
    below = jnp.where(row == 12, mod[EMBEDDING : EMBEDDING + 1, :], below)
    return jnp.where(row == 13, jnp.full(below.shape, lead).astype(f32), below).astype(bf16)


def line_join_kernel(lead, mod, *refs):
    parts, result = refs[:-1], refs[-1]
    count = (result.shape[0] - 16) // len(parts)
    for at, part in enumerate(parts):
        result[at * count : (at + 1) * count, :] = part[:count, :]
    below = total([part[count:, :] for part in parts])
    result[len(parts) * count :, :] = with_lead(below, lead[0], mod)


def line_join(lead, mod, parts):
    rows, width = parts[0].shape
    shape = (len(parts) * (rows - 16) + 16, width)
    return pl.pallas_call(
        line_join_kernel,
        grid=(1,),
        in_specs=[pl.BlockSpec(memory_space=pltpu.SMEM)]
        + [whole(*item.shape) for item in [mod] + parts],
        out_specs=whole(*shape),
        out_shape=jax.ShapeDtypeStruct(shape, bf16),
        compiler_params=kernel_params(8),
        name="line_join",
    )(lead, mod, *parts)


def picked(place, grp_size, own, received, side, b, write):
    group = place[3]
    for step in range(grp_size):
        here = back(group, grp_size, b) == step
        for ref, mine in ((own[step], True), (received[step], False)):

            @pl.when(here & ((place[2] == side) == mine))
            def _():
                write(ref)


def copy_line(place, line, count, ref, output, first):
    for c in range(line):
        from_c = back(place[4], line, c) if line > 1 else 0
        here = pl.ds(pl.multiple_of(from_c * count, count), count) if line > 1 else slice(0, count)
        output[first + c * count : first + (c + 1) * count, :] = ref[here, :].astype(f32)


def first_sums_kernel(grp_size, line, place, *refs):
    own, received = refs[:grp_size], refs[grp_size : 2 * grp_size]
    refs = refs[2 * grp_size :]
    weight, output = refs[:2]
    owners = len(refs) - 14
    pieces, refs = refs[2 : 2 + owners], refs[2 + owners :]
    shrink, expand, grad_weight, copied, rows, table, grad_bias = refs[:7]
    output_bias, expand_bias, shrink_bias, grad_lifted, sums = refs[7:]
    b = pl.program_id(0)
    width = table.shape[1]
    count = own[0].shape[0] - 16
    copied[...] = output[...]
    for step, piece in enumerate(pieces):

        @pl.when(back(place[0], owners, step) == b)
        def _():
            rows[0] = piece[: rows.shape[1], :].astype(f32)

    for side, target in enumerate((shrink, expand)):
        write = lambda ref: copy_line(place, line, count // line, ref, target, 0)
        picked(place, grp_size, own, received, side, b, write)

    parts = [part[count:, :].astype(f32) for part in own]
    pad = jnp.zeros((8 - grp_size, width), f32)
    stacked = jnp.concatenate([part[12:13] for part in parts] + [pad])
    gate = 1.0 / (1.0 + jnp.exp(-stacked))

    @pl.when(b == 0)
    def _():
        sums[...] = total(parts)
        grad_lifted[...] = jnp.zeros_like(grad_lifted)

    @pl.when(b < 3)
    def _():
        lifted = (stacked * gate).astype(bf16)
        line_of = lax.broadcasted_iota(jnp.int32, parts[0].shape, 0)
        for i in range(2):
            here = slice(i * width, (i + 1) * width)
            picks = [column_sum(jnp.where(line_of == 2 * b + i, part, 0.0)) for part in parts]
            picks = jnp.concatenate(picks + [pad]).astype(bf16)
            grad_weight[:, here] = inner(lifted, picks)
            grad_lifted[...] += back_product(picks, weight[:, here])

    @pl.when(b == pl.num_programs(0) - 1)
    def _():
        for at in range(6):
            grad_bias[at * width : (at + 1) * width] = sums[at]
        output_bias[...] = sums[6]
        for at in range(expand_bias.shape[0] // width):
            expand_bias[at * width : (at + 1) * width] = sums[7 + at]
        shrink_bias[...] = sums[7 + expand_bias.shape[0] // width]
        grad_embedding = grad_lifted[...] * gate * (1.0 + stacked * (1.0 - gate))
        lead = lax.broadcasted_iota(jnp.int32, (LEADS, width), 0).astype(f32)
        table[...] = total(
            [
                jnp.where(lead == part[13:14], grad_embedding[p : p + 1], 0.0)
                for p, part in enumerate(parts)
            ]
        )


def first_sums(place, own, weight, output, pieces):
    grp_size = len(own)
    line = 1 if line_size() > 4 else line_size()
    received = [swap_cores(part) for part in own]
    width = weight.shape[0]
    hidden = grp_size * width
    block = pl.BlockSpec((1,) + output.shape[1:], lambda b: (b, 0, 0))
    wide = pl.BlockSpec((width, 2 * width), lambda b: (0, jnp.minimum(b, 2)))
    return pl.pallas_call(
        partial(first_sums_kernel, grp_size, line),
        grid=(grp_size,),
        in_specs=[pl.BlockSpec(memory_space=pltpu.SMEM)]
        + [whole(*own[0].shape)] * (2 * grp_size)
        + [wide, block]
        + [whole(*item.shape) for item in pieces],
        out_specs=[
            pl.BlockSpec((width, width), lambda b: (b, 0)),
            pl.BlockSpec((width, width), lambda b: (0, b)),
            wide,
            block,
            block,
            whole(LEADS, width),
            whole(6 * width),
            whole(width),
            whole(hidden),
            whole(width),
        ],
        out_shape=[
            jax.ShapeDtypeStruct((hidden, width), f32),
            jax.ShapeDtypeStruct((width, hidden), f32),
            jax.ShapeDtypeStruct(weight.shape, f32),
            jax.ShapeDtypeStruct(output.shape, output.dtype),
            jax.ShapeDtypeStruct(output.shape, f32),
            jax.ShapeDtypeStruct((LEADS, width), f32),
            jax.ShapeDtypeStruct((6 * width,), f32),
            jax.ShapeDtypeStruct((width,), f32),
            jax.ShapeDtypeStruct((hidden,), f32),
            jax.ShapeDtypeStruct((width,), f32),
        ],
        scratch_shapes=[pltpu.VMEM((8, width), f32), pltpu.VMEM((16, width), f32)],
        compiler_params=kernel_params(16),
        name="first_sums",
    )(place, *own, *received, weight, output, *pieces)


def second_sums_kernel(grp_size, line, place, *refs):
    own, received = refs[:grp_size], refs[grp_size : 2 * grp_size]
    attend, output = refs[2 * grp_size :]
    width = output.shape[0]
    half = width // 2
    for group in range(grp_size):
        for core in range(2):

            @pl.when((place[3] == group) & (place[2] == core))
            def _():
                for b in range(grp_size):
                    step = back(group, grp_size, b)
                    for side, parts in ((core, own), (1 - core, received)):
                        if b < grp_size - 1:
                            target = attend.at[:, b * width : (b + 1) * width]
                        else:
                            target = output
                        copy_line(place, line, half // line, parts[step], target, side * half)


def second_sums(place, own):
    grp_size, width = len(own), own[0].shape[1]
    line = 1 if line_size() > 4 else line_size()
    received = [swap_cores(part) for part in own]
    shapes = [(width, (grp_size - 1) * width), (width, width)]
    return pl.pallas_call(
        partial(second_sums_kernel, grp_size, line),
        grid=(1,),
        in_specs=[pl.BlockSpec(memory_space=pltpu.SMEM)] + [whole(*own[0].shape)] * (2 * grp_size),
        out_specs=[whole(*shape) for shape in shapes],
        out_shape=[jax.ShapeDtypeStruct(shape, f32) for shape in shapes],
        compiler_params=kernel_params(16),
        name="second_sums",
    )(place, *own, *received)


def long_forward(owner, rank, share, lengths, valid, own, rest, mod, weight):
    rows, width = own.shape
    owners = lengths.shape[0]
    count = rows // owners
    steps = jnp.arange(owners, dtype=jnp.int32)
    ranks = (rank + jnp.arange(share, dtype=jnp.int32)) % share
    blocks = (back(owner, owners, steps)[None, :] * share + ranks[:, None]).reshape(-1, 1)
    key_pos = blocks * count + jnp.arange(count, dtype=jnp.int32)[None, :]
    doc_ends = jnp.cumsum(lax.dynamic_index_in_dim(lengths, owner, 0, False))
    key_seg = sum((key_pos >= doc_ends[doc]).astype(jnp.int32) for doc in range(doc_ends.shape[0]))
    own_valid = lax.dynamic_index_in_dim(valid, owner, 0, False).reshape(-1, count)
    key_valid = own_valid[blocks[:, 0]] > 0
    open_seg = jnp.where(key_valid, key_seg, -1).reshape(1, -1)
    key_pos = key_pos.reshape(1, -1)
    query_seg = key_seg.reshape(-1, 1)[:rows]
    query_pos = key_pos.reshape(-1, 1)[:rows]
    head_width = width // HEADS
    normed = normalize(jnp.concatenate([own, rest], axis=0).astype(f32))[0]
    mixed = (normed * (1.0 + mod[SCALE_ONE]) + mod[SHIFT_ONE]).astype(bf16)
    heads = lambda v: v.reshape(v.shape[0], HEADS, head_width).transpose(1, 0, 2)
    queries = heads(back_product(mixed[:rows], weight[:width]).astype(bf16))
    key_value = back_product(mixed, weight[width:]).astype(bf16)
    keys = heads(key_value[:, :width])
    values = heads(key_value[:, width:])
    probs, attended = attention(
        queries, keys, values, query_seg, query_pos, open_seg, key_pos, 1.0 / math.sqrt(head_width)
    )
    flat = attended.transpose(1, 0, 2).reshape(rows, width).astype(bf16)
    return ((probs, queries, keys, values, attended, normed, mixed), flat)


def long_backward(
    place, saved, grad_attended, own, rest, mod, weight, packed_output, grad_residual, sums
):
    probs, queries, keys, values, attended, normed, mixed = saved
    rows, width = own.shape
    head_width = width // HEADS
    score_scale = 1.0 / math.sqrt(head_width)
    grad_heads = grad_attended.reshape(HEADS, head_width, rows).transpose(0, 2, 1)
    deltas = jnp.sum(grad_heads.astype(f32) * attended, axis=-1, keepdims=True)
    grad_probs = jnp.einsum("hqd,hkd->hqk", grad_heads, values, preferred_element_type=f32)
    grad_scores = (probs.astype(f32) * (grad_probs - deltas)).astype(bf16)
    grad_query = jnp.einsum("hqk,hkd->hqd", grad_scores, keys, preferred_element_type=f32)
    grad_key = jnp.einsum("hqk,hqd->hkd", grad_scores, queries, preferred_element_type=f32)
    grad_value = jnp.einsum("hqk,hqd->hkd", probs, grad_heads, preferred_element_type=f32)
    flat = lambda v: v.transpose(1, 0, 2).reshape(v.shape[1], width)
    grad_query = (flat(grad_query) * score_scale).astype(bf16)
    grad_key = (flat(grad_key) * score_scale).astype(bf16)
    grad_value = flat(grad_value).astype(bf16)
    part = product(grad_key, weight[width : 2 * width]) + product(grad_value, weight[2 * width :])
    part = jnp.concatenate([part[:rows] + product(grad_query, weight[:width]), part[rows:]], axis=0)
    share = mod[SHARE]
    packed = [row_product(mixed[:rows], grad_query), row_product(mixed, grad_key), row_product(mixed, grad_value)]
    packed = [(matrix * share).astype(bf16) for matrix in packed] + [packed_output]
    half = width // 2
    top = jnp.concatenate([matrix[:half] for matrix in packed])
    bottom = jnp.concatenate([matrix[half:] for matrix in packed])
    first_core = place[2] == 0
    keep = jnp.where(first_core, top, bottom)
    send = jnp.where(first_core, bottom, top)
    total_rows = jnp.stack([jnp.sum(part, axis=0), jnp.sum(part * normed, axis=0)]) * share
    sums = jnp.concatenate([total_rows, sums[2:]], axis=0)
    normed, inverse = normalize(own.astype(f32))
    own_part = grad_residual + normalize_back(part[:rows] * (1.0 + mod[SCALE_ONE]), normed, inverse)
    return (keep, send, part[rows:].astype(bf16), own_part.astype(bf16), sums)


def on_device(
    tokens,
    cotangent,
    lengths,
    valid_mask,
    lead_index,
    sample_counts,
    lead_table,
    modulation_weight,
    modulation_bias,
    attend_weight,
    output_weight,
    output_bias,
    expand_weight,
    expand_bias,
    shrink_weight,
    shrink_bias,
):
    owners = tokens.shape[1]
    block_rows = tokens.shape[2]
    width = tokens.shape[3]
    hidden_width = expand_bias.shape[0]
    seq_size = lax.axis_size("seq")
    share = seq_size // owners
    seq_length = block_rows * seq_size
    rows = owners * block_rows
    place = lax.axis_index("seq")
    owner = place // share
    rank = place % share

    where = jnp.stack([owner, rank, place % 2, lax.axis_index("grp"), place // 2]).astype(jnp.int32)

    token_pieces = rows_to_owner(tokens[0], owner, share)

    bias = [modulation_bias, output_bias, expand_bias, shrink_bias]
    bias = after(jnp.concatenate(bias).astype(f32))[None]
    mod, weight = prepare(
        where, lead_index, sample_counts, lead_table, modulation_weight, bias, attend_weight,
        owners * seq_length,
    )
    grad_pieces = rows_to_owner(after(cotangent[0], mod), owner, share)
    token_pieces = after_all(token_pieces, mod)
    own_tokens = jnp.concatenate(token_pieces, axis=0)
    rest_tokens = share_rows(own_tokens, rank, share)
    short = seq_length <= 2048
    if short:
        *saved, attended = forward_attention(
            where, lengths[0], valid_mask[0], own_tokens, rest_tokens, mod, weight
        )
    else:
        saved, attended = long_forward(
            owner, rank, share, lengths[0], valid_mask[0], own_tokens, rest_tokens, mod, weight
        )
    grad_out = jnp.concatenate(after_all(grad_pieces, attended), axis=0)
    ff_keep, ff_send, packed_output, grad_attended, grad_residual, sums, output = middle(
        owners, where, own_tokens, attended, grad_out, mod, bias, output_weight, expand_weight,
        shrink_weight,
    )
    output = rows_from_owner(output, share)
    ff_core = low_total([ff_keep, swap_cores(ff_send)])
    ff_parts = send_plane(plane_parts(ff_core))
    grad_attended = after(grad_attended, ff_core)
    backward = backward_attention if short else long_backward
    held = backward(
        where, saved, grad_attended, own_tokens, rest_tokens, mod, weight, packed_output,
        grad_residual, sums,
    )
    at_keep, at_send, rest_part, own_part, sums = after_all(held, *ff_parts[1:], output)
    ff_plane = sum_parts(ff_parts)
    line = line_size() <= 4
    if line:
        ff_parts = [line_exchange(ff_plane.reshape(line_size(), -1, width))]
    at_core = low_total([at_keep, swap_cores(at_send)])
    if share == 2:
        received = swap_cores(rest_part)
    else:
        received = return_rows(rest_part, rank, share)
    at_slices = plane_parts(at_core)
    at_parts = send_plane(at_slices)
    if line:
        ff_parts = list(after_all(ff_parts, *at_slices))
        ff_line = line_total(ff_parts, sums, received)
        at_parts = after_all(at_parts, ff_line)
    at_plane = low_total(at_parts)
    if line:
        ff_pieces = send_line([ff_line] * line_size())
        ff_plane = line_join(lead_index, mod, ff_pieces)
        at_line = send_line(line_parts(at_plane))
    else:
        vector = with_lead(lax.psum(sums, "seq"), lead_index[0], mod)
        ff_pieces = [sum_line(ff_plane)]
        ff_plane = jnp.concatenate(ff_pieces + [vector])
        at_line = []
    pieces = finish_rows(owners, own_tokens, own_part, received, mod, at_line)
    pieces = pieces_from_owner(pieces, share)
    at_pieces = [piece[block_rows:] for piece in pieces] if line else [sum_line(at_plane)]
    ff_parts = gather_plane(ff_plane)
    at_parts = gather_plane(jnp.concatenate(at_pieces))
    ff_parts = list(after_all(ff_parts, *pieces))
    grad_shrink, grad_expand, grad_mod_weight, output, grad_tokens, grad_table, grad_mod_bias, *biases = (
        first_sums(where, ff_parts, modulation_weight, output, pieces)
    )
    at_parts = list(after_all(at_parts, grad_shrink))
    grad_attend, grad_output = second_sums(where, at_parts)
    return (
        output[None],
        grad_tokens[None],
        grad_table,
        grad_mod_weight,
        grad_mod_bias,
        grad_attend,
        grad_output,
        biases[0],
        grad_expand,
        biases[1],
        grad_shrink,
        biases[2],
    )


def solution(mesh):
    rows = P("grp", None, "seq", None)
    placed = (rows, rows, P("grp", None, None), P("grp", None, None), P("grp")) + (P(),) * 11
    return jax.shard_map(
        on_device,
        mesh=mesh,
        in_specs=placed,
        out_specs=(rows, rows) + (P(),) * 10,
        check_vma=False,
    )
```

```python
from functools import partial
import math

import jax
import jax.numpy as jnp
from jax import lax
from jax.experimental import pallas as pl
from jax.experimental.pallas import tpu as pltpu
from jax.sharding import PartitionSpec as P

HEADS = 6
LEADS = 8

EPSILON = 1e-06
MASKED = -1e30

bf16 = jnp.bfloat16
f32 = jnp.float32


def normalize(values):
    centred = values - jnp.mean(values, axis=-1, keepdims=True)
    inverse = lax.rsqrt(jnp.mean(centred * centred, axis=-1, keepdims=True) + EPSILON)
    return (centred * inverse, inverse)


def normalize_back(grad, normed, inverse):
    return inverse * (
        grad
        - jnp.mean(grad, axis=-1, keepdims=True)
        - normed * jnp.mean(grad * normed, axis=-1, keepdims=True)
    )


def row_product(left, right):
    return lax.dot_general(left, right, (((0,), (0,)), ((), ())), preferred_element_type=f32)


def back_product(grad, weight):
    return lax.dot_general(grad, weight, (((1,), (1,)), ((), ())), preferred_element_type=f32)


def product(left, right):
    return jnp.dot(left, right, preferred_element_type=f32)


def total(parts):
    result = parts[0].astype(f32)
    for part in parts[1:]:
        result = result + part.astype(f32)
    return result


def away(index, size, step):
    return index ^ step if size & (size - 1) == 0 else (index + step) % size


def back(index, size, step):
    return index ^ step if size & (size - 1) == 0 else (index - step) % size


def owner_pairs(seq_size, owners, share, step):
    return [(d, away(d // share, owners, step) * share + d % share) for d in range(seq_size)]


def rows_to_owner(blocks, owner, share, earlier=None):
    owners = blocks.shape[0]
    seq_size = lax.axis_size("seq")
    pieces = []
    for step in range(owners):
        block = lax.dynamic_index_in_dim(blocks, away(owner, owners, step), 0, False)
        if step and earlier:
            block = after(block, earlier[step])
        if step:
            block = lax.ppermute(block, "seq", owner_pairs(seq_size, owners, share, step))
        pieces.append(block)
    return pieces


def pieces_from_owner(pieces, share):
    owners, seq_size = len(pieces), lax.axis_size("seq")
    return [pieces[0]] + [
        lax.ppermute(pieces[step], "seq", owner_pairs(seq_size, owners, share, step))
        for step in range(1, owners)
    ]


def rows_from_owner(blocks, share):
    owners = blocks.shape[0]
    groups = [[owner * share + rank for owner in range(owners)] for rank in range(share)]
    return lax.all_to_all(blocks, "seq", 0, 0, axis_index_groups=groups)


def share_rows(rows, rank, share):
    seq_size = lax.axis_size("seq")
    if share == 2:
        return lax.ppermute(rows, "seq", [(d, d ^ 1) for d in range(seq_size)])
    groups = [list(range(first, first + share)) for first in range(0, seq_size, share)]
    gathered = lax.all_gather(rows, "seq", axis_index_groups=groups)
    gathered = jnp.roll(gathered, -rank, axis=0)[1:]
    return gathered.reshape((share - 1) * rows.shape[0], rows.shape[1])


def return_rows(rest, rank, share):
    seq_size = lax.axis_size("seq")
    if share == 2:
        return lax.ppermute(rest, "seq", [(d, d ^ 1) for d in range(seq_size)])
    groups = [list(range(first, first + share)) for first in range(0, seq_size, share)]
    parts = rest.reshape(share - 1, rest.shape[0] // (share - 1), rest.shape[1])
    parts = jnp.concatenate([jnp.zeros_like(parts[:1]), parts], axis=0)
    parts = jnp.roll(parts, rank, axis=0)
    return lax.psum_scatter(parts, "seq", scatter_dimension=0, axis_index_groups=groups)


def swap_cores(values):
    seq_size = lax.axis_size("seq")
    return lax.ppermute(values, "seq", [(d, d ^ 1) for d in range(seq_size)])


def line_size():
    return lax.axis_size("seq") // 2


def line_send(values, step):
    seq_size = lax.axis_size("seq")
    return lax.ppermute(values, "seq", owner_pairs(seq_size, seq_size // 2, 2, step))


def plane_send(values, step):
    grp_size = lax.axis_size("grp")
    return lax.ppermute(values, "grp", [(d, away(d, grp_size, step)) for d in range(grp_size)])


def rows_at(values, at, count):
    return lax.dynamic_slice_in_dim(values, at * count, count, 0)


def plane_steps():
    return range(1, lax.axis_size("grp"))


def plane_parts(values):
    grp_size = lax.axis_size("grp")
    group = lax.axis_index("grp")
    count = values.shape[0] // grp_size
    return [rows_at(values, away(group, grp_size, step), count) for step in range(grp_size)]


def send_plane(parts):
    return [parts[0]] + [plane_send(parts[step], step) for step in plane_steps()]


def gather_plane(values):
    return [values] + [plane_send(values, step) for step in plane_steps()]


def line_parts(values):
    length = line_size()
    place = lax.axis_index("seq") // 2
    count = values.shape[0] // length
    return [rows_at(values, away(place, length, step), count) for step in range(length)]


def send_line(parts):
    return [parts[0]] + [line_send(parts[step], step) for step in range(1, len(parts))]


def line_exchange(values):
    length = line_size()
    groups = [list(range(core, 2 * length, 2)) for core in range(2)]
    return lax.all_to_all(values, "seq", 0, 0, axis_index_groups=groups)


def sum_line(values):
    length = line_size()
    groups = [list(range(core, 2 * length, 2)) for core in range(2)]
    return lax.psum(values, "seq", axis_index_groups=groups)


def low_total(parts):
    return total(parts).astype(bf16)


def after(values, *others):
    return lax.optimization_barrier((values,) + others)[0]


def columns(values, width):
    return [values[:, at : at + width] for at in range(0, values.shape[1], width)]


def sum_share(values, share):
    seq_size = lax.axis_size("seq")
    groups = [list(range(first, first + share)) for first in range(0, seq_size, share)]
    return lax.psum(values, "seq", axis_index_groups=groups)


def after_all(values, *others):
    return lax.optimization_barrier(tuple(values) + others)[: len(values)]


def attention_kernel(
    score_scale, query, key, value, query_seg, query_pos, open_seg, key_pos, probs, attended, bias
):
    @pl.when(pl.program_id(1) == 0)
    def _():
        allow = (query_seg[...] == open_seg[...]) | (query_pos[...] == key_pos[...])
        bias[...] = jnp.where(allow, 0.0, MASKED)

    scaled = (query[0].astype(f32) * score_scale).astype(bf16)
    scores = back_product(scaled, key[0]) + bias[...]
    expo = jnp.exp(scores - jnp.max(scores, axis=1, keepdims=True))
    low = (expo * (1.0 / jnp.sum(expo, axis=1, keepdims=True))).astype(bf16)
    probs[0] = low
    attended[0] = product(low, value[0])


def attention(queries, keys, values, query_seg, query_pos, open_seg, key_pos, score_scale):
    head_count, rows, head_width = queries.shape
    key_count = keys.shape[1]
    step = max(32, min(rows, 2**18 // key_count))
    row_block = lambda i, h: (h, i, 0)
    key_block = lambda i, h: (h, 0, 0)
    size = head_count * rows * key_count
    return pl.pallas_call(
        partial(attention_kernel, score_scale),
        grid=(rows // step, head_count),
        in_specs=[
            pl.BlockSpec((1, step, head_width), row_block),
            pl.BlockSpec((1, key_count, head_width), key_block),
            pl.BlockSpec((1, key_count, head_width), key_block),
            pl.BlockSpec((step, 1), lambda i, h: (i, 0)),
            pl.BlockSpec((step, 1), lambda i, h: (i, 0)),
            pl.BlockSpec((1, key_count), lambda i, h: (0, 0)),
            pl.BlockSpec((1, key_count), lambda i, h: (0, 0)),
        ],
        out_specs=[
            pl.BlockSpec((1, step, key_count), row_block),
            pl.BlockSpec((1, step, head_width), row_block),
        ],
        out_shape=[
            jax.ShapeDtypeStruct((head_count, rows, key_count), bf16),
            jax.ShapeDtypeStruct((head_count, rows, head_width), f32),
        ],
        scratch_shapes=[pltpu.VMEM((step, key_count), f32)],
        compiler_params=pltpu.CompilerParams(vmem_limit_bytes=40 * 2**20),
        cost_estimate=pl.CostEstimate(
            flops=4 * size * head_width, bytes_accessed=2 * size, transcendentals=size
        ),
        name="attention",
    )(queries, keys, values, query_seg, query_pos, open_seg, key_pos)


GELU_RATE = math.sqrt(2.0 / math.pi)
GELU_CUBE = 0.044715
SHIFT_ONE, SCALE_ONE, GATE_ONE, SHIFT_TWO, SCALE_TWO, GATE_TWO, SHARE, EMBEDDING = range(8)


def inner(left, right):
    return row_product(left, right)


def column_sum(values):
    return jnp.sum(values, axis=0, keepdims=True)


def whole(*shape):
    return pl.BlockSpec(shape, lambda *_: (0,) * len(shape))


def kernel_params(mebibytes):
    return pltpu.CompilerParams(vmem_limit_bytes=mebibytes * 2**20)


def prepare_kernel(factor, place, lead, counts, table, weight, bias, attend_weight, mod, turned):
    width = table.shape[1]
    here = lax.broadcasted_iota(jnp.int32, table.shape, 0) == lead[0]
    embedding = column_sum(jnp.where(here, table[...].astype(f32), 0.0))
    lifted = (embedding / (1.0 + jnp.exp(-embedding))).astype(bf16)
    modulation = product(lifted, weight[...]) + bias[:, : weight.shape[1]]
    for part in range(6):
        mod[part : part + 1, :] = modulation[:, part * width : (part + 1) * width]
    every, mine = 0, 0
    for group in range(counts.shape[0]):
        every = every + counts[group]
        mine = mine + jnp.where(place[3] == group, counts[group], 0)
    row = jnp.zeros((1, width), jnp.int32)
    mod[SHARE : SHARE + 1, :] = (row + mine).astype(f32) / (row + every).astype(f32) * factor
    mod[EMBEDDING : EMBEDDING + 1, :] = embedding
    turned[...] = attend_weight[...].T


def prepare(place, lead, counts, table, weight, bias, attend_weight, positions):
    width = table.shape[1]
    operands = (table, weight, bias, attend_weight)
    shapes = [
        jax.ShapeDtypeStruct((8, width), f32),
        jax.ShapeDtypeStruct(attend_weight.shape[::-1], bf16),
    ]
    return pl.pallas_call(
        partial(prepare_kernel, counts.shape[0] / math.sqrt(positions)),
        grid=(1,),
        in_specs=[pl.BlockSpec(memory_space=pltpu.SMEM)] * 3 + [whole(*item.shape) for item in operands],
        out_specs=[whole(*item.shape) for item in shapes],
        out_shape=shapes,
        compiler_params=kernel_params(8),
        name="prepare",
    )(place, lead, counts, *operands)


def forward_kernel(
    head_width, score_scale, owners, place, lengths, own, rest, valid, mod, weight,
    expo, query, key_value, attended_wide, inverse_total, attended, bias,
):
    pair = pl.program_id(0)
    rows, width = own.shape
    key_count = rows + rest.shape[0]

    @pl.when(pair == 0)
    def _():
        shift, scale = mod[SHIFT_ONE : SHIFT_ONE + 1, :], 1.0 + mod[SCALE_ONE : SCALE_ONE + 1, :]
        first = (normalize(own[...].astype(f32))[0] * scale + shift).astype(bf16)
        query[...] = back_product(weight[:width, :], first).astype(bf16)
        key_value[:, :rows] = back_product(weight[width:, :], first).astype(bf16)
        for at in range(0, rest.shape[0], rows):
            part = normalize(rest[at : at + rows, :].astype(f32))[0]
            part = (part * scale + shift).astype(bf16)
            key_value[:, rows + at : 2 * rows + at] = back_product(weight[width:, :], part).astype(bf16)

        owner, rank = place[0], place[1]
        share = key_count // rows
        count = rows // owners
        ends = []
        for doc in range(lengths.shape[1]):
            ends.append(lengths[owner, doc] + (ends[-1] if doc else 0))

        def segment(positions):
            return sum((positions >= end).astype(jnp.int32) for end in ends)

        def block_at(r, step):
            return back(owner, owners, step) * share + lax.rem(rank + r, share)

        lane = lax.broadcasted_iota(jnp.int32, (1, count), 1)
        query_pos = jnp.concatenate(
            [block_at(0, step) * count + lane for step in range(owners)], axis=1
        )
        query_seg = segment(query_pos)
        down = lax.broadcasted_iota(jnp.int32, (count, 1), 0)
        mine = lax.broadcasted_iota(jnp.int32, (owners, count), 0) == owner
        for r in range(share):
            for step in range(owners):
                block = block_at(r, step)
                key_pos = block * count + down
                open_rows = valid[:, pl.ds(pl.multiple_of(block * count, count), count)]
                open_rows = jnp.where((open_rows > 0) & mine, 1.0, 0.0)
                open_row = jnp.broadcast_to(column_sum(open_rows), (count, count))
                open_key = open_row.T[:, :1] > 0.5
                open_seg = jnp.where(open_key, segment(key_pos), -1)
                allow = (query_seg == open_seg) | (query_pos == key_pos)
                at = (r * owners + step) * count
                bias[at : at + count, :] = jnp.where(allow, 0.0, MASKED)

    heads = [pl.multiple_of((2 * pair + i) * head_width, head_width) for i in range(2)]
    scores = []
    for first in heads:
        here = pl.ds(first, head_width)
        scaled = (query[here, :].astype(f32) * score_scale).astype(bf16)
        scores.append(inner(key_value[here, :], scaled) + bias[...])
    for i, first in enumerate(heads):
        wide = jnp.exp(scores[i] - jnp.max(scores[i], axis=0, keepdims=True))
        inverse = 1.0 / column_sum(wide)
        low = wide.astype(bf16)
        expo[i] = low
        inverse_total[i] = inverse
        values = key_value[pl.ds(pl.multiple_of(width + first, head_width), head_width), :]
        attended_wide[pl.ds(first, head_width), :] = product(values, low) * inverse

    @pl.when(pair == pl.num_programs(0) - 1)
    def _():
        attended[...] = attended_wide[...].T.astype(bf16)


def forward_attention(place, lengths, valid, own, rest, mod, weight):
    rows, width = own.shape
    key_count = rows + rest.shape[0]
    head_width = width // HEADS
    size = HEADS * rows * key_count
    scalars = pl.BlockSpec(memory_space=pltpu.SMEM)
    return pl.pallas_call(
        partial(forward_kernel, head_width, 1.0 / math.sqrt(head_width), lengths.shape[0]),
        grid=(HEADS // 2,),
        in_specs=[scalars, scalars] + [whole(*item.shape) for item in (own, rest, valid, mod, weight)],
        out_specs=[
            pl.BlockSpec((2, key_count, rows), lambda p: (p, 0, 0)),
            whole(width, rows),
            whole(2 * width, key_count),
            whole(width, rows),
            pl.BlockSpec((2, 1, rows), lambda p: (p, 0, 0)),
            whole(rows, width),
        ],
        out_shape=[
            pltpu.HBM((HEADS, key_count, rows), bf16),
            jax.ShapeDtypeStruct((width, rows), bf16),
            jax.ShapeDtypeStruct((2 * width, key_count), bf16),
            jax.ShapeDtypeStruct((width, rows), f32),
            jax.ShapeDtypeStruct((HEADS, 1, rows), f32),
            jax.ShapeDtypeStruct((rows, width), bf16),
        ],
        scratch_shapes=[pltpu.VMEM((key_count, rows), f32)],
        compiler_params=kernel_params(22),
        cost_estimate=pl.CostEstimate(
            flops=16 * size * head_width, bytes_accessed=2 * size, transcendentals=size
        ),
        name="forward_attention",
    )(place, lengths, own, rest, valid, mod, weight)


def middle_kernel(
    place, own, attended, cotangent, mod, bias, output_weight, expand_weight, shrink_weight,
    keep, send, packed_output, grad_attended, grad_residual, sums, output,
):
    first_core = place[2] == 0
    rows, width = own.shape
    blocks = expand_weight.shape[1] // width
    row = lambda at: mod[at : at + 1, :]
    bias_row = lambda at: bias[:, at * width : (at + 1) * width]
    share = row(SHARE)
    scale_two = 1.0 + row(SCALE_TWO)
    branch_one = product(attended[...], output_weight[...]) + bias_row(6)
    residual = own[...].astype(f32) + row(GATE_ONE) * branch_one
    normed, inverse = normalize(residual)
    mixed = (normed * scale_two + row(SHIFT_TWO)).astype(bf16)
    wide = cotangent[...].astype(f32)
    grad_two = (wide * row(GATE_TWO)).astype(bf16)
    sums[...] = jnp.zeros_like(sums)
    hidden = product(mixed, expand_weight[...]) + bias[:, 7 * width : (7 + blocks) * width]
    square = hidden * hidden
    bent = jnp.tanh(GELU_RATE * hidden * (1.0 + GELU_CUBE * square))
    half = 0.5 + 0.5 * bent
    slope = half + 0.5 * hidden * (1.0 - bent * bent) * (
        GELU_RATE + (3.0 * GELU_CUBE * GELU_RATE) * square
    )
    active = (hidden * half).astype(bf16)
    branch_two = product(active, shrink_weight[...]) + bias_row(7 + blocks)
    grad_hidden = (back_product(grad_two, shrink_weight[...]) * slope).astype(bf16)
    grad_mixed = back_product(grad_hidden, expand_weight[...])
    hidden_sum = column_sum(grad_hidden.astype(f32))
    for block in range(blocks):
        part = slice(block * width, (block + 1) * width)
        grad_shrink = inner(active[:, part], grad_two) * share
        grad_expand = inner(mixed, grad_hidden[:, part]) * share
        keep[part, :] = jnp.where(first_core, grad_shrink, grad_expand).astype(bf16)
        send[part, :] = jnp.where(first_core, grad_expand, grad_shrink).astype(bf16)
        sums[7 + block : 8 + block, :] = hidden_sum[:, part] * share
    result = (residual + row(GATE_TWO) * branch_two).astype(bf16)
    owners, count = output.shape[:2]
    for step in range(owners):
        output[back(place[0], owners, step)] = result[step * count : (step + 1) * count, :]
    sums[5:6, :] = column_sum(wide * branch_two) * share
    sums[7 + blocks : 8 + blocks, :] = column_sum(grad_two.astype(f32)) * share
    sums[4:5, :] = column_sum(grad_mixed * normed) * share
    sums[3:4, :] = column_sum(grad_mixed) * share
    grad_wide = wide + normalize_back(grad_mixed * scale_two, normed, inverse)
    grad_residual[...] = grad_wide
    sums[2:3, :] = column_sum(grad_wide * branch_one) * share
    grad_one = (grad_wide * row(GATE_ONE)).astype(bf16)
    sums[6:7, :] = column_sum(grad_one.astype(f32)) * share
    packed_output[...] = (inner(attended[...], grad_one) * share).astype(bf16)
    grad_attended[...] = back_product(output_weight[...], grad_one).astype(bf16)


def middle(
    owners, place, own, attended, cotangent, mod, bias, output_weight, expand_weight, shrink_weight
):
    rows, width = own.shape
    hidden = expand_weight.shape[1]
    operands = (
        own, attended, cotangent, mod, bias, output_weight, expand_weight, shrink_weight
    )
    shapes = [
        jax.ShapeDtypeStruct((hidden, width), bf16),
        jax.ShapeDtypeStruct((hidden, width), bf16),
        pltpu.HBM((width, width), bf16),
        pltpu.HBM((width, rows), bf16),
        pltpu.HBM((rows, width), f32),
        jax.ShapeDtypeStruct((16, width), f32),
        jax.ShapeDtypeStruct((owners, rows // owners, width), bf16),
    ]
    return pl.pallas_call(
        middle_kernel,
        grid=(1,),
        in_specs=[pl.BlockSpec(memory_space=pltpu.SMEM)] + [whole(*item.shape) for item in operands],
        out_specs=[whole(*item.shape) for item in shapes],
        out_shape=shapes,
        compiler_params=kernel_params(20),
        cost_estimate=pl.CostEstimate(
            flops=16 * rows * width * hidden, bytes_accessed=2**24, transcendentals=rows * hidden
        ),
        name="middle",
    )(place, *operands)


def backward_kernel(
    head_width, score_scale, place, expo, query, key_value, attended_wide, inverse_total,
    grad_attended, own, rest, mod, weight, packed_output, grad_residual, sums_in, keep, send,
    rest_part, own_part, sums,
    grad_query, grad_key, grad_value,
):
    pair = pl.program_id(0)
    rows, width = own.shape
    grad_keys, grad_values = [], []
    for i in range(2):
        first = pl.multiple_of((2 * pair + i) * head_width, head_width)
        here = pl.ds(first, head_width)
        scaled = (query[here, :].astype(f32) * score_scale).astype(bf16)
        keys = key_value[here, :]
        values = key_value[pl.ds(pl.multiple_of(width + first, head_width), head_width), :]
        grads = (grad_attended[here, :].astype(f32) * inverse_total[i]).astype(bf16)
        delta = column_sum(grads.astype(f32) * attended_wide[here, :])
        low = expo[i]
        grad_scores = (low.astype(f32) * (inner(values, grads) - delta)).astype(bf16)
        grad_values.append(back_product(low, grads))
        grad_keys.append(back_product(grad_scores, scaled))
        grad_query[here, :] = (product(keys, grad_scores) * score_scale).astype(bf16)
    grad_key[pair] = jnp.concatenate(grad_keys, axis=1).astype(bf16)
    grad_value[pair] = jnp.concatenate(grad_values, axis=1).astype(bf16)

    @pl.when(pair == pl.num_programs(0) - 1)
    def _():
        row = lambda at: mod[at : at + 1, :]
        share = row(SHARE)
        shift, scale = row(SHIFT_ONE), 1.0 + row(SCALE_ONE)
        pairs = range(HEADS // 2)
        packed_key = jnp.zeros((width, width), f32)
        packed_value = jnp.zeros((width, width), f32)
        total_shift = jnp.zeros((1, width), f32)
        total_scale = jnp.zeros((1, width), f32)
        for at in range(0, rows + rest.shape[0], rows):
            here = slice(at, at + rows)
            source = own[...] if at == 0 else rest[at - rows : at, :]
            normed, inverse = normalize(source.astype(f32))
            mixed = (normed * scale + shift).astype(bf16)
            keys = jnp.concatenate([grad_key[pair, here, :] for pair in pairs], axis=1)
            values = jnp.concatenate([grad_value[pair, here, :] for pair in pairs], axis=1)
            part = product(keys, weight[width : 2 * width, :]) + product(
                values, weight[2 * width :, :]
            )
            if at == 0:
                part = part + inner(grad_query[...], weight[:width, :])
                back = normalize_back(part * scale, normed, inverse)
                own_part[...] = (grad_residual[...] + back).astype(bf16)
                packed_query = product(grad_query[...], mixed).T
            else:
                rest_part[at - rows : at, :] = part.astype(bf16)
            packed_key = packed_key + inner(mixed, keys)
            packed_value = packed_value + inner(mixed, values)
            total_shift = total_shift + column_sum(part)
            total_scale = total_scale + column_sum(part * normed)
        first_core = place[2] == 0
        packed = [packed_query * share, packed_key * share, packed_value * share, packed_output[...].astype(f32)]
        half = width // 2
        for at, matrix in enumerate(packed):
            here = slice(at * half, (at + 1) * half)
            keep[here, :] = jnp.where(first_core, matrix[:half], matrix[half:]).astype(bf16)
            send[here, :] = jnp.where(first_core, matrix[half:], matrix[:half]).astype(bf16)
        sums[...] = sums_in[...]
        sums[0:1, :] = total_shift * share
        sums[1:2, :] = total_scale * share
        rest_part[rest.shape[0] :, :] = sums[...].astype(bf16)


def backward_attention(
    place, saved, grad_attended, own, rest, mod, weight, packed_output, grad_residual, sums
):
    expo, query, key_value, attended_wide, inverse_total = saved
    rows, width = own.shape
    key_count = rows + rest.shape[0]
    head_width = width // HEADS
    size = HEADS * rows * key_count
    operands = (
        query, key_value, attended_wide, inverse_total, grad_attended, own, rest, mod, weight,
        packed_output, grad_residual, sums,
    )
    specs = [whole(*item.shape) for item in operands]
    specs[3] = pl.BlockSpec((2, 1, rows), lambda p: (p, 0, 0))
    shapes = [
        pltpu.HBM((2 * width, width), bf16),
        jax.ShapeDtypeStruct((2 * width, width), bf16),
        pltpu.HBM((rest.shape[0] + sums.shape[0], width), bf16),
        jax.ShapeDtypeStruct((rows, width), bf16),
        jax.ShapeDtypeStruct(sums.shape, f32),
    ]
    return pl.pallas_call(
        partial(backward_kernel, head_width, 1.0 / math.sqrt(head_width)),
        grid=(HEADS // 2,),
        in_specs=[
            pl.BlockSpec(memory_space=pltpu.SMEM),
            pl.BlockSpec((2, key_count, rows), lambda p: (p, 0, 0)),
        ]
        + specs,
        out_specs=[whole(*item.shape) for item in shapes],
        out_shape=shapes,
        scratch_shapes=[
            pltpu.VMEM((width, rows), bf16),
            pltpu.VMEM((HEADS // 2, key_count, 2 * head_width), bf16),
            pltpu.VMEM((HEADS // 2, key_count, 2 * head_width), bf16),
        ],
        compiler_params=kernel_params(16),
        cost_estimate=pl.CostEstimate(
            flops=32 * size * head_width, bytes_accessed=2 * size, transcendentals=0
        ),
        name="backward_attention",
    )(place, pltpu.with_memory_space_constraint(expo, pltpu.HBM), *operands)


def finish_kernel(owners, own, part, received, mod, *refs):
    parts, results = refs[:-owners], refs[-owners:]
    rows, width = own.shape
    count = rows // owners
    normed, inverse = normalize(own[...].astype(f32))
    grad = received[:rows, :].astype(f32) * (1.0 + mod[SCALE_ONE : SCALE_ONE + 1, :])
    grad = (part[...].astype(f32) + normalize_back(grad, normed, inverse)).astype(bf16)
    for step, result in enumerate(results):
        result[:count, :] = grad[step * count : (step + 1) * count, :]
    if parts:
        summed = total([ref[...] for ref in parts]).astype(bf16)
        for result in results:
            result[count:, :] = summed


def finish_rows(owners, own, part, received, mod, parts):
    operands = [own, part, received, mod] + parts
    shape = (own.shape[0] // owners + (parts[0].shape[0] if parts else 0), own.shape[1])
    return pl.pallas_call(
        partial(finish_kernel, owners),
        grid=(1,),
        in_specs=[whole(*item.shape) for item in operands],
        out_specs=[whole(*shape)] * owners,
        out_shape=[jax.ShapeDtypeStruct(shape, bf16)] * owners,
        compiler_params=kernel_params(12),
        name="finish_rows",
    )(*operands)


def pair_parts_kernel(grp_size, place, kept, received, *results):
    count = results[0].shape[0]
    for step, result in enumerate(results):
        here = pl.ds(pl.multiple_of(away(place[3], grp_size, step) * count, count), count)
        result[...] = total([kept[here, :], received[here, :]]).astype(bf16)


def pair_parts(place, kept, received):
    grp_size = lax.axis_size("grp")
    shape = (kept.shape[0] // grp_size, kept.shape[1])
    return pl.pallas_call(
        partial(pair_parts_kernel, grp_size),
        grid=(1,),
        in_specs=[pl.BlockSpec(memory_space=pltpu.SMEM)] + [whole(*kept.shape)] * 2,
        out_specs=[whole(*shape)] * grp_size,
        out_shape=[jax.ShapeDtypeStruct(shape, bf16)] * grp_size,
        compiler_params=kernel_params(12),
        name="pair_parts",
    )(place, kept, received)


def sum_parts_kernel(*refs):
    refs[-1][...] = total([ref[...] for ref in refs[:-1]]).astype(bf16)


def sum_parts(parts):
    return pl.pallas_call(
        sum_parts_kernel,
        grid=(1,),
        in_specs=[whole(*parts[0].shape)] * len(parts),
        out_specs=whole(*parts[0].shape),
        out_shape=jax.ShapeDtypeStruct(parts[0].shape, bf16),
        compiler_params=kernel_params(8),
        name="sum_parts",
    )(*parts)


def line_total_kernel(sums, received, *refs):
    parts, result = refs[:-1], refs[-1]
    count = parts[0].shape[-2]
    if len(parts[0].shape) == 3:
        parts = [parts[0].at[at] for at in range(parts[0].shape[0])]
    result[:count, :] = total([part[...] for part in parts]).astype(bf16)
    below = received[received.shape[0] - sums.shape[0] :, :].astype(f32)
    result[count:, :] = (sums[...] + below).astype(bf16)


def line_total(parts, sums, received):
    count, width = parts[0].shape[-2:]
    below = sums.shape[0]
    return pl.pallas_call(
        line_total_kernel,
        grid=(1,),
        in_specs=[whole(*item.shape) for item in [sums, received] + parts],
        out_specs=whole(count + below, width),
        out_shape=jax.ShapeDtypeStruct((count + below, width), bf16),
        compiler_params=kernel_params(4),
        name="line_total",
    )(sums, received, *parts)


def with_lead(below, lead, mod):
    row = lax.broadcasted_iota(jnp.int32, below.shape, 0)
    below = jnp.where(row == 12, mod[EMBEDDING : EMBEDDING + 1, :], below)
    return jnp.where(row == 13, jnp.full(below.shape, lead).astype(f32), below).astype(bf16)


def line_join_kernel(lead, mod, *refs):
    parts, result = refs[:-1], refs[-1]
    count = (result.shape[0] - 16) // len(parts)
    for at, part in enumerate(parts):
        result[at * count : (at + 1) * count, :] = part[:count, :]
    below = total([part[count:, :] for part in parts])
    result[len(parts) * count :, :] = with_lead(below, lead[0], mod)


def line_join(lead, mod, parts):
    rows, width = parts[0].shape
    shape = (len(parts) * (rows - 16) + 16, width)
    return pl.pallas_call(
        line_join_kernel,
        grid=(1,),
        in_specs=[pl.BlockSpec(memory_space=pltpu.SMEM)]
        + [whole(*item.shape) for item in [mod] + parts],
        out_specs=whole(*shape),
        out_shape=jax.ShapeDtypeStruct(shape, bf16),
        compiler_params=kernel_params(8),
        name="line_join",
    )(lead, mod, *parts)


def picked(place, grp_size, own, received, side, b, write):
    group = place[3]
    for step in range(grp_size):
        here = back(group, grp_size, b) == step
        for ref, mine in ((own[step], True), (received[step], False)):

            @pl.when(here & ((place[2] == side) == mine))
            def _():
                write(ref)


def copy_line(place, line, count, ref, output, first):
    for c in range(line):
        from_c = back(place[4], line, c) if line > 1 else 0
        here = pl.ds(pl.multiple_of(from_c * count, count), count) if line > 1 else slice(0, count)
        output[first + c * count : first + (c + 1) * count, :] = ref[here, :].astype(f32)


def first_sums_kernel(grp_size, line, place, *refs):
    own, received = refs[:grp_size], refs[grp_size : 2 * grp_size]
    refs = refs[2 * grp_size :]
    weight, output = refs[:2]
    owners = len(refs) - 14
    pieces, refs = refs[2 : 2 + owners], refs[2 + owners :]
    shrink, expand, grad_weight, copied, rows, table, grad_bias = refs[:7]
    output_bias, expand_bias, shrink_bias, grad_lifted, sums = refs[7:]
    b = pl.program_id(0)
    width = table.shape[1]
    count = own[0].shape[0] - 16
    copied[...] = output[...]
    for step, piece in enumerate(pieces):

        @pl.when(back(place[0], owners, step) == b)
        def _():
            rows[0] = piece[: rows.shape[1], :].astype(f32)

    for side, target in enumerate((shrink, expand)):
        write = lambda ref: copy_line(place, line, count // line, ref, target, 0)
        picked(place, grp_size, own, received, side, b, write)

    parts = [part[count:, :].astype(f32) for part in own]
    pad = jnp.zeros((8 - grp_size, width), f32)
    stacked = jnp.concatenate([part[12:13] for part in parts] + [pad])
    gate = 1.0 / (1.0 + jnp.exp(-stacked))

    @pl.when(b == 0)
    def _():
        sums[...] = total(parts)
        grad_lifted[...] = jnp.zeros_like(grad_lifted)

    @pl.when(b < 3)
    def _():
        lifted = (stacked * gate).astype(bf16)
        line_of = lax.broadcasted_iota(jnp.int32, parts[0].shape, 0)
        for i in range(2):
            here = slice(i * width, (i + 1) * width)
            picks = [column_sum(jnp.where(line_of == 2 * b + i, part, 0.0)) for part in parts]
            picks = jnp.concatenate(picks + [pad]).astype(bf16)
            grad_weight[:, here] = inner(lifted, picks)
            grad_lifted[...] += back_product(picks, weight[:, here])

    @pl.when(b == pl.num_programs(0) - 1)
    def _():
        for at in range(6):
            grad_bias[at * width : (at + 1) * width] = sums[at]
        output_bias[...] = sums[6]
        for at in range(expand_bias.shape[0] // width):
            expand_bias[at * width : (at + 1) * width] = sums[7 + at]
        shrink_bias[...] = sums[7 + expand_bias.shape[0] // width]
        grad_embedding = grad_lifted[...] * gate * (1.0 + stacked * (1.0 - gate))
        lead = lax.broadcasted_iota(jnp.int32, (LEADS, width), 0).astype(f32)
        table[...] = total(
            [
                jnp.where(lead == part[13:14], grad_embedding[p : p + 1], 0.0)
                for p, part in enumerate(parts)
            ]
        )


def first_sums(place, own, weight, output, pieces):
    grp_size = len(own)
    line = 1 if line_size() > 4 else line_size()
    received = [swap_cores(part) for part in own]
    width = weight.shape[0]
    hidden = grp_size * width
    block = pl.BlockSpec((1,) + output.shape[1:], lambda b: (b, 0, 0))
    wide = pl.BlockSpec((width, 2 * width), lambda b: (0, jnp.minimum(b, 2)))
    return pl.pallas_call(
        partial(first_sums_kernel, grp_size, line),
        grid=(grp_size,),
        in_specs=[pl.BlockSpec(memory_space=pltpu.SMEM)]
        + [whole(*own[0].shape)] * (2 * grp_size)
        + [wide, block]
        + [whole(*item.shape) for item in pieces],
        out_specs=[
            pl.BlockSpec((width, width), lambda b: (b, 0)),
            pl.BlockSpec((width, width), lambda b: (0, b)),
            wide,
            block,
            block,
            whole(LEADS, width),
            whole(6 * width),
            whole(width),
            whole(hidden),
            whole(width),
        ],
        out_shape=[
            jax.ShapeDtypeStruct((hidden, width), f32),
            jax.ShapeDtypeStruct((width, hidden), f32),
            jax.ShapeDtypeStruct(weight.shape, f32),
            jax.ShapeDtypeStruct(output.shape, output.dtype),
            jax.ShapeDtypeStruct(output.shape, f32),
            jax.ShapeDtypeStruct((LEADS, width), f32),
            jax.ShapeDtypeStruct((6 * width,), f32),
            jax.ShapeDtypeStruct((width,), f32),
            jax.ShapeDtypeStruct((hidden,), f32),
            jax.ShapeDtypeStruct((width,), f32),
        ],
        scratch_shapes=[pltpu.VMEM((8, width), f32), pltpu.VMEM((16, width), f32)],
        compiler_params=kernel_params(16),
        name="first_sums",
    )(place, *own, *received, weight, output, *pieces)


def second_sums_kernel(grp_size, line, place, *refs):
    own, received = refs[:grp_size], refs[grp_size : 2 * grp_size]
    attend, output = refs[2 * grp_size :]
    width = output.shape[0]
    half = width // 2
    for group in range(grp_size):
        for core in range(2):

            @pl.when((place[3] == group) & (place[2] == core))
            def _():
                for b in range(grp_size):
                    step = back(group, grp_size, b)
                    for side, parts in ((core, own), (1 - core, received)):
                        if b < grp_size - 1:
                            target = attend.at[:, b * width : (b + 1) * width]
                        else:
                            target = output
                        copy_line(place, line, half // line, parts[step], target, side * half)


def second_sums(place, own):
    grp_size, width = len(own), own[0].shape[1]
    line = 1 if line_size() > 4 else line_size()
    received = [swap_cores(part) for part in own]
    shapes = [(width, (grp_size - 1) * width), (width, width)]
    return pl.pallas_call(
        partial(second_sums_kernel, grp_size, line),
        grid=(1,),
        in_specs=[pl.BlockSpec(memory_space=pltpu.SMEM)] + [whole(*own[0].shape)] * (2 * grp_size),
        out_specs=[whole(*shape) for shape in shapes],
        out_shape=[jax.ShapeDtypeStruct(shape, f32) for shape in shapes],
        compiler_params=kernel_params(16),
        name="second_sums",
    )(place, *own, *received)


def long_forward(owner, rank, share, lengths, valid, own, rest, mod, weight):
    rows, width = own.shape
    owners = lengths.shape[0]
    count = rows // owners
    steps = jnp.arange(owners, dtype=jnp.int32)
    ranks = (rank + jnp.arange(share, dtype=jnp.int32)) % share
    blocks = (back(owner, owners, steps)[None, :] * share + ranks[:, None]).reshape(-1, 1)
    key_pos = blocks * count + jnp.arange(count, dtype=jnp.int32)[None, :]
    doc_ends = jnp.cumsum(lax.dynamic_index_in_dim(lengths, owner, 0, False))
    key_seg = sum((key_pos >= doc_ends[doc]).astype(jnp.int32) for doc in range(doc_ends.shape[0]))
    own_valid = lax.dynamic_index_in_dim(valid, owner, 0, False).reshape(-1, count)
    key_valid = own_valid[blocks[:, 0]] > 0
    open_seg = jnp.where(key_valid, key_seg, -1).reshape(1, -1)
    key_pos = key_pos.reshape(1, -1)
    query_seg = key_seg.reshape(-1, 1)[:rows]
    query_pos = key_pos.reshape(-1, 1)[:rows]
    head_width = width // HEADS
    normed = normalize(jnp.concatenate([own, rest], axis=0).astype(f32))[0]
    mixed = (normed * (1.0 + mod[SCALE_ONE]) + mod[SHIFT_ONE]).astype(bf16)
    heads = lambda v: v.reshape(v.shape[0], HEADS, head_width).transpose(1, 0, 2)
    queries = heads(back_product(mixed[:rows], weight[:width]).astype(bf16))
    key_value = back_product(mixed, weight[width:]).astype(bf16)
    keys = heads(key_value[:, :width])
    values = heads(key_value[:, width:])
    probs, attended = attention(
        queries, keys, values, query_seg, query_pos, open_seg, key_pos, 1.0 / math.sqrt(head_width)
    )
    flat = attended.transpose(1, 0, 2).reshape(rows, width).astype(bf16)
    return ((probs, queries, keys, values, attended, normed, mixed), flat)


def long_backward(
    place, saved, grad_attended, own, rest, mod, weight, packed_output, grad_residual, sums
):
    probs, queries, keys, values, attended, normed, mixed = saved
    rows, width = own.shape
    head_width = width // HEADS
    score_scale = 1.0 / math.sqrt(head_width)
    grad_heads = grad_attended.reshape(HEADS, head_width, rows).transpose(0, 2, 1)
    deltas = jnp.sum(grad_heads.astype(f32) * attended, axis=-1, keepdims=True)
    grad_probs = jnp.einsum("hqd,hkd->hqk", grad_heads, values, preferred_element_type=f32)
    grad_scores = (probs.astype(f32) * (grad_probs - deltas)).astype(bf16)
    grad_query = jnp.einsum("hqk,hkd->hqd", grad_scores, keys, preferred_element_type=f32)
    grad_key = jnp.einsum("hqk,hqd->hkd", grad_scores, queries, preferred_element_type=f32)
    grad_value = jnp.einsum("hqk,hqd->hkd", probs, grad_heads, preferred_element_type=f32)
    flat = lambda v: v.transpose(1, 0, 2).reshape(v.shape[1], width)
    grad_query = (flat(grad_query) * score_scale).astype(bf16)
    grad_key = (flat(grad_key) * score_scale).astype(bf16)
    grad_value = flat(grad_value).astype(bf16)
    part = product(grad_key, weight[width : 2 * width]) + product(grad_value, weight[2 * width :])
    part = jnp.concatenate([part[:rows] + product(grad_query, weight[:width]), part[rows:]], axis=0)
    share = mod[SHARE]
    packed = [row_product(mixed[:rows], grad_query), row_product(mixed, grad_key), row_product(mixed, grad_value)]
    packed = [(matrix * share).astype(bf16) for matrix in packed] + [packed_output]
    half = width // 2
    top = jnp.concatenate([matrix[:half] for matrix in packed])
    bottom = jnp.concatenate([matrix[half:] for matrix in packed])
    first_core = place[2] == 0
    keep = jnp.where(first_core, top, bottom)
    send = jnp.where(first_core, bottom, top)
    total_rows = jnp.stack([jnp.sum(part, axis=0), jnp.sum(part * normed, axis=0)]) * share
    sums = jnp.concatenate([total_rows, sums[2:]], axis=0)
    normed, inverse = normalize(own.astype(f32))
    own_part = grad_residual + normalize_back(part[:rows] * (1.0 + mod[SCALE_ONE]), normed, inverse)
    return (keep, send, part[rows:].astype(bf16), own_part.astype(bf16), sums)


def on_device(
    tokens,
    cotangent,
    lengths,
    valid_mask,
    lead_index,
    sample_counts,
    lead_table,
    modulation_weight,
    modulation_bias,
    attend_weight,
    output_weight,
    output_bias,
    expand_weight,
    expand_bias,
    shrink_weight,
    shrink_bias,
):
    owners = tokens.shape[1]
    block_rows = tokens.shape[2]
    width = tokens.shape[3]
    hidden_width = expand_bias.shape[0]
    seq_size = lax.axis_size("seq")
    share = seq_size // owners
    seq_length = block_rows * seq_size
    rows = owners * block_rows
    place = lax.axis_index("seq")
    owner = place // share
    rank = place % share

    where = jnp.stack([owner, rank, place % 2, lax.axis_index("grp"), place // 2]).astype(jnp.int32)

    token_pieces = rows_to_owner(tokens[0], owner, share)

    bias = [modulation_bias, output_bias, expand_bias, shrink_bias]
    bias = after(jnp.concatenate(bias).astype(f32))[None]
    mod, weight = prepare(
        where, lead_index, sample_counts, lead_table, modulation_weight, bias, attend_weight,
        owners * seq_length,
    )
    grad_pieces = rows_to_owner(cotangent[0], owner, share, {step: bias if step in (1,) else mod for step in range(1, owners)})
    token_pieces = after_all(token_pieces, mod, grad_pieces[1])
    own_tokens = jnp.concatenate(token_pieces, axis=0)
    rest_tokens = share_rows(own_tokens, rank, share)
    short = seq_length <= 2048
    if short:
        *saved, attended = forward_attention(
            where, lengths[0], valid_mask[0], own_tokens, rest_tokens, mod, weight
        )
    else:
        saved, attended = long_forward(
            owner, rank, share, lengths[0], valid_mask[0], own_tokens, rest_tokens, mod, weight
        )
    grad_out = jnp.concatenate(after_all(grad_pieces, attended), axis=0)
    ff_keep, ff_send, packed_output, grad_attended, grad_residual, sums, output = middle(
        owners, where, own_tokens, attended, grad_out, mod, bias, output_weight, expand_weight,
        shrink_weight,
    )
    output = rows_from_owner(output, share)
    ff_core = low_total([ff_keep, swap_cores(ff_send)])
    ff_parts = send_plane(plane_parts(ff_core))
    grad_attended = after(grad_attended, ff_core)
    backward = backward_attention if short else long_backward
    held = backward(
        where, saved, grad_attended, own_tokens, rest_tokens, mod, weight, packed_output,
        grad_residual, sums,
    )
    at_keep, at_send, rest_part, own_part, sums = after_all(held, *ff_parts[1:], output)
    ff_plane = sum_parts(ff_parts)
    line = line_size() <= 4
    if line:
        ff_parts = [line_exchange(ff_plane.reshape(line_size(), -1, width))]
    at_core = low_total([at_keep, swap_cores(at_send)])
    if share == 2:
        received = swap_cores(rest_part)
    else:
        received = return_rows(rest_part, rank, share)
    at_slices = plane_parts(at_core)
    at_parts = send_plane(at_slices)
    if line:
        ff_parts = list(after_all(ff_parts, *at_slices))
        ff_line = line_total(ff_parts, sums, received)
        at_parts = after_all(at_parts, ff_line)
    at_plane = low_total(at_parts)
    if line:
        ff_pieces = send_line([ff_line] * line_size())
        ff_plane = line_join(lead_index, mod, ff_pieces)
        at_line = send_line(line_parts(at_plane))
    else:
        vector = with_lead(lax.psum(sums, "seq"), lead_index[0], mod)
        ff_pieces = [sum_line(ff_plane)]
        ff_plane = jnp.concatenate(ff_pieces + [vector])
        at_line = []
    pieces = finish_rows(owners, own_tokens, own_part, received, mod, at_line)
    pieces = pieces_from_owner(pieces, share)
    at_pieces = [piece[block_rows:] for piece in pieces] if line else [sum_line(at_plane)]
    ff_parts = gather_plane(ff_plane)
    at_parts = gather_plane(jnp.concatenate(at_pieces))
    ff_parts = list(after_all(ff_parts, *pieces))
    grad_shrink, grad_expand, grad_mod_weight, output, grad_tokens, grad_table, grad_mod_bias, *biases = (
        first_sums(where, ff_parts, modulation_weight, output, pieces)
    )
    at_parts = list(after_all(at_parts, grad_shrink))
    grad_attend, grad_output = second_sums(where, at_parts)
    return (
        output[None],
        grad_tokens[None],
        grad_table,
        grad_mod_weight,
        grad_mod_bias,
        grad_attend,
        grad_output,
        biases[0],
        grad_expand,
        biases[1],
        grad_shrink,
        biases[2],
    )


def solution(mesh):
    rows = P("grp", None, "seq", None)
    placed = (rows, rows, P("grp", None, None), P("grp", None, None), P("grp")) + (P(),) * 11
    return jax.shard_map(
        on_device,
        mesh=mesh,
        in_specs=placed,
        out_specs=(rows, rows) + (P(),) * 10,
        check_vma=False,
    )
```

```python
from functools import partial
import math

import jax
import jax.numpy as jnp
from jax import lax
from jax.experimental import pallas as pl
from jax.experimental.pallas import tpu as pltpu
from jax.sharding import PartitionSpec as P

HEADS = 6
LEADS = 8

EPSILON = 1e-06
MASKED = -1e30

bf16 = jnp.bfloat16
f32 = jnp.float32


def normalize(values):
    centred = values - jnp.mean(values, axis=-1, keepdims=True)
    inverse = lax.rsqrt(jnp.mean(centred * centred, axis=-1, keepdims=True) + EPSILON)
    return (centred * inverse, inverse)


def normalize_back(grad, normed, inverse):
    return inverse * (
        grad
        - jnp.mean(grad, axis=-1, keepdims=True)
        - normed * jnp.mean(grad * normed, axis=-1, keepdims=True)
    )


def row_product(left, right):
    return lax.dot_general(left, right, (((0,), (0,)), ((), ())), preferred_element_type=f32)


def back_product(grad, weight):
    return lax.dot_general(grad, weight, (((1,), (1,)), ((), ())), preferred_element_type=f32)


def product(left, right):
    return jnp.dot(left, right, preferred_element_type=f32)


def total(parts):
    result = parts[0].astype(f32)
    for part in parts[1:]:
        result = result + part.astype(f32)
    return result


def away(index, size, step):
    return index ^ step if size & (size - 1) == 0 else (index + step) % size


def back(index, size, step):
    return index ^ step if size & (size - 1) == 0 else (index - step) % size


def owner_pairs(seq_size, owners, share, step):
    return [(d, away(d // share, owners, step) * share + d % share) for d in range(seq_size)]


def rows_to_owner(blocks, owner, share, earlier=None):
    owners = blocks.shape[0]
    seq_size = lax.axis_size("seq")
    pieces = []
    for step in range(owners):
        block = lax.dynamic_index_in_dim(blocks, away(owner, owners, step), 0, False)
        if step and earlier:
            block = after(block, earlier[step])
        if step:
            block = lax.ppermute(block, "seq", owner_pairs(seq_size, owners, share, step))
        pieces.append(block)
    return pieces


def pieces_from_owner(pieces, share):
    owners, seq_size = len(pieces), lax.axis_size("seq")
    return [pieces[0]] + [
        lax.ppermute(pieces[step], "seq", owner_pairs(seq_size, owners, share, step))
        for step in range(1, owners)
    ]


def rows_from_owner(blocks, share):
    owners = blocks.shape[0]
    groups = [[owner * share + rank for owner in range(owners)] for rank in range(share)]
    return lax.all_to_all(blocks, "seq", 0, 0, axis_index_groups=groups)


def share_rows(rows, rank, share):
    seq_size = lax.axis_size("seq")
    if share == 2:
        return lax.ppermute(rows, "seq", [(d, d ^ 1) for d in range(seq_size)])
    groups = [list(range(first, first + share)) for first in range(0, seq_size, share)]
    gathered = lax.all_gather(rows, "seq", axis_index_groups=groups)
    gathered = jnp.roll(gathered, -rank, axis=0)[1:]
    return gathered.reshape((share - 1) * rows.shape[0], rows.shape[1])


def return_rows(rest, rank, share):
    seq_size = lax.axis_size("seq")
    if share == 2:
        return lax.ppermute(rest, "seq", [(d, d ^ 1) for d in range(seq_size)])
    groups = [list(range(first, first + share)) for first in range(0, seq_size, share)]
    parts = rest.reshape(share - 1, rest.shape[0] // (share - 1), rest.shape[1])
    parts = jnp.concatenate([jnp.zeros_like(parts[:1]), parts], axis=0)
    parts = jnp.roll(parts, rank, axis=0)
    return lax.psum_scatter(parts, "seq", scatter_dimension=0, axis_index_groups=groups)


def swap_cores(values):
    seq_size = lax.axis_size("seq")
    return lax.ppermute(values, "seq", [(d, d ^ 1) for d in range(seq_size)])


def line_size():
    return lax.axis_size("seq") // 2


def line_send(values, step):
    seq_size = lax.axis_size("seq")
    return lax.ppermute(values, "seq", owner_pairs(seq_size, seq_size // 2, 2, step))


def plane_send(values, step):
    grp_size = lax.axis_size("grp")
    return lax.ppermute(values, "grp", [(d, away(d, grp_size, step)) for d in range(grp_size)])


def rows_at(values, at, count):
    return lax.dynamic_slice_in_dim(values, at * count, count, 0)


def plane_steps():
    return range(1, lax.axis_size("grp"))


def plane_parts(values):
    grp_size = lax.axis_size("grp")
    group = lax.axis_index("grp")
    count = values.shape[0] // grp_size
    return [rows_at(values, away(group, grp_size, step), count) for step in range(grp_size)]


def send_plane(parts):
    return [parts[0]] + [plane_send(parts[step], step) for step in plane_steps()]


def gather_plane(values):
    return [values] + [plane_send(values, step) for step in plane_steps()]


def line_parts(values):
    length = line_size()
    place = lax.axis_index("seq") // 2
    count = values.shape[0] // length
    return [rows_at(values, away(place, length, step), count) for step in range(length)]


def send_line(parts):
    return [parts[0]] + [line_send(parts[step], step) for step in range(1, len(parts))]


def line_exchange(values):
    length = line_size()
    groups = [list(range(core, 2 * length, 2)) for core in range(2)]
    return lax.all_to_all(values, "seq", 0, 0, axis_index_groups=groups)


def sum_line(values):
    length = line_size()
    groups = [list(range(core, 2 * length, 2)) for core in range(2)]
    return lax.psum(values, "seq", axis_index_groups=groups)


def low_total(parts):
    return total(parts).astype(bf16)


def after(values, *others):
    return lax.optimization_barrier((values,) + others)[0]


def columns(values, width):
    return [values[:, at : at + width] for at in range(0, values.shape[1], width)]


def sum_share(values, share):
    seq_size = lax.axis_size("seq")
    groups = [list(range(first, first + share)) for first in range(0, seq_size, share)]
    return lax.psum(values, "seq", axis_index_groups=groups)


def after_all(values, *others):
    return lax.optimization_barrier(tuple(values) + others)[: len(values)]


def attention_kernel(
    score_scale, query, key, value, query_seg, query_pos, open_seg, key_pos, probs, attended, bias
):
    @pl.when(pl.program_id(1) == 0)
    def _():
        allow = (query_seg[...] == open_seg[...]) | (query_pos[...] == key_pos[...])
        bias[...] = jnp.where(allow, 0.0, MASKED)

    scaled = (query[0].astype(f32) * score_scale).astype(bf16)
    scores = back_product(scaled, key[0]) + bias[...]
    expo = jnp.exp(scores - jnp.max(scores, axis=1, keepdims=True))
    low = (expo * (1.0 / jnp.sum(expo, axis=1, keepdims=True))).astype(bf16)
    probs[0] = low
    attended[0] = product(low, value[0])


def attention(queries, keys, values, query_seg, query_pos, open_seg, key_pos, score_scale):
    head_count, rows, head_width = queries.shape
    key_count = keys.shape[1]
    step = max(32, min(rows, 2**18 // key_count))
    row_block = lambda i, h: (h, i, 0)
    key_block = lambda i, h: (h, 0, 0)
    size = head_count * rows * key_count
    return pl.pallas_call(
        partial(attention_kernel, score_scale),
        grid=(rows // step, head_count),
        in_specs=[
            pl.BlockSpec((1, step, head_width), row_block),
            pl.BlockSpec((1, key_count, head_width), key_block),
            pl.BlockSpec((1, key_count, head_width), key_block),
            pl.BlockSpec((step, 1), lambda i, h: (i, 0)),
            pl.BlockSpec((step, 1), lambda i, h: (i, 0)),
            pl.BlockSpec((1, key_count), lambda i, h: (0, 0)),
            pl.BlockSpec((1, key_count), lambda i, h: (0, 0)),
        ],
        out_specs=[
            pl.BlockSpec((1, step, key_count), row_block),
            pl.BlockSpec((1, step, head_width), row_block),
        ],
        out_shape=[
            jax.ShapeDtypeStruct((head_count, rows, key_count), bf16),
            jax.ShapeDtypeStruct((head_count, rows, head_width), f32),
        ],
        scratch_shapes=[pltpu.VMEM((step, key_count), f32)],
        compiler_params=pltpu.CompilerParams(vmem_limit_bytes=40 * 2**20),
        cost_estimate=pl.CostEstimate(
            flops=4 * size * head_width, bytes_accessed=2 * size, transcendentals=size
        ),
        name="attention",
    )(queries, keys, values, query_seg, query_pos, open_seg, key_pos)


GELU_RATE = math.sqrt(2.0 / math.pi)
GELU_CUBE = 0.044715
SHIFT_ONE, SCALE_ONE, GATE_ONE, SHIFT_TWO, SCALE_TWO, GATE_TWO, SHARE, EMBEDDING = range(8)


def inner(left, right):
    return row_product(left, right)


def column_sum(values):
    return jnp.sum(values, axis=0, keepdims=True)


def whole(*shape):
    return pl.BlockSpec(shape, lambda *_: (0,) * len(shape))


def kernel_params(mebibytes):
    return pltpu.CompilerParams(vmem_limit_bytes=mebibytes * 2**20)


def prepare_kernel(factor, place, lead, counts, table, weight, bias, attend_weight, mod, turned):
    width = table.shape[1]
    here = lax.broadcasted_iota(jnp.int32, table.shape, 0) == lead[0]
    embedding = column_sum(jnp.where(here, table[...].astype(f32), 0.0))
    lifted = (embedding / (1.0 + jnp.exp(-embedding))).astype(bf16)
    modulation = product(lifted, weight[...]) + bias[:, : weight.shape[1]]
    for part in range(6):
        mod[part : part + 1, :] = modulation[:, part * width : (part + 1) * width]
    every, mine = 0, 0
    for group in range(counts.shape[0]):
        every = every + counts[group]
        mine = mine + jnp.where(place[3] == group, counts[group], 0)
    row = jnp.zeros((1, width), jnp.int32)
    mod[SHARE : SHARE + 1, :] = (row + mine).astype(f32) / (row + every).astype(f32) * factor
    mod[EMBEDDING : EMBEDDING + 1, :] = embedding
    turned[...] = attend_weight[...].T


def prepare(place, lead, counts, table, weight, bias, attend_weight, positions):
    width = table.shape[1]
    operands = (table, weight, bias, attend_weight)
    shapes = [
        jax.ShapeDtypeStruct((8, width), f32),
        jax.ShapeDtypeStruct(attend_weight.shape[::-1], bf16),
    ]
    return pl.pallas_call(
        partial(prepare_kernel, counts.shape[0] / math.sqrt(positions)),
        grid=(1,),
        in_specs=[pl.BlockSpec(memory_space=pltpu.SMEM)] * 3 + [whole(*item.shape) for item in operands],
        out_specs=[whole(*item.shape) for item in shapes],
        out_shape=shapes,
        compiler_params=kernel_params(8),
        name="prepare",
    )(place, lead, counts, *operands)


def forward_kernel(
    head_width, score_scale, owners, place, lengths, own, rest, valid, mod, weight,
    expo, query, key_value, attended_wide, inverse_total, attended, bias,
):
    pair = pl.program_id(0)
    rows, width = own.shape
    key_count = rows + rest.shape[0]

    @pl.when(pair == 0)
    def _():
        shift, scale = mod[SHIFT_ONE : SHIFT_ONE + 1, :], 1.0 + mod[SCALE_ONE : SCALE_ONE + 1, :]
        first = (normalize(own[...].astype(f32))[0] * scale + shift).astype(bf16)
        query[...] = back_product(weight[:width, :], first).astype(bf16)
        key_value[:, :rows] = back_product(weight[width:, :], first).astype(bf16)
        for at in range(0, rest.shape[0], rows):
            part = normalize(rest[at : at + rows, :].astype(f32))[0]
            part = (part * scale + shift).astype(bf16)
            key_value[:, rows + at : 2 * rows + at] = back_product(weight[width:, :], part).astype(bf16)

        owner, rank = place[0], place[1]
        share = key_count // rows
        count = rows // owners
        ends = []
        for doc in range(lengths.shape[1]):
            ends.append(lengths[owner, doc] + (ends[-1] if doc else 0))

        def segment(positions):
            return sum((positions >= end).astype(jnp.int32) for end in ends)

        def block_at(r, step):
            return back(owner, owners, step) * share + lax.rem(rank + r, share)

        lane = lax.broadcasted_iota(jnp.int32, (1, count), 1)
        query_pos = jnp.concatenate(
            [block_at(0, step) * count + lane for step in range(owners)], axis=1
        )
        query_seg = segment(query_pos)
        down = lax.broadcasted_iota(jnp.int32, (count, 1), 0)
        mine = lax.broadcasted_iota(jnp.int32, (owners, count), 0) == owner
        for r in range(share):
            for step in range(owners):
                block = block_at(r, step)
                key_pos = block * count + down
                open_rows = valid[:, pl.ds(pl.multiple_of(block * count, count), count)]
                open_rows = jnp.where((open_rows > 0) & mine, 1.0, 0.0)
                open_row = jnp.broadcast_to(column_sum(open_rows), (count, count))
                open_key = open_row.T[:, :1] > 0.5
                open_seg = jnp.where(open_key, segment(key_pos), -1)
                allow = (query_seg == open_seg) | (query_pos == key_pos)
                at = (r * owners + step) * count
                bias[at : at + count, :] = jnp.where(allow, 0.0, MASKED)

    heads = [pl.multiple_of((2 * pair + i) * head_width, head_width) for i in range(2)]
    scores = []
    for first in heads:
        here = pl.ds(first, head_width)
        scaled = (query[here, :].astype(f32) * score_scale).astype(bf16)
        scores.append(inner(key_value[here, :], scaled) + bias[...])
    for i, first in enumerate(heads):
        wide = jnp.exp(scores[i] - jnp.max(scores[i], axis=0, keepdims=True))
        inverse = 1.0 / column_sum(wide)
        low = wide.astype(bf16)
        expo[i] = low
        inverse_total[i] = inverse
        values = key_value[pl.ds(pl.multiple_of(width + first, head_width), head_width), :]
        attended_wide[pl.ds(first, head_width), :] = product(values, low) * inverse

    @pl.when(pair == pl.num_programs(0) - 1)
    def _():
        attended[...] = attended_wide[...].T.astype(bf16)


def forward_attention(place, lengths, valid, own, rest, mod, weight):
    rows, width = own.shape
    key_count = rows + rest.shape[0]
    head_width = width // HEADS
    size = HEADS * rows * key_count
    scalars = pl.BlockSpec(memory_space=pltpu.SMEM)
    return pl.pallas_call(
        partial(forward_kernel, head_width, 1.0 / math.sqrt(head_width), lengths.shape[0]),
        grid=(HEADS // 2,),
        in_specs=[scalars, scalars] + [whole(*item.shape) for item in (own, rest, valid, mod, weight)],
        out_specs=[
            pl.BlockSpec((2, key_count, rows), lambda p: (p, 0, 0)),
            whole(width, rows),
            whole(2 * width, key_count),
            whole(width, rows),
            pl.BlockSpec((2, 1, rows), lambda p: (p, 0, 0)),
            whole(rows, width),
        ],
        out_shape=[
            pltpu.HBM((HEADS, key_count, rows), bf16),
            jax.ShapeDtypeStruct((width, rows), bf16),
            jax.ShapeDtypeStruct((2 * width, key_count), bf16),
            jax.ShapeDtypeStruct((width, rows), f32),
            jax.ShapeDtypeStruct((HEADS, 1, rows), f32),
            jax.ShapeDtypeStruct((rows, width), bf16),
        ],
        scratch_shapes=[pltpu.VMEM((key_count, rows), f32)],
        compiler_params=kernel_params(22),
        cost_estimate=pl.CostEstimate(
            flops=16 * size * head_width, bytes_accessed=2 * size, transcendentals=size
        ),
        name="forward_attention",
    )(place, lengths, own, rest, valid, mod, weight)


def middle_kernel(
    place, own, attended, cotangent, mod, bias, output_weight, expand_weight, shrink_weight,
    keep, send, packed_output, grad_attended, grad_residual, sums, output,
):
    first_core = place[2] == 0
    rows, width = own.shape
    blocks = expand_weight.shape[1] // width
    row = lambda at: mod[at : at + 1, :]
    bias_row = lambda at: bias[:, at * width : (at + 1) * width]
    share = row(SHARE)
    scale_two = 1.0 + row(SCALE_TWO)
    branch_one = product(attended[...], output_weight[...]) + bias_row(6)
    residual = own[...].astype(f32) + row(GATE_ONE) * branch_one
    normed, inverse = normalize(residual)
    mixed = (normed * scale_two + row(SHIFT_TWO)).astype(bf16)
    wide = cotangent[...].astype(f32)
    grad_two = (wide * row(GATE_TWO)).astype(bf16)
    sums[...] = jnp.zeros_like(sums)
    hidden = product(mixed, expand_weight[...]) + bias[:, 7 * width : (7 + blocks) * width]
    square = hidden * hidden
    bent = jnp.tanh(GELU_RATE * hidden * (1.0 + GELU_CUBE * square))
    half = 0.5 + 0.5 * bent
    slope = half + 0.5 * hidden * (1.0 - bent * bent) * (
        GELU_RATE + (3.0 * GELU_CUBE * GELU_RATE) * square
    )
    active = (hidden * half).astype(bf16)
    branch_two = product(active, shrink_weight[...]) + bias_row(7 + blocks)
    grad_hidden = (back_product(grad_two, shrink_weight[...]) * slope).astype(bf16)
    grad_mixed = back_product(grad_hidden, expand_weight[...])
    hidden_sum = column_sum(grad_hidden.astype(f32))
    for block in range(blocks):
        part = slice(block * width, (block + 1) * width)
        grad_shrink = inner(active[:, part], grad_two) * share
        grad_expand = inner(mixed, grad_hidden[:, part]) * share
        keep[part, :] = jnp.where(first_core, grad_shrink, grad_expand).astype(bf16)
        send[part, :] = jnp.where(first_core, grad_expand, grad_shrink).astype(bf16)
        sums[7 + block : 8 + block, :] = hidden_sum[:, part] * share
    result = (residual + row(GATE_TWO) * branch_two).astype(bf16)
    owners, count = output.shape[:2]
    for step in range(owners):
        output[back(place[0], owners, step)] = result[step * count : (step + 1) * count, :]
    sums[5:6, :] = column_sum(wide * branch_two) * share
    sums[7 + blocks : 8 + blocks, :] = column_sum(grad_two.astype(f32)) * share
    sums[4:5, :] = column_sum(grad_mixed * normed) * share
    sums[3:4, :] = column_sum(grad_mixed) * share
    grad_wide = wide + normalize_back(grad_mixed * scale_two, normed, inverse)
    grad_residual[...] = grad_wide
    sums[2:3, :] = column_sum(grad_wide * branch_one) * share
    grad_one = (grad_wide * row(GATE_ONE)).astype(bf16)
    sums[6:7, :] = column_sum(grad_one.astype(f32)) * share
    packed_output[...] = (inner(attended[...], grad_one) * share).astype(bf16)
    grad_attended[...] = back_product(output_weight[...], grad_one).astype(bf16)


def middle(
    owners, place, own, attended, cotangent, mod, bias, output_weight, expand_weight, shrink_weight
):
    rows, width = own.shape
    hidden = expand_weight.shape[1]
    operands = (
        own, attended, cotangent, mod, bias, output_weight, expand_weight, shrink_weight
    )
    shapes = [
        jax.ShapeDtypeStruct((hidden, width), bf16),
        jax.ShapeDtypeStruct((hidden, width), bf16),
        pltpu.HBM((width, width), bf16),
        pltpu.HBM((width, rows), bf16),
        pltpu.HBM((rows, width), f32),
        jax.ShapeDtypeStruct((16, width), f32),
        jax.ShapeDtypeStruct((owners, rows // owners, width), bf16),
    ]
    return pl.pallas_call(
        middle_kernel,
        grid=(1,),
        in_specs=[pl.BlockSpec(memory_space=pltpu.SMEM)] + [whole(*item.shape) for item in operands],
        out_specs=[whole(*item.shape) for item in shapes],
        out_shape=shapes,
        compiler_params=kernel_params(20),
        cost_estimate=pl.CostEstimate(
            flops=16 * rows * width * hidden, bytes_accessed=2**24, transcendentals=rows * hidden
        ),
        name="middle",
    )(place, *operands)


def backward_kernel(
    head_width, score_scale, place, expo, query, key_value, attended_wide, inverse_total,
    grad_attended, own, rest, mod, weight, packed_output, grad_residual, sums_in, keep, send,
    rest_part, own_part, sums,
    grad_query, grad_key, grad_value,
):
    pair = pl.program_id(0)
    rows, width = own.shape
    grad_keys, grad_values = [], []
    for i in range(2):
        first = pl.multiple_of((2 * pair + i) * head_width, head_width)
        here = pl.ds(first, head_width)
        scaled = (query[here, :].astype(f32) * score_scale).astype(bf16)
        keys = key_value[here, :]
        values = key_value[pl.ds(pl.multiple_of(width + first, head_width), head_width), :]
        grads = (grad_attended[here, :].astype(f32) * inverse_total[i]).astype(bf16)
        delta = column_sum(grads.astype(f32) * attended_wide[here, :])
        low = expo[i]
        grad_scores = (low.astype(f32) * (inner(values, grads) - delta)).astype(bf16)
        grad_values.append(back_product(low, grads))
        grad_keys.append(back_product(grad_scores, scaled))
        grad_query[here, :] = (product(keys, grad_scores) * score_scale).astype(bf16)
    grad_key[pair] = jnp.concatenate(grad_keys, axis=1).astype(bf16)
    grad_value[pair] = jnp.concatenate(grad_values, axis=1).astype(bf16)

    @pl.when(pair == pl.num_programs(0) - 1)
    def _():
        row = lambda at: mod[at : at + 1, :]
        share = row(SHARE)
        shift, scale = row(SHIFT_ONE), 1.0 + row(SCALE_ONE)
        pairs = range(HEADS // 2)
        packed_key = jnp.zeros((width, width), f32)
        packed_value = jnp.zeros((width, width), f32)
        total_shift = jnp.zeros((1, width), f32)
        total_scale = jnp.zeros((1, width), f32)
        for at in range(0, rows + rest.shape[0], rows):
            here = slice(at, at + rows)
            source = own[...] if at == 0 else rest[at - rows : at, :]
            normed, inverse = normalize(source.astype(f32))
            mixed = (normed * scale + shift).astype(bf16)
            keys = jnp.concatenate([grad_key[pair, here, :] for pair in pairs], axis=1)
            values = jnp.concatenate([grad_value[pair, here, :] for pair in pairs], axis=1)
            part = product(keys, weight[width : 2 * width, :]) + product(
                values, weight[2 * width :, :]
            )
            if at == 0:
                part = part + inner(grad_query[...], weight[:width, :])
                back = normalize_back(part * scale, normed, inverse)
                own_part[...] = (grad_residual[...] + back).astype(bf16)
                packed_query = product(grad_query[...], mixed).T
            else:
                rest_part[at - rows : at, :] = part.astype(bf16)
            packed_key = packed_key + inner(mixed, keys)
            packed_value = packed_value + inner(mixed, values)
            total_shift = total_shift + column_sum(part)
            total_scale = total_scale + column_sum(part * normed)
        first_core = place[2] == 0
        packed = [packed_query * share, packed_key * share, packed_value * share, packed_output[...].astype(f32)]
        half = width // 2
        for at, matrix in enumerate(packed):
            here = slice(at * half, (at + 1) * half)
            keep[here, :] = jnp.where(first_core, matrix[:half], matrix[half:]).astype(bf16)
            send[here, :] = jnp.where(first_core, matrix[half:], matrix[:half]).astype(bf16)
        sums[...] = sums_in[...]
        sums[0:1, :] = total_shift * share
        sums[1:2, :] = total_scale * share
        rest_part[rest.shape[0] :, :] = sums[...].astype(bf16)


def backward_attention(
    place, saved, grad_attended, own, rest, mod, weight, packed_output, grad_residual, sums
):
    expo, query, key_value, attended_wide, inverse_total = saved
    rows, width = own.shape
    key_count = rows + rest.shape[0]
    head_width = width // HEADS
    size = HEADS * rows * key_count
    operands = (
        query, key_value, attended_wide, inverse_total, grad_attended, own, rest, mod, weight,
        packed_output, grad_residual, sums,
    )
    specs = [whole(*item.shape) for item in operands]
    specs[3] = pl.BlockSpec((2, 1, rows), lambda p: (p, 0, 0))
    shapes = [
        pltpu.HBM((2 * width, width), bf16),
        jax.ShapeDtypeStruct((2 * width, width), bf16),
        pltpu.HBM((rest.shape[0] + sums.shape[0], width), bf16),
        jax.ShapeDtypeStruct((rows, width), bf16),
        jax.ShapeDtypeStruct(sums.shape, f32),
    ]
    return pl.pallas_call(
        partial(backward_kernel, head_width, 1.0 / math.sqrt(head_width)),
        grid=(HEADS // 2,),
        in_specs=[
            pl.BlockSpec(memory_space=pltpu.SMEM),
            pl.BlockSpec((2, key_count, rows), lambda p: (p, 0, 0)),
        ]
        + specs,
        out_specs=[whole(*item.shape) for item in shapes],
        out_shape=shapes,
        scratch_shapes=[
            pltpu.VMEM((width, rows), bf16),
            pltpu.VMEM((HEADS // 2, key_count, 2 * head_width), bf16),
            pltpu.VMEM((HEADS // 2, key_count, 2 * head_width), bf16),
        ],
        compiler_params=kernel_params(16),
        cost_estimate=pl.CostEstimate(
            flops=32 * size * head_width, bytes_accessed=2 * size, transcendentals=0
        ),
        name="backward_attention",
    )(place, pltpu.with_memory_space_constraint(expo, pltpu.HBM), *operands)


def finish_kernel(owners, own, part, received, mod, *refs):
    parts, results = refs[:-owners], refs[-owners:]
    rows, width = own.shape
    count = rows // owners
    normed, inverse = normalize(own[...].astype(f32))
    grad = received[:rows, :].astype(f32) * (1.0 + mod[SCALE_ONE : SCALE_ONE + 1, :])
    grad = (part[...].astype(f32) + normalize_back(grad, normed, inverse)).astype(bf16)
    for step, result in enumerate(results):
        result[:count, :] = grad[step * count : (step + 1) * count, :]
    if parts:
        summed = total([ref[...] for ref in parts]).astype(bf16)
        for result in results:
            result[count:, :] = summed


def finish_rows(owners, own, part, received, mod, parts):
    operands = [own, part, received, mod] + parts
    shape = (own.shape[0] // owners + (parts[0].shape[0] if parts else 0), own.shape[1])
    return pl.pallas_call(
        partial(finish_kernel, owners),
        grid=(1,),
        in_specs=[whole(*item.shape) for item in operands],
        out_specs=[whole(*shape)] * owners,
        out_shape=[jax.ShapeDtypeStruct(shape, bf16)] * owners,
        compiler_params=kernel_params(12),
        name="finish_rows",
    )(*operands)


def pair_parts_kernel(grp_size, place, kept, received, *results):
    count = results[0].shape[0]
    for step, result in enumerate(results):
        here = pl.ds(pl.multiple_of(away(place[3], grp_size, step) * count, count), count)
        result[...] = total([kept[here, :], received[here, :]]).astype(bf16)


def pair_parts(place, kept, received):
    grp_size = lax.axis_size("grp")
    shape = (kept.shape[0] // grp_size, kept.shape[1])
    return pl.pallas_call(
        partial(pair_parts_kernel, grp_size),
        grid=(1,),
        in_specs=[pl.BlockSpec(memory_space=pltpu.SMEM)] + [whole(*kept.shape)] * 2,
        out_specs=[whole(*shape)] * grp_size,
        out_shape=[jax.ShapeDtypeStruct(shape, bf16)] * grp_size,
        compiler_params=kernel_params(12),
        name="pair_parts",
    )(place, kept, received)


def sum_parts_kernel(*refs):
    refs[-1][...] = total([ref[...] for ref in refs[:-1]]).astype(bf16)


def sum_parts(parts):
    return pl.pallas_call(
        sum_parts_kernel,
        grid=(1,),
        in_specs=[whole(*parts[0].shape)] * len(parts),
        out_specs=whole(*parts[0].shape),
        out_shape=jax.ShapeDtypeStruct(parts[0].shape, bf16),
        compiler_params=kernel_params(8),
        name="sum_parts",
    )(*parts)


def line_total_kernel(sums, received, *refs):
    parts, result = refs[:-1], refs[-1]
    count = parts[0].shape[-2]
    if len(parts[0].shape) == 3:
        parts = [parts[0].at[at] for at in range(parts[0].shape[0])]
    result[:count, :] = total([part[...] for part in parts]).astype(bf16)
    below = received[received.shape[0] - sums.shape[0] :, :].astype(f32)
    result[count:, :] = (sums[...] + below).astype(bf16)


def line_total(parts, sums, received):
    count, width = parts[0].shape[-2:]
    below = sums.shape[0]
    return pl.pallas_call(
        line_total_kernel,
        grid=(1,),
        in_specs=[whole(*item.shape) for item in [sums, received] + parts],
        out_specs=whole(count + below, width),
        out_shape=jax.ShapeDtypeStruct((count + below, width), bf16),
        compiler_params=kernel_params(4),
        name="line_total",
    )(sums, received, *parts)


def with_lead(below, lead, mod):
    row = lax.broadcasted_iota(jnp.int32, below.shape, 0)
    below = jnp.where(row == 12, mod[EMBEDDING : EMBEDDING + 1, :], below)
    return jnp.where(row == 13, jnp.full(below.shape, lead).astype(f32), below).astype(bf16)


def line_join_kernel(lead, mod, *refs):
    parts, result = refs[:-1], refs[-1]
    count = (result.shape[0] - 16) // len(parts)
    for at, part in enumerate(parts):
        result[at * count : (at + 1) * count, :] = part[:count, :]
    below = total([part[count:, :] for part in parts])
    result[len(parts) * count :, :] = with_lead(below, lead[0], mod)


def line_join(lead, mod, parts):
    rows, width = parts[0].shape
    shape = (len(parts) * (rows - 16) + 16, width)
    return pl.pallas_call(
        line_join_kernel,
        grid=(1,),
        in_specs=[pl.BlockSpec(memory_space=pltpu.SMEM)]
        + [whole(*item.shape) for item in [mod] + parts],
        out_specs=whole(*shape),
        out_shape=jax.ShapeDtypeStruct(shape, bf16),
        compiler_params=kernel_params(8),
        name="line_join",
    )(lead, mod, *parts)


def picked(place, grp_size, own, received, side, b, write):
    group = place[3]
    for step in range(grp_size):
        here = back(group, grp_size, b) == step
        for ref, mine in ((own[step], True), (received[step], False)):

            @pl.when(here & ((place[2] == side) == mine))
            def _():
                write(ref)


def copy_line(place, line, count, ref, output, first):
    for c in range(line):
        from_c = back(place[4], line, c) if line > 1 else 0
        here = pl.ds(pl.multiple_of(from_c * count, count), count) if line > 1 else slice(0, count)
        output[first + c * count : first + (c + 1) * count, :] = ref[here, :].astype(f32)


def first_sums_kernel(grp_size, line, place, *refs):
    own, received = refs[:grp_size], refs[grp_size : 2 * grp_size]
    refs = refs[2 * grp_size :]
    weight, output = refs[:2]
    owners = len(refs) - 14
    pieces, refs = refs[2 : 2 + owners], refs[2 + owners :]
    shrink, expand, grad_weight, copied, rows, table, grad_bias = refs[:7]
    output_bias, expand_bias, shrink_bias, grad_lifted, sums = refs[7:]
    b = pl.program_id(0)
    width = table.shape[1]
    count = own[0].shape[0] - 16
    copied[...] = output[...]
    for step, piece in enumerate(pieces):

        @pl.when(back(place[0], owners, step) == b)
        def _():
            rows[0] = piece[: rows.shape[1], :].astype(f32)

    for side, target in enumerate((shrink, expand)):
        write = lambda ref: copy_line(place, line, count // line, ref, target, 0)
        picked(place, grp_size, own, received, side, b, write)

    parts = [part[count:, :].astype(f32) for part in own]
    pad = jnp.zeros((8 - grp_size, width), f32)
    stacked = jnp.concatenate([part[12:13] for part in parts] + [pad])
    gate = 1.0 / (1.0 + jnp.exp(-stacked))

    @pl.when(b == 0)
    def _():
        sums[...] = total(parts)
        grad_lifted[...] = jnp.zeros_like(grad_lifted)

    @pl.when(b < 3)
    def _():
        lifted = (stacked * gate).astype(bf16)
        line_of = lax.broadcasted_iota(jnp.int32, parts[0].shape, 0)
        for i in range(2):
            here = slice(i * width, (i + 1) * width)
            picks = [column_sum(jnp.where(line_of == 2 * b + i, part, 0.0)) for part in parts]
            picks = jnp.concatenate(picks + [pad]).astype(bf16)
            grad_weight[:, here] = inner(lifted, picks)
            grad_lifted[...] += back_product(picks, weight[:, here])

    @pl.when(b == pl.num_programs(0) - 1)
    def _():
        for at in range(6):
            grad_bias[at * width : (at + 1) * width] = sums[at]
        output_bias[...] = sums[6]
        for at in range(expand_bias.shape[0] // width):
            expand_bias[at * width : (at + 1) * width] = sums[7 + at]
        shrink_bias[...] = sums[7 + expand_bias.shape[0] // width]
        grad_embedding = grad_lifted[...] * gate * (1.0 + stacked * (1.0 - gate))
        lead = lax.broadcasted_iota(jnp.int32, (LEADS, width), 0).astype(f32)
        table[...] = total(
            [
                jnp.where(lead == part[13:14], grad_embedding[p : p + 1], 0.0)
                for p, part in enumerate(parts)
            ]
        )


def first_sums(place, own, first, weight, output, pieces):
    grp_size = len(own)
    line = 1 if line_size() > 4 else line_size()
    received = [first] + [swap_cores(part) for part in own[1:]]
    width = weight.shape[0]
    hidden = grp_size * width
    block = pl.BlockSpec((1,) + output.shape[1:], lambda b: (b, 0, 0))
    wide = pl.BlockSpec((width, 2 * width), lambda b: (0, jnp.minimum(b, 2)))
    return pl.pallas_call(
        partial(first_sums_kernel, grp_size, line),
        grid=(grp_size,),
        in_specs=[pl.BlockSpec(memory_space=pltpu.SMEM)]
        + [whole(*own[0].shape)] * (2 * grp_size)
        + [wide, block]
        + [whole(*item.shape) for item in pieces],
        out_specs=[
            pl.BlockSpec((width, width), lambda b: (b, 0)),
            pl.BlockSpec((width, width), lambda b: (0, b)),
            wide,
            block,
            block,
            whole(LEADS, width),
            whole(6 * width),
            whole(width),
            whole(hidden),
            whole(width),
        ],
        out_shape=[
            jax.ShapeDtypeStruct((hidden, width), f32),
            jax.ShapeDtypeStruct((width, hidden), f32),
            jax.ShapeDtypeStruct(weight.shape, f32),
            jax.ShapeDtypeStruct(output.shape, output.dtype),
            jax.ShapeDtypeStruct(output.shape, f32),
            jax.ShapeDtypeStruct((LEADS, width), f32),
            jax.ShapeDtypeStruct((6 * width,), f32),
            jax.ShapeDtypeStruct((width,), f32),
            jax.ShapeDtypeStruct((hidden,), f32),
            jax.ShapeDtypeStruct((width,), f32),
        ],
        scratch_shapes=[pltpu.VMEM((8, width), f32), pltpu.VMEM((16, width), f32)],
        compiler_params=kernel_params(16),
        name="first_sums",
    )(place, *own, *received, weight, output, *pieces)


def second_sums_kernel(grp_size, line, place, *refs):
    own, received = refs[:grp_size], refs[grp_size : 2 * grp_size]
    attend, output = refs[2 * grp_size :]
    width = output.shape[0]
    half = width // 2
    for group in range(grp_size):
        for core in range(2):

            @pl.when((place[3] == group) & (place[2] == core))
            def _():
                for b in range(grp_size):
                    step = back(group, grp_size, b)
                    for side, parts in ((core, own), (1 - core, received)):
                        if b < grp_size - 1:
                            target = attend.at[:, b * width : (b + 1) * width]
                        else:
                            target = output
                        copy_line(place, line, half // line, parts[step], target, side * half)


def second_sums(place, own, first):
    grp_size, width = len(own), own[0].shape[1]
    line = 1 if line_size() > 4 else line_size()
    received = [first] + [swap_cores(part) for part in own[1:]]
    shapes = [(width, (grp_size - 1) * width), (width, width)]
    return pl.pallas_call(
        partial(second_sums_kernel, grp_size, line),
        grid=(1,),
        in_specs=[pl.BlockSpec(memory_space=pltpu.SMEM)] + [whole(*own[0].shape)] * (2 * grp_size),
        out_specs=[whole(*shape) for shape in shapes],
        out_shape=[jax.ShapeDtypeStruct(shape, f32) for shape in shapes],
        compiler_params=kernel_params(16),
        name="second_sums",
    )(place, *own, *received)


def long_forward(owner, rank, share, lengths, valid, own, rest, mod, weight):
    rows, width = own.shape
    owners = lengths.shape[0]
    count = rows // owners
    steps = jnp.arange(owners, dtype=jnp.int32)
    ranks = (rank + jnp.arange(share, dtype=jnp.int32)) % share
    blocks = (back(owner, owners, steps)[None, :] * share + ranks[:, None]).reshape(-1, 1)
    key_pos = blocks * count + jnp.arange(count, dtype=jnp.int32)[None, :]
    doc_ends = jnp.cumsum(lax.dynamic_index_in_dim(lengths, owner, 0, False))
    key_seg = sum((key_pos >= doc_ends[doc]).astype(jnp.int32) for doc in range(doc_ends.shape[0]))
    own_valid = lax.dynamic_index_in_dim(valid, owner, 0, False).reshape(-1, count)
    key_valid = own_valid[blocks[:, 0]] > 0
    open_seg = jnp.where(key_valid, key_seg, -1).reshape(1, -1)
    key_pos = key_pos.reshape(1, -1)
    query_seg = key_seg.reshape(-1, 1)[:rows]
    query_pos = key_pos.reshape(-1, 1)[:rows]
    head_width = width // HEADS
    normed = normalize(jnp.concatenate([own, rest], axis=0).astype(f32))[0]
    mixed = (normed * (1.0 + mod[SCALE_ONE]) + mod[SHIFT_ONE]).astype(bf16)
    heads = lambda v: v.reshape(v.shape[0], HEADS, head_width).transpose(1, 0, 2)
    queries = heads(back_product(mixed[:rows], weight[:width]).astype(bf16))
    key_value = back_product(mixed, weight[width:]).astype(bf16)
    keys = heads(key_value[:, :width])
    values = heads(key_value[:, width:])
    probs, attended = attention(
        queries, keys, values, query_seg, query_pos, open_seg, key_pos, 1.0 / math.sqrt(head_width)
    )
    flat = attended.transpose(1, 0, 2).reshape(rows, width).astype(bf16)
    return ((probs, queries, keys, values, attended, normed, mixed), flat)


def long_backward(
    place, saved, grad_attended, own, rest, mod, weight, packed_output, grad_residual, sums
):
    probs, queries, keys, values, attended, normed, mixed = saved
    rows, width = own.shape
    head_width = width // HEADS
    score_scale = 1.0 / math.sqrt(head_width)
    grad_heads = grad_attended.reshape(HEADS, head_width, rows).transpose(0, 2, 1)
    deltas = jnp.sum(grad_heads.astype(f32) * attended, axis=-1, keepdims=True)
    grad_probs = jnp.einsum("hqd,hkd->hqk", grad_heads, values, preferred_element_type=f32)
    grad_scores = (probs.astype(f32) * (grad_probs - deltas)).astype(bf16)
    grad_query = jnp.einsum("hqk,hkd->hqd", grad_scores, keys, preferred_element_type=f32)
    grad_key = jnp.einsum("hqk,hqd->hkd", grad_scores, queries, preferred_element_type=f32)
    grad_value = jnp.einsum("hqk,hqd->hkd", probs, grad_heads, preferred_element_type=f32)
    flat = lambda v: v.transpose(1, 0, 2).reshape(v.shape[1], width)
    grad_query = (flat(grad_query) * score_scale).astype(bf16)
    grad_key = (flat(grad_key) * score_scale).astype(bf16)
    grad_value = flat(grad_value).astype(bf16)
    part = product(grad_key, weight[width : 2 * width]) + product(grad_value, weight[2 * width :])
    part = jnp.concatenate([part[:rows] + product(grad_query, weight[:width]), part[rows:]], axis=0)
    share = mod[SHARE]
    packed = [row_product(mixed[:rows], grad_query), row_product(mixed, grad_key), row_product(mixed, grad_value)]
    packed = [(matrix * share).astype(bf16) for matrix in packed] + [packed_output]
    half = width // 2
    top = jnp.concatenate([matrix[:half] for matrix in packed])
    bottom = jnp.concatenate([matrix[half:] for matrix in packed])
    first_core = place[2] == 0
    keep = jnp.where(first_core, top, bottom)
    send = jnp.where(first_core, bottom, top)
    total_rows = jnp.stack([jnp.sum(part, axis=0), jnp.sum(part * normed, axis=0)]) * share
    sums = jnp.concatenate([total_rows, sums[2:]], axis=0)
    normed, inverse = normalize(own.astype(f32))
    own_part = grad_residual + normalize_back(part[:rows] * (1.0 + mod[SCALE_ONE]), normed, inverse)
    return (keep, send, part[rows:].astype(bf16), own_part.astype(bf16), sums)


def on_device(
    tokens,
    cotangent,
    lengths,
    valid_mask,
    lead_index,
    sample_counts,
    lead_table,
    modulation_weight,
    modulation_bias,
    attend_weight,
    output_weight,
    output_bias,
    expand_weight,
    expand_bias,
    shrink_weight,
    shrink_bias,
):
    owners = tokens.shape[1]
    block_rows = tokens.shape[2]
    width = tokens.shape[3]
    hidden_width = expand_bias.shape[0]
    seq_size = lax.axis_size("seq")
    share = seq_size // owners
    seq_length = block_rows * seq_size
    rows = owners * block_rows
    place = lax.axis_index("seq")
    owner = place // share
    rank = place % share

    where = jnp.stack([owner, rank, place % 2, lax.axis_index("grp"), place // 2]).astype(jnp.int32)

    token_pieces = rows_to_owner(tokens[0], owner, share)

    bias = [modulation_bias, output_bias, expand_bias, shrink_bias]
    bias = after(jnp.concatenate(bias).astype(f32))[None]
    mod, weight = prepare(
        where, lead_index, sample_counts, lead_table, modulation_weight, bias, attend_weight,
        owners * seq_length,
    )
    grad_pieces = rows_to_owner(cotangent[0], owner, share, {step: bias if step in (1,) else mod for step in range(1, owners)})
    token_pieces = after_all(token_pieces, mod, grad_pieces[1])
    own_tokens = jnp.concatenate(token_pieces, axis=0)
    rest_tokens = share_rows(own_tokens, rank, share)
    short = seq_length <= 2048
    if short:
        *saved, attended = forward_attention(
            where, lengths[0], valid_mask[0], own_tokens, rest_tokens, mod, weight
        )
    else:
        saved, attended = long_forward(
            owner, rank, share, lengths[0], valid_mask[0], own_tokens, rest_tokens, mod, weight
        )
    grad_out = jnp.concatenate(after_all(grad_pieces, attended), axis=0)
    ff_keep, ff_send, packed_output, grad_attended, grad_residual, sums, output = middle(
        owners, where, own_tokens, attended, grad_out, mod, bias, output_weight, expand_weight,
        shrink_weight,
    )
    output = rows_from_owner(output, share)
    ff_core = low_total([ff_keep, swap_cores(ff_send)])
    ff_parts = send_plane(plane_parts(ff_core))
    grad_attended = after(grad_attended, ff_core)
    backward = backward_attention if short else long_backward
    held = backward(
        where, saved, grad_attended, own_tokens, rest_tokens, mod, weight, packed_output,
        grad_residual, sums,
    )
    at_keep, at_send, rest_part, own_part, sums = after_all(held, *ff_parts[1:], output)
    ff_plane = sum_parts(ff_parts)
    line = line_size() <= 4
    if line:
        ff_parts = [line_exchange(ff_plane.reshape(line_size(), -1, width))]
    at_core = low_total([at_keep, swap_cores(at_send)])
    if share == 2:
        received = swap_cores(rest_part)
    else:
        received = return_rows(rest_part, rank, share)
    at_slices = plane_parts(at_core)
    at_parts = send_plane(at_slices)
    if line:
        ff_parts = list(after_all(ff_parts, *at_slices))
        ff_line = line_total(ff_parts, sums, received)
        at_parts = after_all(at_parts, ff_line)
    at_plane = low_total(at_parts)
    if line:
        ff_pieces = send_line([ff_line] * line_size())
        ff_plane = line_join(lead_index, mod, ff_pieces)
        at_line = send_line(line_parts(at_plane))
    else:
        vector = with_lead(lax.psum(sums, "seq"), lead_index[0], mod)
        ff_pieces = [sum_line(ff_plane)]
        ff_plane = jnp.concatenate(ff_pieces + [vector])
        at_line = []
    pieces = finish_rows(owners, own_tokens, own_part, received, mod, at_line)
    pieces = pieces_from_owner(pieces, share)
    at_pieces = [piece[block_rows:] for piece in pieces] if line else [sum_line(at_plane)]
    ff_parts = gather_plane(ff_plane)
    ff_first = swap_cores(ff_plane)
    at_held = jnp.concatenate(at_pieces)
    at_parts = gather_plane(at_held)
    at_first = swap_cores(at_held)
    ff_parts = list(after_all(ff_parts, *pieces))
    grad_shrink, grad_expand, grad_mod_weight, output, grad_tokens, grad_table, grad_mod_bias, *biases = (
        first_sums(where, ff_parts, ff_first, modulation_weight, output, pieces)
    )
    at_parts = list(after_all(at_parts, grad_shrink))
    grad_attend, grad_output = second_sums(where, at_parts, at_first)
    return (
        output[None],
        grad_tokens[None],
        grad_table,
        grad_mod_weight,
        grad_mod_bias,
        grad_attend,
        grad_output,
        biases[0],
        grad_expand,
        biases[1],
        grad_shrink,
        biases[2],
    )


def solution(mesh):
    rows = P("grp", None, "seq", None)
    placed = (rows, rows, P("grp", None, None), P("grp", None, None), P("grp")) + (P(),) * 11
    return jax.shard_map(
        on_device,
        mesh=mesh,
        in_specs=placed,
        out_specs=(rows, rows) + (P(),) * 10,
        check_vma=False,
    )
```
